128 devices in a mesh: section: 2 (over z_hi), shard: 16 (over x, z_lo, core), replica: 4 (over y).
Axes of the slice: x: 4, y: 4, z: 4 (z_hi: 2, z_lo: 2; z = z_hi * 2 + z_lo), core: 2. Of those that a mesh axis runs over, the one named last changes fastest.
Arguments:
- edge_inputs: bfloat16 [2, 2, 64, 128, 1024], P('section', None, ('shard', 'replica')), may hold values from -6 to 6
- image_counts: int32 [2], replicated, may hold values from 32 to 64, as said below
- w_qkv: bfloat16 [2, 1024, 3072], P('section', 'shard'), may hold values from -0.1875 to 0.1875
- w_proj: bfloat16 [2, 1024, 1024], P('section', 'shard'), may hold values from -0.5 to 0.5
- w_fc1: bfloat16 [2, 1024, 4096], P('section', 'shard'), may hold values from -0.1875 to 0.1875
- w_fc2: bfloat16 [2, 4096, 1024], P('section', 'shard'), may hold values from -0.09375 to 0.09375
- vectors: bfloat16 [2, 10, 1024], P('section', None, 'shard'), may hold values from -1.5 to 1.5
- fc1_bias: bfloat16 [2, 4096], P('section', 'shard'), may hold values from -1.75 to 1.75
Outputs:
- edge_values: float32 [2, 2, 64, 128, 1024], P('section', None, ('shard', 'replica'))
- grad_qkv: float32 [2, 1024, 3072], P('section', 'shard')
- grad_proj: float32 [2, 1024, 1024], P('section', 'shard')
- grad_fc1: float32 [2, 1024, 4096], P('section', 'shard')
- grad_fc2: float32 [2, 4096, 1024], P('section', 'shard')
- grad_vectors: float32 [2, 10, 1024], P('section', None, 'shard')
- grad_fc1_bias: float32 [2, 4096], P('section', 'shard')
The draws below stay inside these ranges and needn't reach their ends.
Inputs may be any that keep to these rules, and one draw needn't show every extreme that they name: micro-batch m holds images 0 to image_counts[m] - 1.
All inputs are finite; a program needn't handle non-finite values.
Results may differ from the reference program's by a relative error of at most 0.022.
Values may be sent and summed in bfloat16 or wider, within the bound.
No kernel may reach another device: no remote copies, remote signals or barrier semaphores. Data moves between devices by JAX's collectives and lax.ppermute only.
A program may use at most 256 MiB of HBM per device.

```python
import jax
import jax.numpy as jnp
from jax import lax

D = 1024
HEADS = 16
HEAD_DIM = 64
FF = 4096
SEQ = 128
MICRO = 2
IMAGES = 64


def draw_image_counts(key, part):
    key = jax.random.fold_in(key, 11)
    key_pick, key_count = jax.random.split(key)
    chosen = jax.random.randint(key_pick, (), 0, MICRO)
    shorter = jax.random.randint(key_count, (), IMAGES // 2, IMAGES)
    positions = jnp.arange(MICRO)
    return jnp.where(positions == chosen, shorter, IMAGES).astype(jnp.int32)


def draw_vectors(key, part):
    key = jax.random.fold_in(key, 23)
    key_gain, key_bias = jax.random.split(key)
    rows = jnp.arange(10)[None, :, None]
    is_scale = (rows == 0) | (rows == 5) | (rows == 6) | (rows == 9)
    gains = jax.random.uniform(key_gain, (2, 10, D), jnp.float32, 0.5, 1.5)
    biases = jnp.clip(0.3 * jax.random.normal(key_bias, (2, 10, D), jnp.float32), -1.5, 1.5)
    return jnp.where(is_scale, gains, biases).astype(jnp.bfloat16)


def levels(rng, extent, cuts, least, high):
    level = 1.0
    for dim, shards_of in cuts:
        draws = jax.random.uniform(jax.random.fold_in(jax.random.fold_in(rng, 6), dim), (shards_of,), jnp.float32, least / len(cuts), high / len(cuts))
        level = level * jnp.repeat(jnp.exp(draws), extent[dim] // shards_of).reshape((-1,) + (1,) * (len(extent) - 1 - dim))
    return level


def bell_draw(own_key, shape, scale, bound, cuts=(), held_as=jnp.bfloat16):
    loudness = levels(own_key, shape, cuts, -0.22, 0.18) if cuts else 1.0
    values = jax.random.normal(own_key, shape, jnp.float32) * scale * loudness
    return jnp.minimum(jnp.maximum(values, -bound), bound).astype(held_as)


def setup_inputs(seed: int = 0) -> dict:
    splits = jax.random.split(jax.random.key(seed), 9)
    edge_inputs = bell_draw(splits[0], (2, MICRO, IMAGES, SEQ, D), 1.0, 6.0, ((0, 2), (2, 64)))
    image_counts = draw_image_counts(jax.random.fold_in(splits[8], 71), 0)
    w_qkv = bell_draw(splits[2], (2, D, 3 * D), D ** -0.5, 0.1875, ((0, 2), (1, 16)))
    w_proj = bell_draw(splits[3], (2, D, D), (D // 8) ** -0.5, 0.5, ((0, 2), (1, 16)))
    w_fc1 = bell_draw(splits[4], (2, D, FF), D ** -0.5, 0.1875, ((0, 2), (1, 16)))
    w_fc2 = bell_draw(splits[5], (2, FF, D), FF ** -0.5, 0.09375, ((0, 2), (1, 16)))
    vectors = draw_vectors(jax.random.fold_in(splits[8], 71), 0)
    fc1_bias = bell_draw(splits[7], (2, FF), 0.3, 1.75, ((0, 2), (1, 16)))
    return dict(edge_inputs=edge_inputs, image_counts=image_counts, w_qkv=w_qkv, w_proj=w_proj, w_fc1=w_fc1, w_fc2=w_fc2, vectors=vectors, fc1_bias=fc1_bias)


@jax.custom_vjp
def low(v):
    return lax.optimization_barrier(v.astype(jnp.bfloat16)).astype(jnp.float32)

@jax.custom_vjp
def low_back(v):
    return v

def low_keep(v):
    return (low(v), None)

def low_pass(kept, grad):
    return (grad,)

def back_keep(v):
    return (v, None)

def back_low(kept, grad):
    return (low(grad),)
low.defvjp(low_keep, low_pass)
low_back.defvjp(back_keep, back_low)
epsilon = 1e-06
highest = lax.Precision.HIGHEST

def layer_norm(values, gain, shift):
    average = lax.optimization_barrier(jnp.mean(values, axis=-1, keepdims=True))
    centered = values - average
    spread = lax.optimization_barrier(jnp.mean(centered * centered, axis=-1, keepdims=True))
    return centered * lax.rsqrt(spread + epsilon) * gain + shift

def attend_image(projected):
    seq_len = projected.shape[0]
    split_heads = projected.reshape(seq_len, 3, HEADS, HEAD_DIM)
    queries = split_heads[:, 0]
    keys_all = split_heads[:, 1]
    values_all = split_heads[:, 2]
    scaling = 1.0 / HEAD_DIM ** 0.5
    scores = low_back(jnp.einsum('qhd,khd->hqk', queries, keys_all, precision=highest) * scaling)
    soft_weights = low(jax.nn.softmax(scores, axis=-1))
    mixed_heads = jnp.einsum('hqk,khd->qhd', soft_weights, values_all, precision=highest)
    return mixed_heads.reshape(seq_len, HEADS * HEAD_DIM)

def layer_forward(inputs, layer_params):
    weight_qkv, weight_proj, weight_fc1, weight_fc2, small_params, hidden_bias = layer_params
    width = inputs.shape[-1]
    normed = low(layer_norm(inputs, small_params[0], small_params[1]))
    qkv_bias = jnp.concatenate([small_params[2], jnp.zeros((width,), jnp.float32), small_params[3]])
    projected = low_back(low(jnp.einsum('isd,de->ise', normed, weight_qkv, precision=highest) + qkv_bias))
    mixed_rows = low_back(low(lax.map(jax.checkpoint(attend_image), projected)))
    branch = low_back(jnp.einsum('isd,de->ise', mixed_rows, weight_proj, precision=highest) + small_params[4])
    middle = inputs + small_params[5] * branch
    second = low(layer_norm(middle, small_params[6], small_params[7]))
    hidden = low_back(jnp.einsum('isd,df->isf', second, weight_fc1, precision=highest) + hidden_bias)
    activated = low(jax.nn.gelu(hidden, approximate=False))
    out_branch = low_back(jnp.einsum('isf,fd->isd', activated, weight_fc2, precision=highest) + small_params[8])
    return middle + small_params[9] * out_branch

def pick_layer(params, layer_index):
    return tuple((array[layer_index] for array in params))

def stack_forward(inputs, params):
    first_out = layer_forward(inputs, pick_layer(params, 0))
    passed = low_back(low(first_out))
    return layer_forward(passed, pick_layer(params, 1))

def reference(edge_inputs, image_counts, w_qkv, w_proj, w_fc1, w_fc2, vectors, fc1_bias):
    params = tuple((array.astype(jnp.float32) for array in (w_qkv, w_proj, w_fc1, w_fc2, vectors, fc1_bias)))
    layer_inputs = edge_inputs[0].astype(jnp.float32)
    image_ids = jnp.arange(IMAGES, dtype=jnp.int32)
    present = (image_ids[None, :] < image_counts[:, None]).astype(jnp.float32)
    cotangent = edge_inputs[1].astype(jnp.float32) * present[:, :, None, None]

    def per_micro(totals, pair):
        batch_in, batch_cot = pair
        outputs, pullback = jax.vjp(stack_forward, batch_in, params)
        grad_in, grad_params = pullback(batch_cot)
        totals = jax.tree.map(jnp.add, totals, grad_params)
        return (totals, (outputs, grad_in))
    zero_grads = tuple((jnp.zeros_like(array) for array in params))
    totals, (outputs, grad_in) = lax.scan(per_micro, zero_grads, (layer_inputs, cotangent))
    edge_values = jnp.stack([grad_in, outputs])
    return (edge_values, totals[0], totals[1], totals[2], totals[3], totals[4], totals[5])
```

```python
import jax
import jax.numpy as jnp
from jax import lax
from jax.sharding import PartitionSpec as P

HEAD_DIM = 64
XS, ZS, CS, YS = 4, 2, 2, 4
epsilon = 1e-06
bf16, f32 = jnp.bfloat16, jnp.float32


def shard_of(x, z, c):
    return (x % XS) * 4 + (z % ZS) * 2 + (c % CS)


def from_shard(value, dx=0, dz=0, dc=0):
    pairs = [
        (shard_of(x + dx, z + dz, c + dc), shard_of(x, z, c))
        for x in range(XS)
        for z in range(ZS)
        for c in range(CS)
    ]
    return lax.ppermute(value, "shard", pairs)


def from_replica(value, dy):
    return lax.ppermute(value, "replica", [((y + dy) % YS, y) for y in range(YS)])


def passed_along(value, steps):
    pairs = [(0, 1)] if steps == 1 else [(1, 0)]
    return lax.ppermute(value, "section", pairs)


def pick(array, index, axis, keep=False):
    return lax.dynamic_index_in_dim(array, index, axis, keepdims=keep)


def rolled(array, shift, axis):
    n = array.shape[axis]
    twice = jnp.concatenate([array, array], axis=axis)
    return lax.dynamic_slice_in_dim(twice, shift, n, axis)


def normalize(values, gain, shift):
    average = jnp.mean(values, axis=-1, keepdims=True)
    centered = values - average
    spread = jnp.mean(centered * centered, axis=-1, keepdims=True)
    return centered * lax.rsqrt(spread + epsilon) * gain + shift


def gelu_exact(values):
    return jax.nn.gelu(values, approximate=False)


def gather_columns(unit):
    other = from_shard(unit, dz=1)
    pair = jnp.stack([unit, other])
    plus = from_shard(pair, dx=1)
    minus = from_shard(pair, dx=3)
    far_a = from_shard(plus[0], dx=1)
    far_b = from_shard(minus[1], dx=3)
    mine = [pair, plus, jnp.stack([far_a, far_b]), minus]
    theirs = [
        from_shard(pair, dc=1),
        from_shard(plus, dc=1),
        jnp.stack([from_shard(far_a, dc=1), from_shard(far_b, dc=1)]),
        from_shard(minus, dc=1),
    ]
    return jnp.stack([jnp.stack(mine), jnp.stack(theirs)])


def gather_rows(piece):
    near = [piece if (dx, dz) == (0, 0) else from_shard(piece, dx=dx, dz=dz) for dx in range(XS) for dz in range(ZS)]
    here = jnp.stack(near)
    plus = from_replica(here, 1)
    minus = from_replica(here, 3)
    far_a = from_replica(plus[:, :64], 1)
    far_b = from_replica(minus[:, 64:], 3)
    mine = [here, plus, jnp.concatenate([far_a, far_b], axis=1), minus]
    theirs = [
        from_shard(here, dc=1),
        from_shard(plus, dc=1),
        jnp.concatenate([from_shard(far_a, dc=1), from_shard(far_b, dc=1)], axis=1),
        from_shard(minus, dc=1),
    ]
    both = jnp.stack([jnp.stack(mine), jnp.stack(theirs)])
    return both.reshape(CS, YS, XS, ZS, 96, 1024)


def gather_all(w_qkv, w_proj, w_fc1, w_fc2, vectors, fc1_bias, place):
    x, z, c, y = place
    small = jnp.concatenate([vectors, fc1_bias.reshape(4, 64)], axis=0).T
    small = jnp.pad(small, ((0, 0), (0, 114)))
    unit = jnp.concatenate([w_qkv, w_proj, w_fc2[128:192], w_fc2[192:], small], axis=1)
    piece = jnp.concatenate(
        [
            lax.dynamic_slice(w_fc1, (0, y * 1024), (64, 1024)),
            lax.dynamic_slice(w_fc2, (y * 32, 0), (32, 1024)),
        ],
        axis=0,
    )
    columns = gather_columns(unit)
    rows = gather_rows(piece)
    back = lambda v, i, axis: rolled(v, (v.shape[axis] - i) % v.shape[axis], axis)
    columns = back(back(back(columns, c, 0), x, 1), z, 2)
    columns = columns.transpose(1, 2, 0, 3, 4)
    rows = back(back(back(back(rows, c, 0), y, 1), x, 2), z, 3)
    qkv = columns[..., :3072].reshape(1024, 3072)
    proj = columns[..., 3072:4096].reshape(1024, 1024)
    fc2_b = columns[..., 4096:6144].reshape(XS, ZS, CS, 64, 2, 1024).transpose(0, 1, 2, 4, 3, 5)
    fc2_b = fc2_b.reshape(16, 128, 1024)
    small = columns[..., 6144:6158].reshape(16, 64, 14)
    fc1 = rows[..., :64, :].transpose(2, 3, 0, 4, 1, 5).reshape(1024, 4096)
    fc2_a = rows[..., 64:, :].transpose(2, 3, 0, 1, 4, 5).reshape(16, 128, 1024)
    fc2 = jnp.concatenate([fc2_a, fc2_b], axis=1).reshape(4096, 1024)
    vec = small[:, :, :10].transpose(2, 0, 1).reshape(10, 1024).astype(f32)
    bias = small[:, :, 10:].transpose(0, 2, 1).reshape(4096).astype(f32)
    return qkv, proj, fc1, fc2, vec, bias


def forward_layer(inputs, layer_weights):
    qkv, proj, fc1, fc2, vec, bias = layer_weights
    rows, width = inputs.shape
    images, heads = rows // 128, width // HEAD_DIM
    normed = normalize(inputs, vec[0], vec[1]).astype(bf16)
    qkv_bias = jnp.concatenate([vec[2], jnp.zeros((width,), f32), vec[3]])
    projected = (jnp.dot(normed, qkv, preferred_element_type=f32) + qkv_bias).astype(bf16)
    split = projected.reshape(images, 128, 3, heads, HEAD_DIM).transpose(2, 0, 3, 1, 4)
    queries, keys, values = split[0], split[1], split[2]
    scores = jnp.einsum("ihqd,ihkd->ihqk", queries, keys, preferred_element_type=f32) * 0.125
    soft = jax.nn.softmax(scores, axis=-1)
    mixed = jnp.einsum("ihqk,ihkd->ihqd", soft.astype(bf16), values, preferred_element_type=f32)
    mixed = mixed.astype(bf16).transpose(0, 2, 1, 3).reshape(rows, width)
    branch = jnp.dot(mixed, proj, preferred_element_type=f32) + vec[4]
    middle = inputs + vec[5] * branch
    second = normalize(middle, vec[6], vec[7]).astype(bf16)
    hidden = jnp.dot(second, fc1, preferred_element_type=f32) + bias
    activated = gelu_exact(hidden).astype(bf16)
    out_branch = jnp.dot(activated, fc2, preferred_element_type=f32) + vec[8]
    output = middle + vec[9] * out_branch
    return output, (normed, queries, keys, values, soft, mixed, branch, middle, second, hidden, activated, out_branch)


def backward_layer(inputs, upstream, saved, layer_weights):
    qkv, proj, fc1, fc2, vec, bias = layer_weights
    normed, queries, keys, values, soft, mixed, branch, middle, second, hidden, activated, out_branch = saved
    rows, width = inputs.shape
    d_out = (vec[9] * upstream).astype(bf16)
    g9 = jnp.sum(upstream * out_branch, axis=0)
    g8 = jnp.sum(d_out.astype(f32), axis=0)
    d_act = jnp.einsum("sd,fd->sf", d_out, fc2, preferred_element_type=f32)
    _, gelu_pull = jax.vjp(gelu_exact, hidden)
    d_hidden = gelu_pull(d_act)[0].astype(bf16)
    g_bias = jnp.sum(d_hidden.astype(f32), axis=0)
    d_second = jnp.einsum("sf,df->sd", d_hidden, fc1, preferred_element_type=f32)
    _, norm_pull = jax.vjp(normalize, middle, vec[6], vec[7])
    d_norm, g6, g7 = norm_pull(d_second)
    d_middle = upstream + d_norm
    g5 = jnp.sum(d_middle * branch, axis=0)
    d_branch = (vec[5] * d_middle).astype(bf16)
    g4 = jnp.sum(d_branch.astype(f32), axis=0)
    d_mixed = jnp.einsum("se,de->sd", d_branch, proj, preferred_element_type=f32).astype(bf16)
    images, heads = rows // 128, width // HEAD_DIM
    d_mixed = d_mixed.reshape(images, 128, heads, HEAD_DIM).transpose(0, 2, 1, 3)
    d_values = jnp.einsum("ihqk,ihqd->ihkd", soft.astype(bf16), d_mixed, preferred_element_type=f32)
    d_soft = jnp.einsum("ihqd,ihkd->ihqk", d_mixed, values, preferred_element_type=f32)
    row_terms = jnp.sum(soft * d_soft, axis=-1, keepdims=True)
    d_scores = (soft * (d_soft - row_terms)).astype(bf16)
    d_queries = jnp.einsum("ihqk,ihkd->ihqd", d_scores, keys, preferred_element_type=f32) * 0.125
    d_keys = jnp.einsum("ihqk,ihqd->ihkd", d_scores, queries, preferred_element_type=f32) * 0.125
    d_proj = jnp.stack([d_queries, d_keys, d_values]).astype(bf16)
    d_proj = d_proj.transpose(1, 3, 0, 2, 4).reshape(rows, 3 * width)
    sums = jnp.sum(d_proj.astype(f32), axis=0)
    d_normed = jnp.einsum("se,de->sd", d_proj, qkv, preferred_element_type=f32)
    _, first_pull = jax.vjp(normalize, inputs, vec[0], vec[1])
    d_first, g0, g1 = first_pull(d_normed)
    d_inputs = d_middle + d_first
    small = jnp.stack([g0, g1, sums[:width], sums[2 * width :], g4, g5, g6, g7, g8, g9])
    return d_inputs, (d_proj, d_branch, d_hidden, d_out), small, g_bias


def with_twin(acts, c):
    tokens = acts.shape[0]
    parts = acts.T.reshape(XS, ZS, CS, -1, tokens)
    mine = pick(parts, c, 2)
    theirs = from_shard(pick(parts, 1 - c, 2), dc=1)
    return jnp.concatenate([mine, theirs], axis=-1)


def scatter_columns(d_unit):
    first = from_shard(d_unit[2, 0], dx=3)
    second = from_shard(d_unit[2, 1], dx=1)
    to_plus = jnp.stack([d_unit[1, 0].astype(f32) + first.astype(f32), d_unit[1, 1].astype(f32)]).astype(bf16)
    to_minus = jnp.stack([d_unit[3, 0].astype(f32), d_unit[3, 1].astype(f32) + second.astype(f32)]).astype(bf16)
    got_a = from_shard(to_plus, dx=3)
    got_b = from_shard(to_minus, dx=1)
    total = d_unit[0].astype(f32) + got_a.astype(f32) + got_b.astype(f32)
    got = from_shard(total[1].astype(bf16), dz=1)
    return total[0] + got.astype(f32)


def summed_over_replicas(part, y):
    low = part.astype(bf16).reshape(YS, 16, -1)
    mine = pick(part.reshape(YS, 16, -1), y, 0)
    for dy in range(1, YS):
        got = from_replica(pick(low, (y + YS - dy) % YS, 0), dy)
        mine = mine + got.astype(f32)
    mine = mine.astype(bf16)
    parts = [mine] + [from_replica(mine, dy) for dy in range(1, YS)]
    return rolled(jnp.stack(parts), (YS - y) % YS, 0).reshape(part.shape).astype(f32)


def scatter_rows(chunks, y):
    first = from_replica(chunks[2][:, :, :64], 3)
    second = from_replica(chunks[2][:, :, 64:], 1)
    add = lambda a, b: (a.astype(f32) + b.astype(f32)).astype(bf16)
    to_plus = jnp.concatenate([add(chunks[1][:, :, :64], first), chunks[1][:, :, 64:]], axis=2)
    to_minus = jnp.concatenate([chunks[3][:, :, :64], add(chunks[3][:, :, 64:], second)], axis=2)
    got_a = from_replica(to_plus, 3)
    got_b = from_replica(to_minus, 1)
    total = chunks[0].astype(f32) + got_a.astype(f32) + got_b.astype(f32)
    low = total.astype(bf16)
    mine = total[0, 0]
    for dx in range(XS):
        for dz in range(ZS):
            if (dx, dz) != (0, 0):
                mine = mine + from_shard(low[dx, dz], dx=XS - dx, dz=dz).astype(f32)
    mine = mine.astype(bf16)
    parts = [mine] + [from_replica(mine, dy) for dy in range(1, YS)]
    return rolled(jnp.stack(parts), (YS - y) % YS, 0).astype(f32)


def shards(edge_inputs, image_counts, w_qkv, w_proj, w_fc1, w_fc2, vectors, fc1_bias):
    section = lax.axis_index("section")
    shard = lax.axis_index("shard")
    y = lax.axis_index("replica")
    x, z, c = shard // 4, (shard // 2) % 2, shard % 2
    place = (x, z, c, y)
    source = edge_inputs[0, :, 0]
    present = (shard * YS + y < image_counts).astype(f32)
    layer_weights = gather_all(w_qkv[0], w_proj[0], w_fc1[0], w_fc2[0], vectors[0], fc1_bias[0], place)

    own = source.reshape(256, 1024)
    first_out, _ = forward_layer(own.astype(f32), layer_weights)
    received = passed_along(first_out.astype(bf16), 1)
    inputs = jnp.where(section == 0, own, received).astype(f32)
    output, saved = forward_layer(inputs, layer_weights)
    normed, mixed, second, activated = saved[0], saved[5], saved[8], saved[10]
    acts_a = with_twin(normed, c)
    acts_m = with_twin(mixed, c)
    acts_c = with_twin(second, c)
    acts_u = with_twin(activated, c)

    cotangent = (source.astype(f32) * present[:, None, None]).reshape(256, 1024)
    d_first, _, _, _ = backward_layer(inputs, cotangent, saved, layer_weights)
    received_grad = passed_along(d_first.astype(bf16), -1)
    upstream = jnp.where(section == 1, cotangent, received_grad.astype(f32))
    d_inputs, cots, g_small, g_bias = backward_layer(inputs, upstream, saved, layer_weights)
    d_qkv, d_proj, d_fc1, d_fc2 = [
        jnp.concatenate([v, from_shard(v, dc=1)], axis=0) for v in cots
    ]

    relative = lambda v: rolled(rolled(v, x, 0), z, 1)
    acts_a, acts_m, acts_c, acts_u = [relative(v) for v in (acts_a, acts_m, acts_c, acts_u)]
    product = lambda a, b: jnp.einsum("xzrt,tn->xzrn", a, b, preferred_element_type=f32)
    small = jnp.concatenate(
        [g_small.reshape(10, XS, ZS, CS, 64).transpose(1, 2, 3, 4, 0),
         g_bias.reshape(XS, ZS, CS, 4, 64).transpose(0, 1, 2, 4, 3)], axis=-1
    )
    mine = pick(small, c, 2)
    theirs = from_shard(pick(small, 1 - c, 2).astype(bf16), dc=1)
    small = relative(jnp.pad(mine + theirs.astype(f32), ((0, 0),) * 3 + ((0, 114),)))
    d_unit = jnp.concatenate(
        [
            product(acts_a, d_qkv).astype(bf16),
            product(acts_m, d_proj).astype(bf16),
            product(acts_u[:, :, 128:192], d_fc2).astype(bf16),
            product(acts_u[:, :, 192:], d_fc2).astype(bf16),
            small.astype(bf16),
        ],
        axis=-1,
    )
    acts_y = rolled(acts_u[:, :, :128].reshape(XS, ZS, YS, 32, 512), y, 2)
    d_fc1_y = rolled(d_fc1.reshape(512, YS, 1024), y, 1)
    chunks = [
        jnp.concatenate(
            [product(acts_c, d_fc1_y[:, dy]).astype(bf16), product(acts_y[:, :, dy], d_fc2).astype(bf16)],
            axis=2,
        )
        for dy in range(YS)
    ]
    rows = scatter_rows(chunks, y)
    columns = summed_over_replicas(scatter_columns(d_unit), y)
    grad_qkv = columns[:, :3072]
    grad_proj = columns[:, 3072:4096]
    grad_fc1 = rows[:, :64].transpose(1, 0, 2).reshape(64, 4096)
    grad_fc2 = jnp.concatenate(
        [rows[:, 64:].reshape(128, 1024), columns[:, 4096:5120], columns[:, 5120:6144]], axis=0
    )
    grad_vec = columns[:, 6144:6154].T
    grad_bias = columns[:, 6154:6158].T.reshape(256)
    edge_values = jnp.where(section == 0, d_inputs, output).reshape(1, 2, 1, 128, 1024)
    return (
        edge_values,
        grad_qkv[None],
        grad_proj[None],
        grad_fc1[None],
        grad_fc2[None],
        grad_vec[None],
        grad_bias[None],
    )


def solution(mesh):
    placed = (
        P("section", None, ("shard", "replica"), None, None),
        P(),
        P("section", "shard", None),
        P("section", "shard", None),
        P("section", "shard", None),
        P("section", "shard", None),
        P("section", None, "shard"),
        P("section", "shard"),
    )
    return jax.shard_map(
        shards,
        mesh=mesh,
        in_specs=placed,
        out_specs=(placed[0],) + placed[2:],
        check_vma=False,
    )
```

```python
import jax
import jax.numpy as jnp
from jax import lax
from jax.experimental import pallas as pl
from jax.experimental.pallas import tpu as pltpu
from jax.sharding import PartitionSpec as P

XS, ZS, CS, YS = 4, 2, 2, 4
T = 256
D, FF = 1024, 4096
UNIT = 6272
QP = 4224
epsilon = 1e-06
bf16, f32 = jnp.bfloat16, jnp.float32
ANY = pl.BlockSpec(memory_space=pl.ANY)
VM = pl.BlockSpec(memory_space=pltpu.VMEM)
NT = (((1,), (1,)), ((), ()))
TN = (((0,), (0,)), ((), ()))


def shard_of(x, z, c):
    return (x % XS) * 4 + (z % ZS) * 2 + (c % CS)


def from_shard(value, dx=0, dz=0, dc=0):
    pairs = [
        (shard_of(x + dx, z + dz, c + dc), shard_of(x, z, c))
        for x in range(XS)
        for z in range(ZS)
        for c in range(CS)
    ]
    return lax.ppermute(value, "shard", pairs)


def from_replica(value, dy):
    return lax.ppermute(value, "replica", [((y + dy) % YS, y) for y in range(YS)])


def passed_along(value, steps):
    return lax.ppermute(value, "section", [(0, 1)] if steps == 1 else [(1, 0)])


def place():
    shard = lax.axis_index("shard")
    x = lax.div(shard, jnp.int32(4))
    z = lax.rem(lax.div(shard, jnp.int32(2)), jnp.int32(2))
    c = lax.rem(shard, jnp.int32(2))
    return x, z, c, lax.axis_index("replica")


def near(base, step, size):
    return lax.rem(base + jnp.int32(step), jnp.int32(size))


def call(kernel, outs, args, kinds, scratch=(), flops=0, moved=0, out_kinds=None, name=None):
    return pl.pallas_call(
        kernel,
        out_shape=[jax.ShapeDtypeStruct(s, d) for s, d in outs],
        in_specs=list(kinds),
        out_specs=list(out_kinds or [VM] * len(outs)),
        scratch_shapes=list(scratch),
        compiler_params=pltpu.CompilerParams(vmem_limit_bytes=56 * 2**20),
        cost_estimate=pl.CostEstimate(flops=flops, bytes_accessed=moved, transcendentals=0),
        name=name,
    )(*args)


def dot(a, b, dims=(((1,), (0,)), ((), ()))):
    return lax.dot_general(a, b, dims, preferred_element_type=f32)


def stats(values):
    average = jnp.mean(values, axis=-1, keepdims=True)
    centered = values - average
    spread = jnp.mean(centered * centered, axis=-1, keepdims=True)
    scale = lax.rsqrt(spread + epsilon)
    return centered * scale, scale


def norm_back(grad, gain, hat, scale):
    d_hat = grad * gain
    d_in = scale * (
        d_hat - jnp.mean(d_hat, axis=-1, keepdims=True) - hat * jnp.mean(d_hat * hat, axis=-1, keepdims=True)
    )
    return d_in, jnp.sum(grad * hat, axis=0, keepdims=True), jnp.sum(grad, axis=0, keepdims=True)


def pack_kernel(qkv, proj, fc1, fc2, vectors, bias, unit, piece, small, sems):
    _, _, _, y = place()
    small[...] = jnp.zeros_like(small)
    small[0:10, 0:64] = vectors[...].astype(f32)
    small[16:18, :] = bias[...].astype(f32)
    low = small[...].astype(bf16)
    copies = [
        pltpu.make_async_copy(fc1.at[:, pl.ds(pl.multiple_of(y * 1024, 1024), 1024)], piece.at[0:64], sems.at[0]),
        pltpu.make_async_copy(fc2.at[pl.ds(pl.multiple_of(y * 32, 32), 32)], piece.at[64:96], sems.at[1]),
        pltpu.make_async_copy(qkv, unit.at[:, 0:3072], sems.at[2]),
        pltpu.make_async_copy(proj, unit.at[:, 3072:4096], sems.at[3]),
        pltpu.make_async_copy(fc2.at[128:192], unit.at[:, 4096:5120], sems.at[4]),
        pltpu.make_async_copy(fc2.at[192:256], unit.at[:, 5120:6144], sems.at[5]),
    ]
    for copy in copies:
        copy.start()
    for copy in copies:
        copy.wait()
    unit[:, 6144:6272] = low


def pack(w_qkv, w_proj, w_fc1, w_fc2, vectors, fc1_bias):
    return call(
        pack_kernel,
        [((64, UNIT), bf16), ((96, 1024), bf16)],
        (w_qkv, w_proj, w_fc1, w_fc2, vectors, fc1_bias.reshape(2, 128)),
        [ANY] * 4 + [VM] * 2,
        scratch=[pltpu.VMEM((64, 128), f32), pltpu.SemaphoreType.DMA((6,))],
        moved=4 * 2**20,
        name="pack_parts",
    )


def halves_kernel(*refs):
    pieces, low, high, sems = refs[:8], refs[8], refs[9], refs[10]
    x, z, _, _ = place()
    waits = []
    for n, piece in enumerate(pieces):
        index = near(x, n // 2, XS) * 2 + near(z, n % 2, ZS)

        @pl.when(index < 4)
        def _(piece=piece, index=index, n=n):
            pltpu.make_async_copy(piece, low.at[index], sems.at[n]).start()

        @pl.when(index >= 4)
        def _(piece=piece, index=index, n=n):
            pltpu.make_async_copy(piece, high.at[index - 4], sems.at[n]).start()

        waits.append(pltpu.make_async_copy(piece, low.at[0], sems.at[n]))
    for copy in waits:
        copy.wait()


def halves(pieces):
    return call(
        halves_kernel,
        [((4, 96, 1024), bf16)] * 2,
        pieces,
        [ANY] * 8,
        scratch=[pltpu.SemaphoreType.DMA((8,))],
        out_kinds=[ANY] * 2,
        moved=4 * 2**20,
        name="place_pieces",
    )


def vectors_kernel(*refs):
    pieces, vec, bias, held, sems = refs[:16], refs[16], refs[17], refs[18], refs[19]
    x, z, c, _ = place()
    copies = []
    for n, piece in enumerate(pieces):
        k, dx, dz = n // 8, (n // 2) % 4, n % 2
        index = near(x, dx, XS) * 4 + near(z, dz, ZS) * 2 + near(c, k, CS)
        copies.append(pltpu.make_async_copy(piece.at[0:32, 6144:6272], held.at[index], sems.at[n]))
        copies[-1].start()
    for copy in copies:
        copy.wait()
    lane = lax.broadcasted_iota(jnp.int32, (16, 128), 1)
    for t in range(8):
        a = held[2 * t, 0:16].astype(f32)
        b = held[2 * t + 1, 0:16].astype(f32)
        vec[:, t * 128 : t * 128 + 128] = jnp.where(lane < 64, a, pltpu.roll(b, 64, 1))
    for s in range(16):
        tail = held[s, 16:32].astype(f32)
        bias[0:1, s * 256 : s * 256 + 128] = tail[0:1]
        bias[0:1, s * 256 + 128 : s * 256 + 256] = tail[1:2]


def gathered_vectors(columns):
    flat = [columns[k][dx][dz] for k in range(CS) for dx in range(XS) for dz in range(ZS)]
    return call(
        vectors_kernel,
        [((16, 1024), f32), ((1, FF), f32)],
        flat,
        [ANY] * 16,
        scratch=[pltpu.VMEM((16, 32, 128), bf16), pltpu.SemaphoreType.DMA((16,))],
        moved=2**20,
        name="gathered_vectors",
    )


def column_copies(pieces, target, low, high, sems):
    x, z, c, _ = place()
    out = []
    for n, piece in enumerate(pieces):
        k, dx, dz = n // 8, (n // 2) % 4, n % 2
        xz = near(x, dx, XS) * 2 + near(z, dz, ZS)
        out.append(pltpu.make_async_copy(piece.at[:, low:high], target(xz, near(c, k, CS)), sems.at[n]))
    return out


def attention_weights(pieces, w_qkv, w_proj, sems):
    a = column_copies(pieces, lambda xz, c: w_qkv.at[xz, c], 0, 3072, sems.at[0])
    b = column_copies(pieces, lambda xz, c: w_proj.at[xz, c], 3072, 4096, sems.at[1])
    return a, b


ATTENTION_SCRATCH = [
    pltpu.VMEM((8, 2, 64, 3072), bf16),
    pltpu.VMEM((8, 2, 64, 1024), bf16),
    pltpu.SemaphoreType.DMA((2, 16)),
]


def feed_weights(columns, rows, w1, w2, sems):
    x, z, c, y = place()
    first, second = [], []
    for n, piece in enumerate(rows):
        k, dy, half = n // 8, (n // 2) % 4, n % 2
        ck, yk = near(c, k, CS), near(y, dy, YS)
        first.append(pltpu.make_async_copy(piece.at[:, 0:64], w1.at[yk, 4 * half : 4 * half + 4, ck], sems.at[0, n]))
        second.append(
            pltpu.make_async_copy(
                piece.at[:, 64:96],
                w2.at[4 * half : 4 * half + 4, ck, pl.ds(pl.multiple_of(yk * 32, 32), 32)],
                sems.at[1, n],
            )
        )
    second += column_copies(columns, lambda xz, c: w2.at[xz, c, 128:192], 4096, 5120, sems.at[2])
    second += column_copies(columns, lambda xz, c: w2.at[xz, c, 192:256], 5120, 6144, sems.at[3])
    return first, second


FEED_SCRATCH = [
    pltpu.VMEM((4, 8, 2, 64, 1024), bf16),
    pltpu.VMEM((8, 2, 256, 1024), bf16),
    pltpu.SemaphoreType.DMA((4, 16)),
]


def start(copies):
    for copy in copies:
        copy.start()


def wait(copies):
    for copy in copies:
        copy.wait()


def stacked_heads(pair, lane):
    zero = jnp.zeros_like(pair)
    return jnp.concatenate([jnp.where(lane, pair, zero), jnp.where(lane, zero, pair)], axis=0)


def attention_forward_kernel(keep, x_ref, vec, *refs):
    pieces, refs = refs[:16], refs[16:]
    if keep:
        a_out, p_out, soft_out, m_out, o_out, x1_out, c_out, w_qkv, w_proj, sems = refs
    else:
        x1_out, c_out, w_qkv, w_proj, sems, p_out, m_out = refs
    first, second = attention_weights(pieces, w_qkv, w_proj, sems)
    start(first)
    start(second)
    x = x_ref[...].astype(f32)
    hat, _ = stats(x)
    a = (hat * vec[0:1, :] + vec[1:2, :]).astype(bf16)
    if keep:
        a_out[...] = a
    wait(first)
    for j in range(6):
        part = dot(a, w_qkv[:, :, :, j * 512 : j * 512 + 512].reshape(D, 512))
        if j < 2:
            part = part + vec[2:3, j * 512 : j * 512 + 512]
        if j >= 4:
            part = part + vec[3:4, j * 512 - 2048 : j * 512 - 1536]
        p_out[:, j * 512 : j * 512 + 512] = part.astype(bf16)
    lane = lax.broadcasted_iota(jnp.int32, (128, 128), 1) < 64

    def unit(u, _):
        i, h = lax.div(u, jnp.int32(8)), lax.rem(u, jnp.int32(8))
        rows = pl.ds(pl.multiple_of(i * 128, 128), 128)
        q, k, v = [p_out[rows, pl.ds(pl.multiple_of(h * 128 + o, 128), 128)] for o in (0, 1024, 2048)]
        s = dot(stacked_heads(q, lane), k, NT) * 0.125
        e = jnp.exp(s - jnp.max(s, axis=-1, keepdims=True))
        soft = e / jnp.sum(e, axis=-1, keepdims=True)
        if keep:
            soft_out[u] = soft
        mixed = dot(soft.astype(bf16), v)
        m_out[rows, pl.ds(pl.multiple_of(h * 128, 128), 128)] = jnp.where(lane, mixed[:128], mixed[128:]).astype(bf16)
        return 0

    lax.fori_loop(0, 16, unit, 0, unroll=4)
    wait(second)
    o = dot(m_out[...], w_proj[...].reshape(D, D)) + vec[4:5, :]
    x1 = x + vec[5:6, :] * o
    if keep:
        o_out[...] = o
    x1_out[...] = x1
    hat, _ = stats(x1)
    c_out[...] = (hat * vec[6:7, :] + vec[7:8, :]).astype(bf16)


def attention_forward(keep, x, vec, columns):
    flat = [columns[k][dx][dz] for k in range(CS) for dx in range(XS) for dz in range(ZS)]
    outs = [((T, D), f32), ((T, D), bf16)]
    scratch = list(ATTENTION_SCRATCH)
    if keep:
        outs = [((T, D), bf16), ((T, 3072), bf16), ((16, 256, 128), f32), ((T, D), bf16), ((T, D), f32)] + outs
    else:
        scratch += [pltpu.VMEM((T, 3072), bf16), pltpu.VMEM((T, D), bf16)]
    return call(
        lambda *refs: attention_forward_kernel(keep, *refs),
        outs,
        [x, vec] + flat,
        [VM, VM] + [ANY] * 16,
        scratch=scratch,
        flops=2 * T * D * 4 * D,
        moved=14 * 2**20,
        name="attention_forward",
    )


def feed_forward_kernel(keep, x1_ref, c_ref, vec, bias, *refs):
    columns, rows, refs = refs[:16], refs[16:32], refs[32:]
    if keep:
        u_out, gp_out, f_out, y_out, w1, w2, sems = refs
    else:
        y_out, w1, w2, sems = refs
    first, second = feed_weights(columns, rows, w1, w2, sems)
    start(first)
    start(second)
    c = c_ref[...]
    total = None
    wait(first)
    for t in range(8):
        y, off = t // 2, (t % 2) * 512
        h = dot(c, w1[y, :, :, :, off : off + 512].reshape(D, 512)) + bias[0:1, t * 512 : t * 512 + 512]
        cdf = 0.5 * (1.0 + lax.erf(h * 0.7071067811865476))
        u = (h * cdf).astype(bf16)
        if keep:
            gp = cdf + h * (jnp.exp(-0.5 * h * h) * 0.3989422804014327)
            u_out[:, t * 512 : t * 512 + 512] = u
            gp_out[:, t * 512 : t * 512 + 512] = gp.astype(bf16)
        if t == 0:
            wait(second)
        part = dot(u, w2[t].reshape(512, D))
        total = part if total is None else total + part
    f = total + vec[8:9, :]
    if keep:
        f_out[...] = f
    y_out[...] = (x1_ref[...] + vec[9:10, :] * f).astype(y_out.dtype)


def feed_forward(keep, x1, c, vec, bias, columns, rows):
    flat = [columns[k][dx][dz] for k in range(CS) for dx in range(XS) for dz in range(ZS)]
    flat += [rows[k][dy][half] for k in range(CS) for dy in range(YS) for half in range(2)]
    outs = [((T, D), f32 if keep else bf16)]
    if keep:
        outs = [((T, FF), bf16), ((T, FF), bf16), ((T, D), f32)] + outs
    return call(
        lambda *refs: feed_forward_kernel(keep, *refs),
        outs,
        [x1, c, vec, bias] + flat,
        [VM] * 4 + [ANY] * 32,
        scratch=FEED_SCRATCH,
        flops=4 * T * D * FF,
        moved=24 * 2**20,
        name="feed_forward",
    )


def feed_backward_kernel(g_ref, f_ref, gp_ref, x1_ref, o_ref, vec, *refs):
    columns, rows, refs = refs[:16], refs[16:32], refs[32:]
    df_out, dh_out, dx1_out, do_out, small, gbias, w1, w2, sems = refs
    first, second = feed_weights(columns, rows, w1, w2, sems)
    start(second)
    start(first)
    g = g_ref[...]
    df = (vec[9:10, :] * g).astype(bf16)
    df_out[...] = df
    small[8:9, :] = jnp.sum(df.astype(f32), axis=0, keepdims=True)
    small[9:10, :] = jnp.sum(g * f_ref[...], axis=0, keepdims=True)
    small[0:4, :] = jnp.zeros((4, D), f32)
    small[10:16, :] = jnp.zeros((6, D), f32)
    wait(second)
    total = None
    for t in range(8):
        y, off = t // 2, (t % 2) * 512
        cols = slice(t * 512, t * 512 + 512)
        du = dot(df, w2[t].reshape(512, D), NT)
        dh = (gp_ref[:, cols].astype(f32) * du).astype(bf16)
        dh_out[:, cols] = dh
        gbias[0:1, cols] = jnp.sum(dh.astype(f32), axis=0, keepdims=True)
        if t == 0:
            wait(first)
        part = dot(dh, w1[y, :, :, :, off : off + 512].reshape(D, 512), NT)
        total = part if total is None else total + part
    hat, scale = stats(x1_ref[...])
    d_norm, small[6:7, :], small[7:8, :] = norm_back(total, vec[6:7, :], hat, scale)
    dx1 = g + d_norm
    dx1_out[...] = dx1
    small[5:6, :] = jnp.sum(dx1 * o_ref[...], axis=0, keepdims=True)
    do = (vec[5:6, :] * dx1).astype(bf16)
    do_out[...] = do
    small[4:5, :] = jnp.sum(do.astype(f32), axis=0, keepdims=True)


def feed_backward(g, f, gp, x1, o, vec, columns, rows):
    flat = [columns[k][dx][dz] for k in range(CS) for dx in range(XS) for dz in range(ZS)]
    flat += [rows[k][dy][half] for k in range(CS) for dy in range(YS) for half in range(2)]
    return call(
        feed_backward_kernel,
        [((T, D), bf16), ((T, FF), bf16), ((T, D), f32), ((T, D), bf16), ((16, D), f32), ((1, FF), f32)],
        [g, f, gp, x1, o, vec] + flat,
        [VM] * 6 + [ANY] * 32,
        scratch=FEED_SCRATCH,
        flops=4 * T * D * FF,
        moved=26 * 2**20,
        name="feed_backward",
    )


def attention_backward_kernel(do_ref, dx1_ref, x_ref, p_ref, soft_ref, vec, *refs):
    pieces, refs = refs[:16], refs[16:]
    dp_out, dx_out, small, w_qkv, w_proj, sems, dm_ref = refs
    first, second = attention_weights(pieces, w_qkv, w_proj, sems)
    start(second)
    start(first)
    wait(second)
    dm_ref[...] = dot(do_ref[...], w_proj[...].reshape(D, D), NT).astype(bf16)
    lane = lax.broadcasted_iota(jnp.int32, (128, 128), 1) < 64

    def unit(u, _):
        i, h = lax.div(u, jnp.int32(8)), lax.rem(u, jnp.int32(8))
        rows = pl.ds(pl.multiple_of(i * 128, 128), 128)
        at = lambda o: pl.ds(pl.multiple_of(h * 128 + o, 128), 128)
        q, k, v = [p_ref[rows, at(o)] for o in (0, 1024, 2048)]
        dm = stacked_heads(dm_ref[rows, at(0)], lane)
        soft = soft_ref[u]
        dp_out[rows, at(2048)] = dot(soft.astype(bf16), dm, TN).astype(bf16)
        dw = dot(dm, v, NT)
        ds = (soft * (dw - jnp.sum(soft * dw, axis=-1, keepdims=True))).astype(bf16)
        dq = dot(ds, k) * 0.125
        dp_out[rows, at(0)] = jnp.where(lane, dq[:128], dq[128:]).astype(bf16)
        dp_out[rows, at(1024)] = (dot(ds, stacked_heads(q, lane), TN) * 0.125).astype(bf16)
        return 0

    lax.fori_loop(0, 16, unit, 0, unroll=4)
    small[2:3, :] = jnp.sum(dp_out[:, 0:1024].astype(f32), axis=0, keepdims=True)
    small[3:4, :] = jnp.sum(dp_out[:, 2048:3072].astype(f32), axis=0, keepdims=True)
    small[4:16, :] = jnp.zeros((12, D), f32)
    wait(first)
    total = None
    for j in range(6):
        cols = slice(j * 512, j * 512 + 512)
        part = dot(dp_out[:, cols], w_qkv[:, :, :, cols].reshape(D, 512), NT)
        total = part if total is None else total + part
    hat, scale = stats(x_ref[...].astype(f32))
    d_norm, small[0:1, :], small[1:2, :] = norm_back(total, vec[0:1, :], hat, scale)
    dx_out[...] = dx1_ref[...] + d_norm


def attention_backward(do, dx1, x, p, soft, vec, columns):
    flat = [columns[k][dx][dz] for k in range(CS) for dx in range(XS) for dz in range(ZS)]
    return call(
        attention_backward_kernel,
        [((T, 3072), bf16), ((T, D), f32), ((16, D), f32)],
        [do, dx1, x, p, soft, vec] + flat,
        [VM] * 6 + [ANY] * 16,
        scratch=list(ATTENTION_SCRATCH) + [pltpu.VMEM((T, D), bf16)],
        flops=2 * T * D * 4 * D,
        moved=18 * 2**20,
        name="attention_backward",
    )


def picked_kernel(a_ref, m_ref, c_ref, u_ref, mine, theirs):
    x, z, c, _ = place()
    row = lax.broadcasted_iota(jnp.int32, (512, D), 0)
    col = lax.broadcasted_iota(jnp.int32, (512, D), 1)
    eye_r = lax.broadcasted_iota(jnp.int32, (256, 256), 0)
    eye = jnp.where(eye_r == lax.broadcasted_iota(jnp.int32, (256, 256), 1), 1.0, 0.0).astype(bf16)
    dx, dz, inner = row >> 7, (row >> 6) & 1, row & 63
    base = (((x + dx) & 3) << 8) + (((z + dz) & 1) << 7) + inner
    for k, out in enumerate((mine, theirs)):
        ck = near(c, k, CS)
        chosen = jnp.where(col == base + ck * 64, 1.0, 0.0).astype(bf16)
        for n, ref in enumerate((a_ref, m_ref, c_ref)):
            out[n * 512 : n * 512 + 512, :] = dot(chosen, ref[...], NT).astype(bf16)
        for j in range(8):
            s = near(x, j // 2, XS) * 4 + near(z, j % 2, ZS) * 2 + ck
            block = u_ref[:, pl.ds(pl.multiple_of(s * 256, 256), 256)]
            out[1536 + j * 256 : 1792 + j * 256, :] = dot(eye, block, NT).astype(bf16)


def picked(a, m, c, u):
    return call(
        picked_kernel,
        [((3584, T), bf16)] * 2,
        [a, m, c, u],
        [VM] * 4,
        flops=2 * 10**9,
        moved=8 * 2**20,
        name="transposed_acts",
    )


def feed_grads_kernel(mine, theirs, dh, dh2, df, df2, *refs):
    outs, acts, dh_all, df_all, rows, tail, sems, out_sems = refs[:16], *refs[16:]
    _, _, _, y = place()
    copies = [
        pltpu.make_async_copy(mine.at[1024:3584], acts.at[:, 0:256], sems.at[0]),
        pltpu.make_async_copy(theirs.at[1024:3584], acts.at[:, 256:512], sems.at[1]),
        pltpu.make_async_copy(df, df_all.at[0:256], sems.at[2]),
        pltpu.make_async_copy(df2, df_all.at[256:512], sems.at[3]),
        pltpu.make_async_copy(dh, dh_all.at[0:256], sems.at[4]),
        pltpu.make_async_copy(dh2, dh_all.at[256:512], sems.at[5]),
    ]
    start(copies)
    wait(copies[:4])
    sends = []
    for j in range(8):
        grad = dot(acts[512 + j * 256 : 768 + j * 256, :], df_all[...]).astype(bf16)
        tail[j, :, 0:1024] = grad[128:192]
        tail[j, :, 1024:2048] = grad[192:256]
        sends.append(pltpu.make_async_copy(tail.at[j], outs[8 + j], out_sems.at[8 + j]))
        sends[-1].start()
        for yk in range(YS):
            dy = near(jnp.int32(yk + YS) - y, 0, YS)
            rows[dy, j // 4, j % 4, 64:96] = grad[yk * 32 : yk * 32 + 32]
    wait(copies[4:])
    for dy in (2, 1, 3, 0):
        start_col = pl.multiple_of(near(y, dy, YS) * 1024, 1024)
        for half in range(2):
            grad = dot(acts[half * 256 : half * 256 + 256, :], dh_all[:, pl.ds(start_col, 1024)]).astype(bf16)
            rows[dy, half, :, 0:64] = grad.reshape(4, 64, 1024)
            sends.append(pltpu.make_async_copy(rows.at[dy, half], outs[dy * 2 + half], out_sems.at[dy * 2 + half]))
            sends[-1].start()
    wait(sends)


def feed_grads(mine, theirs, dh, dh2, df, df2):
    out = call(
        feed_grads_kernel,
        [((4, 96, 1024), bf16)] * 8 + [((64, 2048), bf16)] * 8,
        [mine, theirs, dh, dh2, df, df2],
        [ANY] * 6,
        scratch=[
            pltpu.VMEM((2560, 512), bf16),
            pltpu.VMEM((512, FF), bf16),
            pltpu.VMEM((512, D), bf16),
            pltpu.VMEM((4, 2, 4, 96, 1024), bf16),
            pltpu.VMEM((8, 64, 2048), bf16),
            pltpu.SemaphoreType.DMA((6,)),
            pltpu.SemaphoreType.DMA((16,)),
        ],
        out_kinds=[ANY] * 16,
        flops=8 * T * D * FF,
        moved=24 * 2**20,
        name="feed_grads",
    )
    return [[out[dy * 2], out[dy * 2 + 1]] for dy in range(YS)], out[8:]


def attention_grads_kernel(mine, theirs, dp, dp2, do, do2, s1, s2, s3, s4, b1, b2, *refs):
    outs, acts, dp_all, do_all, held, sems, out_sems = refs[:8], *refs[8:]
    x, z, c, _ = place()
    copies = [
        pltpu.make_async_copy(mine.at[0:1024], acts.at[:, 0:256], sems.at[0]),
        pltpu.make_async_copy(theirs.at[0:1024], acts.at[:, 256:512], sems.at[1]),
        pltpu.make_async_copy(do, do_all.at[0:256], sems.at[2]),
        pltpu.make_async_copy(do2, do_all.at[256:512], sems.at[3]),
        pltpu.make_async_copy(dp, dp_all.at[0:256], sems.at[4]),
        pltpu.make_async_copy(dp2, dp_all.at[256:512], sems.at[5]),
    ]
    start(copies)
    vec = (s1[...] + s2[...] + s3[...] + s4[...]).astype(bf16)
    row = lax.broadcasted_iota(jnp.int32, (D, 128), 0)
    col = lax.broadcasted_iota(jnp.int32, (D, 128), 1)
    for j in range(8):
        s = near(x, j // 2, XS) * 4 + near(z, j % 2, ZS) * 2 + c
        chosen = jnp.where((row == col + s * 64) & (col < 64), 1.0, 0.0).astype(bf16)
        held[j, :, 4096:4224] = jnp.zeros((64, 128), bf16)
        held[j, 0:16, 4096:4224] = dot(vec, chosen).astype(bf16)
        a = b1[0:1, pl.ds(pl.multiple_of(s * 256, 256), 128)] + b2[0:1, pl.ds(pl.multiple_of(s * 256, 256), 128)]
        b = b1[0:1, pl.ds(pl.multiple_of(s * 256 + 128, 128), 128)] + b2[0:1, pl.ds(pl.multiple_of(s * 256 + 128, 128), 128)]
        line = lax.broadcasted_iota(jnp.int32, (16, 128), 0)
        held[j, 16:32, 4096:4224] = jnp.where(line == 0, a, jnp.where(line == 1, b, 0.0)).astype(bf16)
    wait(copies[:4])
    for n in range(2):
        grad = dot(acts[512:1024, :], do_all[:, n * 512 : n * 512 + 512]).astype(bf16)
        held[:, :, 3072 + n * 512 : 3584 + n * 512] = grad.reshape(8, 64, 512)
    wait(copies[4:])
    for n in range(6):
        grad = dot(acts[0:512, :], dp_all[:, n * 512 : n * 512 + 512]).astype(bf16)
        held[:, :, n * 512 : n * 512 + 512] = grad.reshape(8, 64, 512)
    sends = [pltpu.make_async_copy(held.at[j], outs[j], out_sems.at[j]) for j in range(8)]
    start(sends)
    wait(sends)


def attention_grads(mine, theirs, dp, dp2, do, do2, smalls, biases):
    return call(
        attention_grads_kernel,
        [((64, QP), bf16)] * 8,
        [mine, theirs, dp, dp2, do, do2] + smalls + biases,
        [ANY] * 6 + [VM] * 6,
        scratch=[
            pltpu.VMEM((1024, 512), bf16),
            pltpu.VMEM((512, 3072), bf16),
            pltpu.VMEM((512, D), bf16),
            pltpu.VMEM((8, 64, QP), bf16),
            pltpu.SemaphoreType.DMA((6,)),
            pltpu.SemaphoreType.DMA((8,)),
        ],
        out_kinds=[ANY] * 8,
        flops=8 * T * D * 2 * D,
        moved=16 * 2**20,
        name="attention_grads",
    )


def sum_kernel(count, *refs):
    total = refs[0][...].astype(f32)
    for ref in refs[1:count]:
        total = total + ref[...].astype(f32)
    outs = refs[count:]
    if len(outs) == 1:
        outs[0][...] = total.astype(bf16)
    else:
        for n, out in enumerate(outs):
            out[...] = total[n].astype(bf16)


def summed(parts, split=False):
    shape = parts[0].shape
    outs = [(shape[1:], bf16)] * shape[0] if split else [(shape, bf16)]
    size = 1
    for n in shape:
        size *= n
    out = call(
        lambda *refs: sum_kernel(len(parts), *refs),
        outs,
        parts,
        [VM] * len(parts),
        flops=size * len(parts),
        moved=2 * size * (len(parts) + 1),
        name="summed",
    )
    return out if split else out[0]


def scatter_columns(parts):
    far_a = from_shard(parts[4], dx=3)
    far_b = from_shard(parts[5], dx=1)
    plus_b = from_shard(parts[3], dx=3)
    minus_a = from_shard(parts[6], dx=1)
    plus_a = from_shard(summed([parts[2], far_a]), dx=3)
    minus_b = from_shard(summed([parts[7], far_b]), dx=1)
    other = summed([parts[1], plus_b, minus_b])
    got = from_shard(other, dz=1)
    return summed([parts[0], plus_a, minus_a, got])


def scatter_rows(parts):
    far_a = from_replica(parts[2][0], 3)
    far_b = from_replica(parts[2][1], 1)
    plus_b = from_replica(parts[1][1], 3)
    minus_a = from_replica(parts[3][0], 1)
    plus_a = from_replica(summed([parts[1][0], far_a]), 3)
    minus_b = from_replica(summed([parts[3][1], far_b]), 1)
    high = summed([parts[0][1], plus_b, minus_b], split=True)
    low = summed([parts[0][0], plus_a, minus_a], split=True)
    places = low + high
    got = [
        from_shard(places[2 * dx + dz], dx=XS - dx, dz=dz)
        for dx in range(XS)
        for dz in range(ZS)
        if (dx, dz) != (0, 0)
    ]
    return summed([places[0]] + got)


def own_quarter(part, y):
    quarters = part.reshape(YS, 16, -1)
    at = lambda dy: lax.dynamic_index_in_dim(quarters, lax.rem(y + dy, YS), 0, keepdims=False)
    return summed([at(0)] + [from_replica(at(dy), YS - dy) for dy in range(1, YS)])


def results_kernel(*refs):
    rows, columns, tails = refs[0:4], refs[4:8], refs[8:12]
    g_qkv, g_proj, g_fc1, g_fc2, g_vec, g_bias, rows_all, cols_all, tail_all, sems = refs[12:]
    _, _, _, y = place()
    copies = []
    for dy in range(YS):
        yk = near(y, dy, YS)
        copies.append(pltpu.make_async_copy(rows[dy], rows_all.at[yk], sems.at[0, dy]))
        copies.append(pltpu.make_async_copy(columns[dy], cols_all.at[yk], sems.at[1, dy]))
        copies.append(pltpu.make_async_copy(tails[dy], tail_all.at[yk], sems.at[2, dy]))
    start(copies)
    wait(copies)
    for k in range(YS):
        g_fc1[:, k * 1024 : k * 1024 + 1024] = rows_all[k, 0:64].astype(f32)
        g_fc2[k * 32 : k * 32 + 32, :] = rows_all[k, 64:96].astype(f32)
        line = slice(k * 16, k * 16 + 16)
        g_qkv[line, :] = cols_all[k, :, 0:3072].astype(f32)
        g_proj[line, :] = cols_all[k, :, 3072:4096].astype(f32)
        g_fc2[128 + k * 16 : 144 + k * 16, :] = tail_all[k, :, 0:1024].astype(f32)
        g_fc2[192 + k * 16 : 208 + k * 16, :] = tail_all[k, :, 1024:2048].astype(f32)
    g_vec[...] = cols_all[0, :, 4096:4224].astype(f32)
    g_bias[...] = cols_all[1, :, 4096:4224].astype(f32)


def results(rows, columns, tails):
    return call(
        results_kernel,
        [((64, 3072), f32), ((64, 1024), f32), ((64, FF), f32), ((256, D), f32), ((16, 128), f32), ((16, 128), f32)],
        list(rows) + list(columns) + list(tails),
        [ANY] * 12,
        scratch=[
            pltpu.VMEM((4, 96, 1024), bf16),
            pltpu.VMEM((4, 16, QP), bf16),
            pltpu.VMEM((4, 16, 2048), bf16),
            pltpu.SemaphoreType.DMA((3, 4)),
        ],
        moved=10 * 2**20,
        name="results",
    )


def gather(w_qkv, w_proj, w_fc1, w_fc2, vectors, fc1_bias):
    unit, piece = pack(w_qkv, w_proj, w_fc1, w_fc2, vectors, fc1_bias)
    pieces = [
        piece if (dx, dz) == (0, 0) else from_shard(piece, dx=dx, dz=dz) for dx in range(XS) for dz in range(ZS)
    ]
    other = from_shard(unit, dz=1)
    plus = [from_shard(unit, dx=1), from_shard(other, dx=1)]
    minus = [from_shard(unit, dx=3), from_shard(other, dx=3)]
    far = [from_shard(plus[0], dx=1), from_shard(minus[1], dx=3)]
    mine = [[unit, other], plus, far, minus]
    columns = [mine, [[from_shard(v, dc=1) for v in pair] for pair in mine]]
    here = halves(pieces)
    up = [from_replica(v, 1) for v in here]
    down = [from_replica(v, 3) for v in here]
    opposite = [from_replica(up[0], 1), from_replica(down[1], 3)]
    mine = [here, up, opposite, down]
    rows = [mine, [[from_shard(v, dc=1) for v in pair] for pair in mine]]
    return columns, rows


def shards(edge_inputs, image_counts, w_qkv, w_proj, w_fc1, w_fc2, vectors, fc1_bias):
    section = lax.axis_index("section")
    _, _, _, y = place()
    source = edge_inputs[0, :, 0]
    present = (lax.axis_index("shard") * YS + y < image_counts).astype(f32)
    columns, rows = gather(w_qkv[0], w_proj[0], w_fc1[0], w_fc2[0], vectors[0], fc1_bias[0])
    vec, bias = gathered_vectors(columns)

    own = source.reshape(T, D)
    x1, c = attention_forward(False, own, vec, columns)
    (first_out,) = feed_forward(False, x1, c, vec, bias, columns, rows)
    received = passed_along(first_out, 1)
    inputs = jnp.where(section == 0, own, received)
    a, p, soft, m, o, x1, c = attention_forward(True, inputs, vec, columns)
    u, gp, f, output = feed_forward(True, x1, c, vec, bias, columns, rows)

    cotangent = (source.astype(f32) * present[:, None, None]).reshape(T, D)
    _, _, dx1, do, _, _ = feed_backward(cotangent, f, gp, x1, o, vec, columns, rows)
    _, dx, _ = attention_backward(do, dx1, inputs, p, soft, vec, columns)
    received_grad = passed_along(dx.astype(bf16), -1)
    mine, theirs = picked(a, m, c, u)
    theirs = from_shard(theirs, dc=1)
    upstream = jnp.where(section == 1, cotangent, received_grad.astype(f32))
    df, dh, dx1, do, small_a, gbias = feed_backward(upstream, f, gp, x1, o, vec, columns, rows)
    dp, dx, small_b = attention_backward(do, dx1, inputs, p, soft, vec, columns)
    twin = lambda v: from_shard(v, dc=1)
    row_parts, tail_parts = feed_grads(mine, theirs, dh, twin(dh), df, twin(df))
    tail = own_quarter(scatter_columns(tail_parts), y)
    row = scatter_rows(row_parts)
    column_parts = attention_grads(
        mine, theirs, dp, twin(dp), do, twin(do), [small_a, twin(small_a), small_b, twin(small_b)], [gbias, twin(gbias)]
    )
    column = own_quarter(scatter_columns(column_parts), y)
    around = lambda v: [v] + [from_replica(v, dy) for dy in range(1, YS)]
    g_qkv, g_proj, g_fc1, g_fc2, g_vec, g_bias = results(around(row), around(column), around(tail))
    edge_values = jnp.where(section == 0, dx, output).reshape(1, 2, 1, 128, D)
    return (
        edge_values,
        g_qkv[None],
        g_proj[None],
        g_fc1[None],
        g_fc2[None],
        g_vec[None, :10, :64],
        g_bias[:2].reshape(1, 256),
    )


def solution(mesh):
    placed = (
        P("section", None, ("shard", "replica"), None, None),
        P(),
        P("section", "shard", None),
        P("section", "shard", None),
        P("section", "shard", None),
        P("section", "shard", None),
        P("section", None, "shard"),
        P("section", "shard"),
    )
    return jax.shard_map(
        shards,
        mesh=mesh,
        in_specs=placed,
        out_specs=(placed[0],) + placed[2:],
        check_vma=False,
    )
```

```python
import jax
import jax.numpy as jnp
from jax import lax
from jax.experimental import pallas as pl
from jax.experimental.pallas import tpu as pltpu
from jax.sharding import PartitionSpec as P

XS, ZS, CS, YS = 4, 2, 2, 4
T = 256
D, FF = 1024, 4096
GROWS = 48
TAILS = 4 - GROWS // 16
UNIT = 4096 + 1024 * TAILS + 128
QP = 4224
epsilon = 1e-06
bf16, f32 = jnp.bfloat16, jnp.float32
ANY = pl.BlockSpec(memory_space=pl.ANY)
VM = pl.BlockSpec(memory_space=pltpu.VMEM)
NT = (((1,), (1,)), ((), ()))
TN = (((0,), (0,)), ((), ()))


def shard_of(x, z, c):
    return (x % XS) * 4 + (z % ZS) * 2 + (c % CS)


def from_shard(value, dx=0, dz=0, dc=0):
    pairs = [
        (shard_of(x + dx, z + dz, c + dc), shard_of(x, z, c))
        for x in range(XS)
        for z in range(ZS)
        for c in range(CS)
    ]
    return lax.ppermute(value, "shard", pairs)


def from_replica(value, dy):
    return lax.ppermute(value, "replica", [((y + dy) % YS, y) for y in range(YS)])


def onward(value, axis):
    pairs = []
    for x in range(XS):
        for z in range(ZS):
            for c in range(CS):
                for y in range(YS):
                    step = 1 - 2 * c
                    tx, ty = (x + step, y) if axis == "x" else (x, y + step)
                    pairs.append((shard_of(x, z, c) * YS + y, shard_of(tx, z, c) * YS + ty % YS))
    return lax.ppermute(value, ("shard", "replica"), pairs)


def passed_along(value, steps):
    return lax.ppermute(value, "section", [(0, 1)] if steps == 1 else [(1, 0)])


def place():
    shard = lax.axis_index("shard")
    x = lax.div(shard, jnp.int32(4))
    z = lax.rem(lax.div(shard, jnp.int32(2)), jnp.int32(2))
    c = lax.rem(shard, jnp.int32(2))
    return x, z, c, lax.axis_index("replica")


def near(base, step, size):
    return lax.rem(base + jnp.int32(step), jnp.int32(size))


def call(kernel, outs, args, kinds, scratch=(), flops=0, moved=0, out_kinds=None, name=None):
    return pl.pallas_call(
        kernel,
        out_shape=[jax.ShapeDtypeStruct(s, d) for s, d in outs],
        in_specs=list(kinds),
        out_specs=list(out_kinds or [VM] * len(outs)),
        scratch_shapes=list(scratch),
        compiler_params=pltpu.CompilerParams(vmem_limit_bytes=56 * 2**20),
        cost_estimate=pl.CostEstimate(flops=flops, bytes_accessed=moved, transcendentals=0),
        name=name,
    )(*args)


def dot(a, b, dims=(((1,), (0,)), ((), ()))):
    return lax.dot_general(a, b, dims, preferred_element_type=f32)


def stats(values):
    average = jnp.mean(values, axis=-1, keepdims=True)
    centered = values - average
    spread = jnp.mean(centered * centered, axis=-1, keepdims=True)
    scale = lax.rsqrt(spread + epsilon)
    return centered * scale, scale


def norm_back(grad, gain, hat, scale):
    d_hat = grad * gain
    d_in = scale * (
        d_hat - jnp.mean(d_hat, axis=-1, keepdims=True) - hat * jnp.mean(d_hat * hat, axis=-1, keepdims=True)
    )
    return d_in, jnp.sum(grad * hat, axis=0, keepdims=True), jnp.sum(grad, axis=0, keepdims=True)


def pack_kernel(qkv, proj, fc1, fc2, vectors, bias, unit, piece, small, sems):
    _, _, _, y = place()
    small[...] = jnp.zeros_like(small)
    small[0:10, 0:64] = vectors[...].astype(f32)
    small[16:18, :] = bias[...].astype(f32)
    copies = [
        pltpu.make_async_copy(fc1.at[:, pl.ds(pl.multiple_of(y * 1024, 1024), 1024)], piece.at[0:64], sems.at[0]),
        pltpu.make_async_copy(fc2.at[pl.ds(pl.multiple_of(y * GROWS, 16), GROWS)], piece.at[64 : 64 + GROWS], sems.at[1]),
        pltpu.make_async_copy(qkv, unit.at[:, 0:3072], sems.at[2]),
        pltpu.make_async_copy(proj, unit.at[:, 3072:4096], sems.at[3]),
    ]
    for n in range(TAILS):
        row, col = 4 * GROWS + 64 * n, 4096 + 1024 * n
        copies.append(
            pltpu.make_async_copy(fc2.at[row : row + 64], unit.at[:, col : col + 1024], sems.at[4 + n])
        )
    start(copies)
    wait(copies)
    unit[:, UNIT - 128 : UNIT] = small[...].astype(bf16)


def pack(w_qkv, w_proj, w_fc1, w_fc2, vectors, fc1_bias):
    return call(
        pack_kernel,
        [((64, UNIT), bf16), ((64 + GROWS, 1024), bf16)],
        (w_qkv, w_proj, w_fc1, w_fc2, vectors, fc1_bias.reshape(2, 128)),
        [ANY] * 4 + [VM] * 2,
        scratch=[pltpu.VMEM((64, 128), f32), pltpu.SemaphoreType.DMA((4 + TAILS,))],
        moved=4 * 2**20,
        name="pack_parts",
    )


def placed_kernel(*refs):
    pieces, out, sems = refs[:8], refs[8], refs[9]
    x, z, _, _ = place()
    copies = [
        pltpu.make_async_copy(piece, out.at[near(x, n // 2, XS) * 2 + near(z, n % 2, ZS)], sems.at[n])
        for n, piece in enumerate(pieces)
    ]
    start(copies)
    wait(copies)


def placed_pieces(pieces):
    return call(
        placed_kernel,
        [((8, 64 + GROWS, 1024), bf16)],
        pieces,
        [ANY] * 8,
        scratch=[pltpu.SemaphoreType.DMA((8,))],
        moved=4 * 2**20,
        name="placed_pieces",
    )[0]


def vectors_kernel(*refs):
    pieces, vec, bias, held, sems = refs[:16], refs[16], refs[17], refs[18], refs[19]
    x, z, c, _ = place()
    copies = []
    for n, piece in enumerate(pieces):
        k, dx, dz = n // 8, (n // 2) % 4, n % 2
        index = near(x, dx, XS) * 4 + near(z, dz, ZS) * 2 + near(c, k, CS)
        copies.append(pltpu.make_async_copy(piece.at[0:32, UNIT - 128 : UNIT], held.at[index], sems.at[n]))
        copies[-1].start()
    for copy in copies:
        copy.wait()
    lane = lax.broadcasted_iota(jnp.int32, (16, 128), 1)
    for t in range(8):
        a = held[2 * t, 0:16].astype(f32)
        b = held[2 * t + 1, 0:16].astype(f32)
        vec[:, t * 128 : t * 128 + 128] = jnp.where(lane < 64, a, pltpu.roll(b, 64, 1))
    for s in range(16):
        tail = held[s, 16:32].astype(f32)
        bias[0:1, s * 256 : s * 256 + 128] = tail[0:1]
        bias[0:1, s * 256 + 128 : s * 256 + 256] = tail[1:2]


def gathered_vectors(columns):
    flat = [columns[k][dx][dz] for k in range(CS) for dx in range(XS) for dz in range(ZS)]
    return call(
        vectors_kernel,
        [((16, 1024), f32), ((1, FF), f32)],
        flat,
        [ANY] * 16,
        scratch=[pltpu.VMEM((16, 32, 128), bf16), pltpu.SemaphoreType.DMA((16,))],
        moved=2**20,
        name="gathered_vectors",
    )


def column_copies(pieces, target, low, high, sems):
    x, z, c, _ = place()
    out = []
    for n, piece in enumerate(pieces):
        k, dx, dz = n // 8, (n // 2) % 4, n % 2
        xz = near(x, dx, XS) * 2 + near(z, dz, ZS)
        out.append(pltpu.make_async_copy(piece.at[:, low:high], target(xz, near(c, k, CS)), sems.at[n]))
    return out


def attention_weights(pieces, w_qkv, w_proj, sems):
    a = column_copies(pieces, lambda xz, c: w_qkv.at[xz, c], 0, 3072, sems.at[0])
    b = column_copies(pieces, lambda xz, c: w_proj.at[xz, c], 3072, 4096, sems.at[1])
    return a, b


ATTENTION_SCRATCH = [
    pltpu.VMEM((8, 2, 64, 3072), bf16),
    pltpu.VMEM((8, 2, 64, 1024), bf16),
    pltpu.SemaphoreType.DMA((2, 16)),
]


def feed_weights(columns, rows, w1, w2, sems):
    x, z, c, y = place()
    step = 1 - 2 * c
    first, second = [], []
    for n, piece in enumerate(rows):
        k, kind = n // 4, n % 4
        ck = near(c, k, CS)
        yk = near(y + 4, (0, -step, step, 2)[kind], YS)
        first.append(pltpu.make_async_copy(piece.at[:, 0:64], w1.at[yk, :, ck], sems.at[0, n]))
        second.append(
            pltpu.make_async_copy(
                piece.at[:, 64 : 64 + GROWS],
                w2.at[:, ck, pl.ds(pl.multiple_of(yk * GROWS, 16), GROWS)],
                sems.at[1, n],
            )
        )
    for n in range(TAILS):
        row, col = 4 * GROWS + 64 * n, 4096 + 1024 * n
        second += column_copies(
            columns, lambda xz, c, row=row: w2.at[xz, c, row : row + 64], col, col + 1024, sems.at[2 + n]
        )
    return first, second


FEED_SCRATCH = [
    pltpu.VMEM((4, 8, 2, 64, 1024), bf16),
    pltpu.VMEM((8, 2, 256, 1024), bf16),
    pltpu.SemaphoreType.DMA((2 + TAILS, 16)),
]


def start(copies):
    for copy in copies:
        copy.start()


def wait(copies):
    for copy in copies:
        copy.wait()


def stacked_heads(pair, lane):
    zero = jnp.zeros_like(pair)
    return jnp.concatenate([jnp.where(lane, pair, zero), jnp.where(lane, zero, pair)], axis=0)


def attention_forward_kernel(keep, x_ref, vec, *refs):
    pieces, refs = refs[:16], refs[16:]
    if keep:
        a_out, p_out, soft_out, m_out, o_out, x1_out, c_out, w_qkv, w_proj, sems = refs
    else:
        x1_out, c_out, w_qkv, w_proj, sems, p_out, m_out = refs
    first, second = attention_weights(pieces, w_qkv, w_proj, sems)
    start(first)
    start(second)
    x = x_ref[...].astype(f32)
    hat, _ = stats(x)
    a = (hat * vec[0:1, :] + vec[1:2, :]).astype(bf16)
    if keep:
        a_out[...] = a
    wait(first)
    for j in range(6):
        part = dot(a, w_qkv[:, :, :, j * 512 : j * 512 + 512].reshape(D, 512))
        if j < 2:
            part = part + vec[2:3, j * 512 : j * 512 + 512]
        if j >= 4:
            part = part + vec[3:4, j * 512 - 2048 : j * 512 - 1536]
        p_out[:, j * 512 : j * 512 + 512] = part.astype(bf16)
    lane = lax.broadcasted_iota(jnp.int32, (128, 128), 1) < 64

    def unit(u, _):
        i, h = lax.div(u, jnp.int32(8)), lax.rem(u, jnp.int32(8))
        rows = pl.ds(pl.multiple_of(i * 128, 128), 128)
        q, k, v = [p_out[rows, pl.ds(pl.multiple_of(h * 128 + o, 128), 128)] for o in (0, 1024, 2048)]
        s = dot(stacked_heads(q, lane), k, NT) * 0.125
        e = jnp.exp(s - jnp.max(s, axis=-1, keepdims=True))
        soft = e / jnp.sum(e, axis=-1, keepdims=True)
        if keep:
            soft_out[u] = soft
        mixed = dot(soft.astype(bf16), v)
        m_out[rows, pl.ds(pl.multiple_of(h * 128, 128), 128)] = jnp.where(lane, mixed[:128], mixed[128:]).astype(bf16)
        return 0

    lax.fori_loop(0, 16, unit, 0, unroll=4)
    wait(second)
    o = dot(m_out[...], w_proj[...].reshape(D, D)) + vec[4:5, :]
    x1 = x + vec[5:6, :] * o
    if keep:
        o_out[...] = o
    x1_out[...] = x1
    hat, _ = stats(x1)
    c_out[...] = (hat * vec[6:7, :] + vec[7:8, :]).astype(bf16)


def attention_forward(keep, x, vec, columns):
    flat = [columns[k][dx][dz] for k in range(CS) for dx in range(XS) for dz in range(ZS)]
    outs = [((T, D), f32), ((T, D), bf16)]
    scratch = list(ATTENTION_SCRATCH)
    if keep:
        outs = [((T, D), bf16), ((T, 3072), bf16), ((16, 256, 128), f32), ((T, D), bf16), ((T, D), f32)] + outs
    else:
        scratch += [pltpu.VMEM((T, 3072), bf16), pltpu.VMEM((T, D), bf16)]
    return call(
        lambda *refs: attention_forward_kernel(keep, *refs),
        outs,
        [x, vec] + flat,
        [VM, VM] + [ANY] * 16,
        scratch=scratch,
        flops=2 * T * D * 4 * D,
        moved=14 * 2**20,
        name="attention_forward",
    )


def feed_forward_kernel(keep, x1_ref, c_ref, vec, bias, *refs):
    columns, rows, refs = refs[:16], refs[16:24], refs[24:]
    if keep:
        u_out, gp_out, f_out, y_out, w1, w2, sems = refs
    else:
        y_out, w1, w2, sems = refs
    first, second = feed_weights(columns, rows, w1, w2, sems)
    start(first)
    start(second)
    c = c_ref[...]
    total = None
    wait(first)
    for t in range(8):
        y, off = t // 2, (t % 2) * 512
        h = dot(c, w1[y, :, :, :, off : off + 512].reshape(D, 512)) + bias[0:1, t * 512 : t * 512 + 512]
        cdf = 0.5 * (1.0 + lax.erf(h * 0.7071067811865476))
        u = (h * cdf).astype(bf16)
        if keep:
            gp = cdf + h * (jnp.exp(-0.5 * h * h) * 0.3989422804014327)
            u_out[:, t * 512 : t * 512 + 512] = u
            gp_out[:, t * 512 : t * 512 + 512] = gp.astype(bf16)
        if t == 0:
            wait(second)
        part = dot(u, w2[t].reshape(512, D))
        total = part if total is None else total + part
    f = total + vec[8:9, :]
    if keep:
        f_out[...] = f
    y_out[...] = (x1_ref[...] + vec[9:10, :] * f).astype(y_out.dtype)


def feed_forward(keep, x1, c, vec, bias, columns, rows):
    flat = [columns[k][dx][dz] for k in range(CS) for dx in range(XS) for dz in range(ZS)]
    flat += [rows[k][n] for k in range(CS) for n in range(YS)]
    outs = [((T, D), f32 if keep else bf16)]
    if keep:
        outs = [((T, FF), bf16), ((T, FF), bf16), ((T, D), f32)] + outs
    return call(
        lambda *refs: feed_forward_kernel(keep, *refs),
        outs,
        [x1, c, vec, bias] + flat,
        [VM] * 4 + [ANY] * 24,
        scratch=FEED_SCRATCH,
        flops=4 * T * D * FF,
        moved=24 * 2**20,
        name="feed_forward",
    )


def feed_backward_kernel(g_ref, f_ref, gp_ref, x1_ref, o_ref, vec, *refs):
    columns, rows, refs = refs[:16], refs[16:24], refs[24:]
    df_out, dh_out, dx1_out, do_out, small, gbias, w1, w2, sems = refs
    first, second = feed_weights(columns, rows, w1, w2, sems)
    start(second)
    start(first)
    g = g_ref[...]
    df = (vec[9:10, :] * g).astype(bf16)
    df_out[...] = df
    small[8:9, :] = jnp.sum(df.astype(f32), axis=0, keepdims=True)
    small[9:10, :] = jnp.sum(g * f_ref[...], axis=0, keepdims=True)
    small[0:4, :] = jnp.zeros((4, D), f32)
    small[10:16, :] = jnp.zeros((6, D), f32)
    wait(second)
    total = None
    for t in range(8):
        y, off = t // 2, (t % 2) * 512
        cols = slice(t * 512, t * 512 + 512)
        du = dot(df, w2[t].reshape(512, D), NT)
        dh = (gp_ref[:, cols].astype(f32) * du).astype(bf16)
        dh_out[:, cols] = dh
        gbias[0:1, cols] = jnp.sum(dh.astype(f32), axis=0, keepdims=True)
        if t == 0:
            wait(first)
        part = dot(dh, w1[y, :, :, :, off : off + 512].reshape(D, 512), NT)
        total = part if total is None else total + part
    hat, scale = stats(x1_ref[...])
    d_norm, small[6:7, :], small[7:8, :] = norm_back(total, vec[6:7, :], hat, scale)
    dx1 = g + d_norm
    dx1_out[...] = dx1
    small[5:6, :] = jnp.sum(dx1 * o_ref[...], axis=0, keepdims=True)
    do = (vec[5:6, :] * dx1).astype(bf16)
    do_out[...] = do
    small[4:5, :] = jnp.sum(do.astype(f32), axis=0, keepdims=True)


def feed_backward(g, f, gp, x1, o, vec, columns, rows):
    flat = [columns[k][dx][dz] for k in range(CS) for dx in range(XS) for dz in range(ZS)]
    flat += [rows[k][n] for k in range(CS) for n in range(YS)]
    return call(
        feed_backward_kernel,
        [((T, D), bf16), ((T, FF), bf16), ((T, D), f32), ((T, D), bf16), ((16, D), f32), ((1, FF), f32)],
        [g, f, gp, x1, o, vec] + flat,
        [VM] * 6 + [ANY] * 24,
        scratch=FEED_SCRATCH,
        flops=4 * T * D * FF,
        moved=26 * 2**20,
        name="feed_backward",
    )


def attention_backward_kernel(do_ref, dx1_ref, x_ref, p_ref, soft_ref, vec, *refs):
    pieces, refs = refs[:16], refs[16:]
    dp_out, dx_out, small, w_qkv, w_proj, sems, dm_ref = refs
    first, second = attention_weights(pieces, w_qkv, w_proj, sems)
    start(second)
    start(first)
    wait(second)
    dm_ref[...] = dot(do_ref[...], w_proj[...].reshape(D, D), NT).astype(bf16)
    lane = lax.broadcasted_iota(jnp.int32, (128, 128), 1) < 64

    def unit(u, _):
        i, h = lax.div(u, jnp.int32(8)), lax.rem(u, jnp.int32(8))
        rows = pl.ds(pl.multiple_of(i * 128, 128), 128)
        at = lambda o: pl.ds(pl.multiple_of(h * 128 + o, 128), 128)
        q, k, v = [p_ref[rows, at(o)] for o in (0, 1024, 2048)]
        dm = stacked_heads(dm_ref[rows, at(0)], lane)
        soft = soft_ref[u]
        dp_out[rows, at(2048)] = dot(soft.astype(bf16), dm, TN).astype(bf16)
        dw = dot(dm, v, NT)
        ds = (soft * (dw - jnp.sum(soft * dw, axis=-1, keepdims=True))).astype(bf16)
        dq = dot(ds, k) * 0.125
        dp_out[rows, at(0)] = jnp.where(lane, dq[:128], dq[128:]).astype(bf16)
        dp_out[rows, at(1024)] = (dot(ds, stacked_heads(q, lane), TN) * 0.125).astype(bf16)
        return 0

    lax.fori_loop(0, 16, unit, 0, unroll=4)
    small[2:3, :] = jnp.sum(dp_out[:, 0:1024].astype(f32), axis=0, keepdims=True)
    small[3:4, :] = jnp.sum(dp_out[:, 2048:3072].astype(f32), axis=0, keepdims=True)
    small[4:16, :] = jnp.zeros((12, D), f32)
    wait(first)
    total = None
    for j in range(6):
        cols = slice(j * 512, j * 512 + 512)
        part = dot(dp_out[:, cols], w_qkv[:, :, :, cols].reshape(D, 512), NT)
        total = part if total is None else total + part
    hat, scale = stats(x_ref[...].astype(f32))
    d_norm, small[0:1, :], small[1:2, :] = norm_back(total, vec[0:1, :], hat, scale)
    dx_out[...] = dx1_ref[...] + d_norm


def attention_backward(do, dx1, x, p, soft, vec, columns):
    flat = [columns[k][dx][dz] for k in range(CS) for dx in range(XS) for dz in range(ZS)]
    return call(
        attention_backward_kernel,
        [((T, 3072), bf16), ((T, D), f32), ((16, D), f32)],
        [do, dx1, x, p, soft, vec] + flat,
        [VM] * 6 + [ANY] * 16,
        scratch=list(ATTENTION_SCRATCH) + [pltpu.VMEM((T, D), bf16)],
        flops=2 * T * D * 4 * D,
        moved=18 * 2**20,
        name="attention_backward",
    )


def picked_kernel(a_ref, m_ref, c_ref, u_ref, mine, theirs):
    x, z, c, _ = place()
    row = lax.broadcasted_iota(jnp.int32, (512, D), 0)
    col = lax.broadcasted_iota(jnp.int32, (512, D), 1)
    eye_r = lax.broadcasted_iota(jnp.int32, (256, 256), 0)
    eye = jnp.where(eye_r == lax.broadcasted_iota(jnp.int32, (256, 256), 1), 1.0, 0.0).astype(bf16)
    dx, dz, inner = row >> 7, (row >> 6) & 1, row & 63
    base = (((x + dx) & 3) << 8) + (((z + dz) & 1) << 7) + inner
    for k, out in enumerate((mine, theirs)):
        ck = near(c, k, CS)
        chosen = jnp.where(col == base + ck * 64, 1.0, 0.0).astype(bf16)
        for n, ref in enumerate((a_ref, m_ref, c_ref)):
            out[n * 512 : n * 512 + 512, :] = dot(chosen, ref[...], NT).astype(bf16)
        for j in range(8):
            s = near(x, j // 2, XS) * 4 + near(z, j % 2, ZS) * 2 + ck
            block = u_ref[:, pl.ds(pl.multiple_of(s * 256, 256), 256)]
            out[1536 + j * 256 : 1792 + j * 256, :] = dot(eye, block, NT).astype(bf16)


def picked(a, m, c, u):
    return call(
        picked_kernel,
        [((3584, T), bf16)] * 2,
        [a, m, c, u],
        [VM] * 4,
        flops=2 * 10**9,
        moved=8 * 2**20,
        name="transposed_acts",
    )


def feed_grads_kernel(mine, theirs, dh, dh2, df, df2, *refs):
    outs, acts, dh_all, df_all, rows, sems, out_sems = refs[:4], *refs[4:]
    _, _, c, y = place()
    step = 1 - 2 * c
    copies = [
        pltpu.make_async_copy(mine.at[1024:3584], acts.at[:, 0:256], sems.at[0]),
        pltpu.make_async_copy(theirs.at[1024:3584], acts.at[:, 256:512], sems.at[1]),
        pltpu.make_async_copy(df, df_all.at[0:256], sems.at[2]),
        pltpu.make_async_copy(df2, df_all.at[256:512], sems.at[3]),
        pltpu.make_async_copy(dh, dh_all.at[0:256], sems.at[4]),
        pltpu.make_async_copy(dh2, dh_all.at[256:512], sems.at[5]),
    ]
    start(copies)
    wait(copies[:4])
    kinds = [near(y + 4, dy, YS) for dy in (2, -step, step, 0)]
    for j in range(8):
        grad = dot(acts[512 + j * 256 : 768 + j * 256, :], df_all[...]).astype(bf16)
        rows[:, j, 64:128] = grad.reshape(YS, 64, 1024)
    wait(copies[4:])
    sends = []
    for n, yk in enumerate(kinds):
        cols = pl.ds(pl.multiple_of(yk * 1024, 1024), 1024)
        for half in range(2):
            grad = dot(acts[half * 256 : half * 256 + 256, :], dh_all[:, cols]).astype(bf16)
            rows[yk, 4 * half : 4 * half + 4, 0:64] = grad.reshape(4, 64, 1024)
        sends.append(pltpu.make_async_copy(rows.at[yk], outs[n], out_sems.at[n]))
        sends[-1].start()
    wait(sends)


def feed_grads(mine, theirs, dh, dh2, df, df2):
    return call(
        feed_grads_kernel,
        [((8, 128, 1024), bf16)] * 4,
        [mine, theirs, dh, dh2, df, df2],
        [ANY] * 6,
        scratch=[
            pltpu.VMEM((2560, 512), bf16),
            pltpu.VMEM((512, FF), bf16),
            pltpu.VMEM((512, D), bf16),
            pltpu.VMEM((4, 8, 128, 1024), bf16),
            pltpu.SemaphoreType.DMA((6,)),
            pltpu.SemaphoreType.DMA((4,)),
        ],
        out_kinds=[ANY] * 4,
        flops=8 * T * D * FF,
        moved=24 * 2**20,
        name="feed_grads",
    )


def attention_grads_kernel(mine, theirs, dp, dp2, do, do2, s1, s2, s3, s4, b1, b2, *refs):
    outs, acts, dp_all, do_all, held, sems, out_sems = refs[:4], *refs[4:]
    x, z, c, _ = place()
    copies = [
        pltpu.make_async_copy(mine.at[0:1024], acts.at[:, 0:256], sems.at[0]),
        pltpu.make_async_copy(theirs.at[0:1024], acts.at[:, 256:512], sems.at[1]),
        pltpu.make_async_copy(do, do_all.at[0:256], sems.at[2]),
        pltpu.make_async_copy(do2, do_all.at[256:512], sems.at[3]),
        pltpu.make_async_copy(dp, dp_all.at[0:256], sems.at[4]),
        pltpu.make_async_copy(dp2, dp_all.at[256:512], sems.at[5]),
    ]
    start(copies)
    vec = (s1[...] + s2[...] + s3[...] + s4[...]).astype(bf16)
    row = lax.broadcasted_iota(jnp.int32, (D, 128), 0)
    col = lax.broadcasted_iota(jnp.int32, (D, 128), 1)
    for j in range(8):
        s = near(x, j // 2, XS) * 4 + near(z, j % 2, ZS) * 2 + c
        chosen = jnp.where((row == col + s * 64) & (col < 64), 1.0, 0.0).astype(bf16)
        held[j, :, 4096:4224] = jnp.zeros((64, 128), bf16)
        held[j, 0:16, 4096:4224] = dot(vec, chosen).astype(bf16)
        a = b1[0:1, pl.ds(pl.multiple_of(s * 256, 256), 128)] + b2[0:1, pl.ds(pl.multiple_of(s * 256, 256), 128)]
        b = b1[0:1, pl.ds(pl.multiple_of(s * 256 + 128, 128), 128)] + b2[0:1, pl.ds(pl.multiple_of(s * 256 + 128, 128), 128)]
        line = lax.broadcasted_iota(jnp.int32, (16, 128), 0)
        held[j, 16:32, 4096:4224] = jnp.where(line == 0, a, jnp.where(line == 1, b, 0.0)).astype(bf16)
    wait(copies[:4])
    for n in range(2):
        grad = dot(acts[512:1024, :], do_all[:, n * 512 : n * 512 + 512]).astype(bf16)
        held[:, :, 3072 + n * 512 : 3584 + n * 512] = grad.reshape(8, 64, 512)
    wait(copies[4:])
    for n in range(6):
        grad = dot(acts[0:512, :], dp_all[:, n * 512 : n * 512 + 512]).astype(bf16)
        held[:, :, n * 512 : n * 512 + 512] = grad.reshape(8, 64, 512)
    step = 1 - 2 * c
    kinds = [near(jnp.int32(4), dx, XS) for dx in (2, -step, step, 0)]
    sends = [pltpu.make_async_copy(held.at[pl.ds(2 * dx, 2)], outs[n], out_sems.at[n]) for n, dx in enumerate(kinds)]
    start(sends)
    wait(sends)


def attention_grads(mine, theirs, dp, dp2, do, do2, smalls, biases):
    return call(
        attention_grads_kernel,
        [((2, 64, QP), bf16)] * 4,
        [mine, theirs, dp, dp2, do, do2] + smalls + biases,
        [ANY] * 6 + [VM] * 6,
        scratch=[
            pltpu.VMEM((1024, 512), bf16),
            pltpu.VMEM((512, 3072), bf16),
            pltpu.VMEM((512, D), bf16),
            pltpu.VMEM((8, 64, QP), bf16),
            pltpu.SemaphoreType.DMA((6,)),
            pltpu.SemaphoreType.DMA((4,)),
        ],
        out_kinds=[ANY] * 4,
        flops=8 * T * D * 2 * D,
        moved=16 * 2**20,
        name="attention_grads",
    )


def sum_kernel(count, *refs):
    total = refs[0][...].astype(f32)
    for ref in refs[1:count]:
        total = total + ref[...].astype(f32)
    outs = refs[count:]
    if len(outs) == 1:
        outs[0][...] = total.astype(bf16)
    else:
        for n, out in enumerate(outs):
            out[...] = total[n].astype(bf16)


def summed(parts, split=False):
    shape = parts[0].shape
    outs = [(shape[1:], bf16)] * shape[0] if split else [(shape, bf16)]
    size = 1
    for n in shape:
        size *= n
    out = call(
        lambda *refs: sum_kernel(len(parts), *refs),
        outs,
        parts,
        [VM] * len(parts),
        flops=size * len(parts),
        moved=2 * size * (len(parts) + 1),
        name="summed",
    )
    return out if split else out[0]


def scattered(parts, axis):
    opposite, behind, ahead, here = parts
    far = onward(opposite, axis)
    given = onward(from_shard(behind, dc=1), axis)
    own = onward(summed([ahead, far]), axis)
    return [here, own, from_shard(given, dc=1)]


def scatter_columns(parts):
    same, other = summed(scattered(parts, "x"), split=True)
    return summed([same, from_shard(other, dz=1)])


def scatter_rows(parts):
    places = summed(scattered(parts, "y"), split=True)
    got = [
        from_shard(places[2 * dx + dz], dx=XS - dx, dz=dz)
        for dx in range(XS)
        for dz in range(ZS)
        if (dx, dz) != (0, 0)
    ]
    return summed([places[0]] + got)


def own_quarter(part, y):
    quarters = part.reshape(YS, 16, -1)
    at = lambda dy: lax.dynamic_index_in_dim(quarters, lax.rem(y + dy, YS), 0, keepdims=False)
    return summed([at(0)] + [from_replica(at(dy), YS - dy) for dy in range(1, YS)])


def results_kernel(*refs):
    rows, columns = refs[0:4], refs[4:8]
    g_qkv, g_proj, g_fc1, g_fc2, g_vec, g_bias, rows_all, cols_all, sems = refs[8:]
    _, _, _, y = place()
    copies = []
    for dy in range(YS):
        yk = near(y, dy, YS)
        copies.append(pltpu.make_async_copy(rows[dy], rows_all.at[yk], sems.at[0, dy]))
        copies.append(pltpu.make_async_copy(columns[dy], cols_all.at[yk], sems.at[1, dy]))
    start(copies)
    wait(copies)
    for k in range(YS):
        g_fc1[:, k * 1024 : k * 1024 + 1024] = rows_all[k, 0:64].astype(f32)
        g_fc2[k * 64 : k * 64 + 64, :] = rows_all[k, 64:128].astype(f32)
        line = slice(k * 16, k * 16 + 16)
        g_qkv[line, :] = cols_all[k, :, 0:3072].astype(f32)
        g_proj[line, :] = cols_all[k, :, 3072:4096].astype(f32)
    g_vec[...] = cols_all[0, :, 4096:4224].astype(f32)
    g_bias[...] = cols_all[1, :, 4096:4224].astype(f32)


def results(rows, columns):
    return call(
        results_kernel,
        [((64, 3072), f32), ((64, 1024), f32), ((64, FF), f32), ((256, D), f32), ((16, 128), f32), ((16, 128), f32)],
        list(rows) + list(columns),
        [ANY] * 8,
        scratch=[
            pltpu.VMEM((4, 128, 1024), bf16),
            pltpu.VMEM((4, 16, QP), bf16),
            pltpu.SemaphoreType.DMA((2, 4)),
        ],
        moved=10 * 2**20,
        name="results",
    )


def gather(w_qkv, w_proj, w_fc1, w_fc2, vectors, fc1_bias):
    twin = lambda v: from_shard(v, dc=1)
    unit, piece = pack(w_qkv, w_proj, w_fc1, w_fc2, vectors, fc1_bias)
    pieces = [
        piece if (dx, dz) == (0, 0) else from_shard(piece, dx=dx, dz=dz) for dx in range(XS) for dz in range(ZS)
    ]
    here = placed_pieces(pieces)
    unit, here = lax.optimization_barrier((unit, here))
    twin_here = twin(here)
    behind = onward(here, "y")
    twin_behind = onward(twin_here, "y")
    opposite = onward(behind, "y")
    rows = [
        [here, behind, twin(twin_behind), opposite],
        [twin_here, twin_behind, twin(behind), twin(opposite)],
    ]
    other = from_shard(unit, dz=1)
    plus = [from_shard(unit, dx=1), from_shard(other, dx=1)]
    minus = [from_shard(unit, dx=3), from_shard(other, dx=3)]
    far = [from_shard(plus[0], dx=1), from_shard(minus[1], dx=3)]
    mine = [[unit, other], plus, far, minus]
    columns = [mine, [[twin(v) for v in pair] for pair in mine]]
    return columns, rows


def shards(edge_inputs, image_counts, w_qkv, w_proj, w_fc1, w_fc2, vectors, fc1_bias):
    section = lax.axis_index("section")
    _, _, _, y = place()
    source = edge_inputs[0, :, 0]
    present = (lax.axis_index("shard") * YS + y < image_counts).astype(f32)
    columns, rows = gather(w_qkv[0], w_proj[0], w_fc1[0], w_fc2[0], vectors[0], fc1_bias[0])
    vec, bias = gathered_vectors(columns)

    own = source.reshape(T, D)
    x1, c = attention_forward(False, own, vec, columns)
    (first_out,) = feed_forward(False, x1, c, vec, bias, columns, rows)
    received = passed_along(first_out, 1)
    inputs = jnp.where(section == 0, own, received)
    a, p, soft, m, o, x1, c = attention_forward(True, inputs, vec, columns)
    u, gp, f, output = feed_forward(True, x1, c, vec, bias, columns, rows)

    cotangent = (source.astype(f32) * present[:, None, None]).reshape(T, D)
    _, _, dx1, do, _, _ = feed_backward(cotangent, f, gp, x1, o, vec, columns, rows)
    _, dx, _ = attention_backward(do, dx1, inputs, p, soft, vec, columns)
    received_grad = passed_along(dx.astype(bf16), -1)
    mine, theirs = picked(a, m, c, u)
    theirs = from_shard(theirs, dc=1)
    upstream = jnp.where(section == 1, cotangent, received_grad.astype(f32))
    df, dh, dx1, do, small_a, gbias = feed_backward(upstream, f, gp, x1, o, vec, columns, rows)
    dp, dx, small_b = attention_backward(do, dx1, inputs, p, soft, vec, columns)
    twin = lambda v: from_shard(v, dc=1)
    row = scatter_rows(feed_grads(mine, theirs, dh, twin(dh), df, twin(df)))
    column_parts = attention_grads(
        mine, theirs, dp, twin(dp), do, twin(do), [small_a, twin(small_a), small_b, twin(small_b)], [gbias, twin(gbias)]
    )
    column = own_quarter(scatter_columns(column_parts), y)
    around = lambda v: [v] + [from_replica(v, dy) for dy in range(1, YS)]
    g_qkv, g_proj, g_fc1, g_fc2, g_vec, g_bias = results(around(row), around(column))
    edge_values = jnp.where(section == 0, dx, output).reshape(1, 2, 1, 128, D)
    return (
        edge_values,
        g_qkv[None],
        g_proj[None],
        g_fc1[None],
        g_fc2[None],
        g_vec[None, :10, :64],
        g_bias[:2].reshape(1, 256),
    )


def solution(mesh):
    placed = (
        P("section", None, ("shard", "replica"), None, None),
        P(),
        P("section", "shard", None),
        P("section", "shard", None),
        P("section", "shard", None),
        P("section", "shard", None),
        P("section", None, "shard"),
        P("section", "shard"),
    )
    return jax.shard_map(
        shards,
        mesh=mesh,
        in_specs=placed,
        out_specs=(placed[0],) + placed[2:],
        check_vma=False,
    )
```

```python
import jax
import jax.numpy as jnp
from jax import lax
from jax.experimental import pallas as pl
from jax.experimental.pallas import tpu as pltpu
from jax.sharding import PartitionSpec as P

XS, ZS, CS, YS = 4, 2, 2, 4
T = 256
D, FF = 1024, 4096
GROWS = 48
TAILS = 4 - GROWS // 16
UNIT = 4096 + 1024 * TAILS + 128
QP = 4224
epsilon = 1e-06
bf16, f32 = jnp.bfloat16, jnp.float32
ANY = pl.BlockSpec(memory_space=pl.ANY)
VM = pl.BlockSpec(memory_space=pltpu.VMEM)
NT = (((1,), (1,)), ((), ()))
TN = (((0,), (0,)), ((), ()))


def shard_of(x, z, c):
    return (x % XS) * 4 + (z % ZS) * 2 + (c % CS)


def from_shard(value, dx=0, dz=0, dc=0):
    pairs = [
        (shard_of(x + dx, z + dz, c + dc), shard_of(x, z, c))
        for x in range(XS)
        for z in range(ZS)
        for c in range(CS)
    ]
    return lax.ppermute(value, "shard", pairs)


def from_replica(value, dy):
    return lax.ppermute(value, "replica", [((y + dy) % YS, y) for y in range(YS)])


def onward(value, axis):
    pairs = []
    for x in range(XS):
        for z in range(ZS):
            for c in range(CS):
                for y in range(YS):
                    step = 1 - 2 * c
                    tx, ty = (x + step, y) if axis == "x" else (x, y + step)
                    pairs.append((shard_of(x, z, c) * YS + y, shard_of(tx, z, c) * YS + ty % YS))
    return lax.ppermute(value, ("shard", "replica"), pairs)


def passed_along(value, steps):
    return lax.ppermute(value, "section", [(0, 1)] if steps == 1 else [(1, 0)])


def place():
    shard = lax.axis_index("shard")
    x = lax.div(shard, jnp.int32(4))
    z = lax.rem(lax.div(shard, jnp.int32(2)), jnp.int32(2))
    c = lax.rem(shard, jnp.int32(2))
    return x, z, c, lax.axis_index("replica")


def near(base, step, size):
    return lax.rem(base + jnp.int32(step), jnp.int32(size))


def call(kernel, outs, args, kinds, scratch=(), flops=0, moved=0, out_kinds=None, name=None):
    return pl.pallas_call(
        kernel,
        out_shape=[jax.ShapeDtypeStruct(s, d) for s, d in outs],
        in_specs=list(kinds),
        out_specs=list(out_kinds or [VM] * len(outs)),
        scratch_shapes=list(scratch),
        compiler_params=pltpu.CompilerParams(vmem_limit_bytes=56 * 2**20),
        cost_estimate=pl.CostEstimate(flops=flops, bytes_accessed=moved, transcendentals=0),
        name=name,
    )(*args)


def dot(a, b, dims=(((1,), (0,)), ((), ()))):
    return lax.dot_general(a, b, dims, preferred_element_type=f32)


def stats(values):
    average = jnp.mean(values, axis=-1, keepdims=True)
    centered = values - average
    spread = jnp.mean(centered * centered, axis=-1, keepdims=True)
    scale = lax.rsqrt(spread + epsilon)
    return centered * scale, scale


def norm_back(grad, gain, hat, scale):
    d_hat = grad * gain
    d_in = scale * (
        d_hat - jnp.mean(d_hat, axis=-1, keepdims=True) - hat * jnp.mean(d_hat * hat, axis=-1, keepdims=True)
    )
    return d_in, jnp.sum(grad * hat, axis=0, keepdims=True), jnp.sum(grad, axis=0, keepdims=True)


def pack_kernel(qkv, proj, fc1, fc2, vectors, bias, unit, piece, small, sems):
    _, _, _, y = place()
    small[...] = jnp.zeros_like(small)
    small[0:10, 0:64] = vectors[...].astype(f32)
    small[16:18, :] = bias[...].astype(f32)
    copies = [
        pltpu.make_async_copy(fc1.at[:, pl.ds(pl.multiple_of(y * 1024, 1024), 1024)], piece.at[0:64], sems.at[0]),
        pltpu.make_async_copy(fc2.at[pl.ds(pl.multiple_of(y * GROWS, 16), GROWS)], piece.at[64 : 64 + GROWS], sems.at[1]),
        pltpu.make_async_copy(qkv, unit.at[:, 0:3072], sems.at[2]),
        pltpu.make_async_copy(proj, unit.at[:, 3072:4096], sems.at[3]),
    ]
    for n in range(TAILS):
        row, col = 4 * GROWS + 64 * n, 4096 + 1024 * n
        copies.append(
            pltpu.make_async_copy(fc2.at[row : row + 64], unit.at[:, col : col + 1024], sems.at[4 + n])
        )
    start(copies)
    wait(copies)
    unit[:, UNIT - 128 : UNIT] = small[...].astype(bf16)


def pack(w_qkv, w_proj, w_fc1, w_fc2, vectors, fc1_bias):
    return call(
        pack_kernel,
        [((64, UNIT), bf16), ((64 + GROWS, 1024), bf16)],
        (w_qkv, w_proj, w_fc1, w_fc2, vectors, fc1_bias.reshape(2, 128)),
        [ANY] * 4 + [VM] * 2,
        scratch=[pltpu.VMEM((64, 128), f32), pltpu.SemaphoreType.DMA((4 + TAILS,))],
        moved=4 * 2**20,
        name="pack_parts",
    )


def placed_kernel(*refs):
    pieces, out, sems = refs[:8], refs[8], refs[9]
    x, z, _, _ = place()
    copies = [
        pltpu.make_async_copy(piece, out.at[near(x, n // 2, XS) * 2 + near(z, n % 2, ZS)], sems.at[n])
        for n, piece in enumerate(pieces)
    ]
    start(copies)
    wait(copies)


def placed_pieces(pieces):
    return call(
        placed_kernel,
        [((8, 64 + GROWS, 1024), bf16)],
        pieces,
        [ANY] * 8,
        scratch=[pltpu.SemaphoreType.DMA((8,))],
        moved=4 * 2**20,
        name="placed_pieces",
    )[0]


def vectors_kernel(*refs):
    pieces, vec, bias, held, sems = refs[:16], refs[16], refs[17], refs[18], refs[19]
    x, z, c, _ = place()
    copies = []
    for n, piece in enumerate(pieces):
        k, dx, dz = n // 8, (n // 2) % 4, n % 2
        index = near(x, dx, XS) * 4 + near(z, dz, ZS) * 2 + near(c, k, CS)
        copies.append(pltpu.make_async_copy(piece.at[0:32, UNIT - 128 : UNIT], held.at[index], sems.at[n]))
        copies[-1].start()
    for copy in copies:
        copy.wait()
    lane = lax.broadcasted_iota(jnp.int32, (16, 128), 1)
    for t in range(8):
        a = held[2 * t, 0:16].astype(f32)
        b = held[2 * t + 1, 0:16].astype(f32)
        vec[:, t * 128 : t * 128 + 128] = jnp.where(lane < 64, a, pltpu.roll(b, 64, 1))
    for s in range(16):
        tail = held[s, 16:32].astype(f32)
        bias[0:1, s * 256 : s * 256 + 128] = tail[0:1]
        bias[0:1, s * 256 + 128 : s * 256 + 256] = tail[1:2]


def gathered_vectors(columns):
    flat = [columns[k][dx][dz] for k in range(CS) for dx in range(XS) for dz in range(ZS)]
    return call(
        vectors_kernel,
        [((16, 1024), f32), ((1, FF), f32)],
        flat,
        [ANY] * 16,
        scratch=[pltpu.VMEM((16, 32, 128), bf16), pltpu.SemaphoreType.DMA((16,))],
        moved=2**20,
        name="gathered_vectors",
    )


def column_copies(pieces, target, low, high, sems):
    x, z, c, _ = place()
    out = []
    for n, piece in enumerate(pieces):
        k, dx, dz = n // 8, (n // 2) % 4, n % 2
        xz = near(x, dx, XS) * 2 + near(z, dz, ZS)
        out.append(pltpu.make_async_copy(piece.at[:, low:high], target(xz, near(c, k, CS)), sems.at[n]))
    return out


def attention_weights(pieces, w_qkv, w_proj, sems):
    a = column_copies(pieces, lambda xz, c: w_qkv.at[xz, c], 0, 3072, sems.at[0])
    b = column_copies(pieces, lambda xz, c: w_proj.at[xz, c], 3072, 4096, sems.at[1])
    return a, b


ATTENTION_SCRATCH = [
    pltpu.VMEM((8, 2, 64, 3072), bf16),
    pltpu.VMEM((8, 2, 64, 1024), bf16),
    pltpu.SemaphoreType.DMA((2, 16)),
]


def feed_weights(columns, rows, w1, w2, sems):
    x, z, c, y = place()
    step = 1 - 2 * c
    first, second = [], []
    for n, piece in enumerate(rows):
        k, kind = n // 4, n % 4
        ck = near(c, k, CS)
        yk = near(y + 4, (0, -step, step, 2)[kind], YS)
        first.append(pltpu.make_async_copy(piece.at[:, 0:64], w1.at[yk, :, ck], sems.at[0, n]))
        second.append(
            pltpu.make_async_copy(
                piece.at[:, 64 : 64 + GROWS],
                w2.at[:, ck, pl.ds(pl.multiple_of(yk * GROWS, 16), GROWS)],
                sems.at[1, n],
            )
        )
    for n in range(TAILS):
        row, col = 4 * GROWS + 64 * n, 4096 + 1024 * n
        second += column_copies(
            columns, lambda xz, c, row=row: w2.at[xz, c, row : row + 64], col, col + 1024, sems.at[2 + n]
        )
    return first, second


FEED_SCRATCH = [
    pltpu.VMEM((4, 8, 2, 64, 1024), bf16),
    pltpu.VMEM((8, 2, 256, 1024), bf16),
    pltpu.SemaphoreType.DMA((2 + TAILS, 16)),
]


def start(copies):
    for copy in copies:
        copy.start()


def wait(copies):
    for copy in copies:
        copy.wait()


def stacked_heads(pair, lane):
    zero = jnp.zeros_like(pair)
    return jnp.concatenate([jnp.where(lane, pair, zero), jnp.where(lane, zero, pair)], axis=0)


def attention_forward_kernel(keep, x_ref, vec, *refs):
    pieces, refs = refs[:16], refs[16:]
    if keep:
        a_out, p_out, soft_out, m_out, o_out, x1_out, c_out, w_qkv, w_proj, sems = refs
    else:
        x1_out, c_out, w_qkv, w_proj, sems, p_out, m_out = refs
    first, second = attention_weights(pieces, w_qkv, w_proj, sems)
    start(first)
    start(second)
    x = x_ref[...].astype(f32)
    hat, _ = stats(x)
    a = (hat * vec[0:1, :] + vec[1:2, :]).astype(bf16)
    if keep:
        a_out[...] = a
    wait(first)
    for j in range(6):
        part = dot(a, w_qkv[:, :, :, j * 512 : j * 512 + 512].reshape(D, 512))
        if j < 2:
            part = part + vec[2:3, j * 512 : j * 512 + 512]
        if j >= 4:
            part = part + vec[3:4, j * 512 - 2048 : j * 512 - 1536]
        p_out[:, j * 512 : j * 512 + 512] = part.astype(bf16)
    lane = lax.broadcasted_iota(jnp.int32, (128, 128), 1) < 64

    def unit(u, _):
        i, h = lax.div(u, jnp.int32(8)), lax.rem(u, jnp.int32(8))
        rows = pl.ds(pl.multiple_of(i * 128, 128), 128)
        q, k, v = [p_out[rows, pl.ds(pl.multiple_of(h * 128 + o, 128), 128)] for o in (0, 1024, 2048)]
        s = dot(stacked_heads(q, lane), k, NT) * 0.125
        e = jnp.exp(s - jnp.max(s, axis=-1, keepdims=True))
        soft = e / jnp.sum(e, axis=-1, keepdims=True)
        if keep:
            soft_out[u] = soft
        mixed = dot(soft.astype(bf16), v)
        m_out[rows, pl.ds(pl.multiple_of(h * 128, 128), 128)] = jnp.where(lane, mixed[:128], mixed[128:]).astype(bf16)
        return 0

    lax.fori_loop(0, 16, unit, 0, unroll=4)
    wait(second)
    o = dot(m_out[...], w_proj[...].reshape(D, D)) + vec[4:5, :]
    x1 = x + vec[5:6, :] * o
    if keep:
        o_out[...] = o
    x1_out[...] = x1
    hat, _ = stats(x1)
    c_out[...] = (hat * vec[6:7, :] + vec[7:8, :]).astype(bf16)


def attention_forward(keep, x, vec, columns):
    flat = [columns[k][dx][dz] for k in range(CS) for dx in range(XS) for dz in range(ZS)]
    outs = [((T, D), f32), ((T, D), bf16)]
    scratch = list(ATTENTION_SCRATCH)
    if keep:
        outs = [((T, D), bf16), ((T, 3072), bf16), ((16, 256, 128), f32), ((T, D), bf16), ((T, D), f32)] + outs
    else:
        scratch += [pltpu.VMEM((T, 3072), bf16), pltpu.VMEM((T, D), bf16)]
    return call(
        lambda *refs: attention_forward_kernel(keep, *refs),
        outs,
        [x, vec] + flat,
        [VM, VM] + [ANY] * 16,
        scratch=scratch,
        flops=2 * T * D * 4 * D,
        moved=14 * 2**20,
        name="attention_forward",
    )


def feed_forward_kernel(keep, x1_ref, c_ref, vec, bias, *refs):
    columns, rows, refs = refs[:16], refs[16:24], refs[24:]
    if keep:
        u_out, gp_out, f_out, y_out, w1, w2, sems = refs
    else:
        y_out, w1, w2, sems = refs
    first, second = feed_weights(columns, rows, w1, w2, sems)
    start(first)
    start(second)
    c = c_ref[...]
    total = None
    wait(first)
    for t in range(8):
        y, off = t // 2, (t % 2) * 512
        h = dot(c, w1[y, :, :, :, off : off + 512].reshape(D, 512)) + bias[0:1, t * 512 : t * 512 + 512]
        cdf = 0.5 * (1.0 + lax.erf(h * 0.7071067811865476))
        u = (h * cdf).astype(bf16)
        if keep:
            gp = cdf + h * (jnp.exp(-0.5 * h * h) * 0.3989422804014327)
            u_out[:, t * 512 : t * 512 + 512] = u
            gp_out[:, t * 512 : t * 512 + 512] = gp.astype(bf16)
        if t == 0:
            wait(second)
        part = dot(u, w2[t].reshape(512, D))
        total = part if total is None else total + part
    f = total + vec[8:9, :]
    if keep:
        f_out[...] = f
    y_out[...] = (x1_ref[...] + vec[9:10, :] * f).astype(y_out.dtype)


def feed_forward(keep, x1, c, vec, bias, columns, rows):
    flat = [columns[k][dx][dz] for k in range(CS) for dx in range(XS) for dz in range(ZS)]
    flat += [rows[k][n] for k in range(CS) for n in range(YS)]
    outs = [((T, D), f32 if keep else bf16)]
    if keep:
        outs = [((T, FF), bf16), ((T, FF), bf16), ((T, D), f32)] + outs
    return call(
        lambda *refs: feed_forward_kernel(keep, *refs),
        outs,
        [x1, c, vec, bias] + flat,
        [VM] * 4 + [ANY] * 24,
        scratch=FEED_SCRATCH,
        flops=4 * T * D * FF,
        moved=24 * 2**20,
        name="feed_forward",
    )


def feed_backward_kernel(g_ref, df_ref, f_ref, gp_ref, x1_ref, o_ref, vec, *refs):
    columns, rows, refs = refs[:16], refs[16:24], refs[24:]
    dh_out, dx1_out, do_out, small, w1, w2, sems = refs
    first, second = feed_weights(columns, rows, w1, w2, sems)
    start(second)
    start(first)
    g = g_ref[...]
    df = df_ref[...]
    small[8:9, :] = jnp.sum(df.astype(f32), axis=0, keepdims=True)
    small[9:10, :] = jnp.sum(g * f_ref[...], axis=0, keepdims=True)
    small[0:4, :] = jnp.zeros((4, D), f32)
    small[14:16, :] = jnp.zeros((2, D), f32)
    wait(second)
    total = None
    for t in range(8):
        y, off = t // 2, (t % 2) * 512
        cols = slice(t * 512, t * 512 + 512)
        du = dot(df, w2[t].reshape(512, D), NT)
        dh = (gp_ref[:, cols].astype(f32) * du).astype(bf16)
        dh_out[:, cols] = dh
        small[10 + y : 11 + y, off : off + 512] = jnp.sum(dh.astype(f32), axis=0, keepdims=True)
        if t == 0:
            wait(first)
        part = dot(dh, w1[y, :, :, :, off : off + 512].reshape(D, 512), NT)
        total = part if total is None else total + part
    hat, scale = stats(x1_ref[...])
    d_norm, small[6:7, :], small[7:8, :] = norm_back(total, vec[6:7, :], hat, scale)
    dx1 = g + d_norm
    dx1_out[...] = dx1
    small[5:6, :] = jnp.sum(dx1 * o_ref[...], axis=0, keepdims=True)
    do = (vec[5:6, :] * dx1).astype(bf16)
    do_out[...] = do
    small[4:5, :] = jnp.sum(do.astype(f32), axis=0, keepdims=True)


def feed_backward(g, df, f, gp, x1, o, vec, columns, rows):
    flat = [columns[k][dx][dz] for k in range(CS) for dx in range(XS) for dz in range(ZS)]
    flat += [rows[k][n] for k in range(CS) for n in range(YS)]
    return call(
        feed_backward_kernel,
        [((T, FF), bf16), ((T, D), f32), ((T, D), bf16), ((16, D), f32)],
        [g, df, f, gp, x1, o, vec] + flat,
        [VM] * 7 + [ANY] * 24,
        scratch=FEED_SCRATCH,
        flops=4 * T * D * FF,
        moved=26 * 2**20,
        name="feed_backward",
    )


def attention_backward_kernel(do_ref, dx1_ref, x_ref, p_ref, soft_ref, small_ref, vec, *refs):
    pieces, refs = refs[:16], refs[16:]
    dp_out, dx_out, small, w_qkv, w_proj, sems, dm_ref = refs
    first, second = attention_weights(pieces, w_qkv, w_proj, sems)
    start(second)
    start(first)
    wait(second)
    dm_ref[...] = dot(do_ref[...], w_proj[...].reshape(D, D), NT).astype(bf16)
    lane = lax.broadcasted_iota(jnp.int32, (128, 128), 1) < 64

    def unit(u, _):
        i, h = lax.div(u, jnp.int32(8)), lax.rem(u, jnp.int32(8))
        rows = pl.ds(pl.multiple_of(i * 128, 128), 128)
        at = lambda o: pl.ds(pl.multiple_of(h * 128 + o, 128), 128)
        q, k, v = [p_ref[rows, at(o)] for o in (0, 1024, 2048)]
        dm = stacked_heads(dm_ref[rows, at(0)], lane)
        soft = soft_ref[u]
        dp_out[rows, at(2048)] = dot(soft.astype(bf16), dm, TN).astype(bf16)
        dw = dot(dm, v, NT)
        ds = (soft * (dw - jnp.sum(soft * dw, axis=-1, keepdims=True))).astype(bf16)
        dq = dot(ds, k) * 0.125
        dp_out[rows, at(0)] = jnp.where(lane, dq[:128], dq[128:]).astype(bf16)
        dp_out[rows, at(1024)] = (dot(ds, stacked_heads(q, lane), TN) * 0.125).astype(bf16)
        return 0

    lax.fori_loop(0, 16, unit, 0, unroll=4)
    small[2:3, :] = jnp.sum(dp_out[:, 0:1024].astype(f32), axis=0, keepdims=True)
    small[3:4, :] = jnp.sum(dp_out[:, 2048:3072].astype(f32), axis=0, keepdims=True)
    small[4:16, :] = small_ref[4:16, :]
    dp_out[:, 3072:4096] = do_ref[...]
    wait(first)
    total = None
    for j in range(6):
        cols = slice(j * 512, j * 512 + 512)
        part = dot(dp_out[:, cols], w_qkv[:, :, :, cols].reshape(D, 512), NT)
        total = part if total is None else total + part
    hat, scale = stats(x_ref[...].astype(f32))
    d_norm, small[0:1, :], small[1:2, :] = norm_back(total, vec[0:1, :], hat, scale)
    dx_out[...] = (dx1_ref[...] + d_norm).astype(dx_out.dtype)


def attention_backward(do, dx1, x, p, soft, small, vec, columns, kind):
    flat = [columns[k][dx][dz] for k in range(CS) for dx in range(XS) for dz in range(ZS)]
    return call(
        attention_backward_kernel,
        [((T, 4096), bf16), ((T, D), kind), ((16, D), f32)],
        [do, dx1, x, p, soft, small, vec] + flat,
        [VM] * 7 + [ANY] * 16,
        scratch=list(ATTENTION_SCRATCH) + [pltpu.VMEM((T, D), bf16)],
        flops=2 * T * D * 4 * D,
        moved=18 * 2**20,
        name="attention_backward",
    )


def picked_kernel(a_ref, m_ref, c_ref, u_ref, mine, theirs):
    x, z, c, _ = place()
    row = lax.broadcasted_iota(jnp.int32, (512, D), 0)
    col = lax.broadcasted_iota(jnp.int32, (512, D), 1)
    eye_r = lax.broadcasted_iota(jnp.int32, (256, 256), 0)
    eye = jnp.where(eye_r == lax.broadcasted_iota(jnp.int32, (256, 256), 1), 1.0, 0.0).astype(bf16)
    dx, dz, inner = row >> 7, (row >> 6) & 1, row & 63
    base = (((x + dx) & 3) << 8) + (((z + dz) & 1) << 7) + inner
    place_base = (dx << 8) + (dz << 7) + inner
    for k, out in enumerate((mine, theirs)):
        ck = near(c, k, CS)
        chosen = jnp.where(col == base + ck * 64, 1.0, 0.0).astype(bf16)
        for n, ref in enumerate((a_ref, m_ref)):
            out[n * 512 : n * 512 + 512, :] = dot(chosen, ref[...], NT).astype(bf16)
        chosen = jnp.where(col == place_base + ck * 64, 1.0, 0.0).astype(bf16)
        out[1024:1536, :] = dot(chosen, c_ref[...], NT).astype(bf16)
        for j in range(8):
            s = 2 * j + ck
            block = u_ref[:, pl.ds(pl.multiple_of(s * 256, 256), 256)]
            out[1536 + j * 256 : 1792 + j * 256, :] = dot(eye, block, NT).astype(bf16)


def picked(a, m, c, u):
    return call(
        picked_kernel,
        [((3584, T), bf16)] * 2,
        [a, m, c, u],
        [VM] * 4,
        flops=2 * 10**9,
        moved=8 * 2**20,
        name="transposed_acts",
    )


def kinds(base, c, size):
    step = 1 - 2 * c
    return [near(base + 4, d, size) for d in (2, -step, step, 0)]


def fc2_grads_kernel(mine, theirs, df, df2, *refs):
    outs, acts, df_all, rows, sems, out_sems = refs[:4], *refs[4:]
    _, _, c, y = place()
    copies = [
        pltpu.make_async_copy(mine.at[1536:3584], acts.at[:, 0:256], sems.at[0]),
        pltpu.make_async_copy(theirs.at[1536:3584], acts.at[:, 256:512], sems.at[1]),
        pltpu.make_async_copy(df, df_all.at[0:256], sems.at[2]),
        pltpu.make_async_copy(df2, df_all.at[256:512], sems.at[3]),
    ]
    start(copies)
    wait(copies)
    for j in range(8):
        grad = dot(acts[j * 256 : j * 256 + 256, :], df_all[...]).astype(bf16)
        rows[:, j] = grad.reshape(YS, 64, 1024)
    sends = [pltpu.make_async_copy(rows.at[yk], outs[n], out_sems.at[n]) for n, yk in enumerate(kinds(y, c, YS))]
    start(sends)
    wait(sends)


def fc2_grads(mine, theirs, df, df2):
    return call(
        fc2_grads_kernel,
        [((8, 64, 1024), bf16)] * 4,
        [mine, theirs, df, df2],
        [ANY] * 4,
        scratch=[
            pltpu.VMEM((2048, 512), bf16),
            pltpu.VMEM((512, D), bf16),
            pltpu.VMEM((4, 8, 64, 1024), bf16),
            pltpu.SemaphoreType.DMA((4,)),
            pltpu.SemaphoreType.DMA((4,)),
        ],
        out_kinds=[ANY] * 4,
        flops=4 * T * D * FF,
        moved=12 * 2**20,
        name="fc2_grads",
    )


def fc1_grads_kernel(mine, theirs, dh, dh2, *refs):
    outs, acts, dh_all, rows, sems, out_sems = refs[:4], *refs[4:]
    _, _, c, y = place()
    copies = [
        pltpu.make_async_copy(mine.at[1024:1536], acts.at[:, 0:256], sems.at[0]),
        pltpu.make_async_copy(theirs.at[1024:1536], acts.at[:, 256:512], sems.at[1]),
        pltpu.make_async_copy(dh, dh_all.at[0:256], sems.at[2]),
        pltpu.make_async_copy(dh2, dh_all.at[256:512], sems.at[3]),
    ]
    start(copies)
    wait(copies)
    sends = []
    for n, yk in enumerate(kinds(y, c, YS)):
        cols = pl.ds(pl.multiple_of(yk * 1024, 1024), 1024)
        for half in range(2):
            grad = dot(acts[half * 256 : half * 256 + 256, :], dh_all[:, cols]).astype(bf16)
            rows[n, 4 * half : 4 * half + 4] = grad.reshape(4, 64, 1024)
        sends.append(pltpu.make_async_copy(rows.at[n], outs[n], out_sems.at[n]))
        sends[-1].start()
    wait(sends)


def fc1_grads(mine, theirs, dh, dh2):
    return call(
        fc1_grads_kernel,
        [((8, 64, 1024), bf16)] * 4,
        [mine, theirs, dh, dh2],
        [ANY] * 4,
        scratch=[
            pltpu.VMEM((512, 512), bf16),
            pltpu.VMEM((512, FF), bf16),
            pltpu.VMEM((4, 8, 64, 1024), bf16),
            pltpu.SemaphoreType.DMA((4,)),
            pltpu.SemaphoreType.DMA((4,)),
        ],
        out_kinds=[ANY] * 4,
        flops=4 * T * D * FF,
        moved=14 * 2**20,
        name="fc1_grads",
    )


def attention_grads_kernel(mine, theirs, dp, dp2, small, small2, *refs):
    outs, acts, dp_all, total, held, sems, out_sems = refs[:4], *refs[4:]
    x, z, c, _ = place()
    copies = [
        pltpu.make_async_copy(mine.at[0:1024], acts.at[:, 0:256], sems.at[0]),
        pltpu.make_async_copy(theirs.at[0:1024], acts.at[:, 256:512], sems.at[1]),
        pltpu.make_async_copy(dp, dp_all.at[0:256], sems.at[2]),
        pltpu.make_async_copy(dp2, dp_all.at[256:512], sems.at[3]),
    ]
    start(copies)
    total[...] = small[...] + small2[...]
    vec = total[...].astype(bf16)
    row = lax.broadcasted_iota(jnp.int32, (D, 128), 0)
    col = lax.broadcasted_iota(jnp.int32, (D, 128), 1)
    line = lax.broadcasted_iota(jnp.int32, (16, 128), 0)
    for j in range(8):
        x_there = near(x, j // 2, XS)
        inner = near(z, j % 2, ZS) * 2 + c
        chosen = jnp.where((row == col + x_there * 256 + inner * 64) & (col < 64), 1.0, 0.0).astype(bf16)
        held[j, :, 4096:4224] = jnp.zeros((64, 128), bf16)
        held[j, 0:16, 4096:4224] = dot(vec, chosen).astype(bf16)
        there = total[pl.ds(10 + x_there, 1), pl.ds(pl.multiple_of(inner * 256, 256), 256)]
        a, b = there[:, 0:128], there[:, 128:256]
        held[j, 16:32, 4096:4224] = jnp.where(line == 0, a, jnp.where(line == 1, b, 0.0)).astype(bf16)
    wait(copies)
    for n in range(8):
        source = acts[0:512, :] if n < 6 else acts[512:1024, :]
        grad = dot(source, dp_all[:, n * 512 : n * 512 + 512]).astype(bf16)
        held[:, :, n * 512 : n * 512 + 512] = grad.reshape(8, 64, 512)
    sends = [
        pltpu.make_async_copy(held.at[pl.ds(2 * dx, 2)], outs[n], out_sems.at[n])
        for n, dx in enumerate(kinds(jnp.int32(0), c, XS))
    ]
    start(sends)
    wait(sends)


def attention_grads(mine, theirs, dp, dp2, small, small2):
    return call(
        attention_grads_kernel,
        [((2, 64, QP), bf16)] * 4,
        [mine, theirs, dp, dp2, small, small2],
        [ANY] * 4 + [VM] * 2,
        scratch=[
            pltpu.VMEM((1024, 512), bf16),
            pltpu.VMEM((512, 4096), bf16),
            pltpu.VMEM((16, D), f32),
            pltpu.VMEM((8, 64, QP), bf16),
            pltpu.SemaphoreType.DMA((4,)),
            pltpu.SemaphoreType.DMA((4,)),
        ],
        out_kinds=[ANY] * 4,
        flops=8 * T * D * 2 * D,
        moved=16 * 2**20,
        name="attention_grads",
    )


def sum_kernel(count, axis, *refs):
    total = refs[0][...].astype(f32)
    for ref in refs[1:count]:
        total = total + ref[...].astype(f32)
    outs = refs[count:]
    if axis == "add":
        outs[0][...] = jnp.sum(total, axis=0).astype(bf16)
    elif axis == "split":
        for n, out in enumerate(outs):
            out[...] = total[n].astype(bf16)
    else:
        outs[0][...] = total.astype(bf16)


def summed(parts, axis=None):
    shape = parts[0].shape
    outs = [(shape[1:], bf16)] * shape[0] if axis == "split" else [(shape[1:] if axis else shape, bf16)]
    size = 1
    for n in shape:
        size *= n
    out = call(
        lambda *refs: sum_kernel(len(parts), axis, *refs),
        outs,
        parts,
        [VM] * len(parts),
        flops=size * len(parts),
        moved=2 * size * (len(parts) + 1),
        name="summed",
    )
    return out if axis == "split" else out[0]


def scattered(parts, axis):
    opposite, behind, ahead, here = parts
    far = onward(opposite, axis)
    given = onward(from_shard(behind, dc=1), axis)
    own = onward(summed([ahead, far]), axis)
    return [here, own, from_shard(given, dc=1)]


def scatter_columns(parts):
    same, other = summed(scattered(parts, "x"), "split")
    return summed([same, from_shard(other, dz=1)])


def scatter_rows(parts):
    groups = [[shard_of(x, z, c) for x in range(XS) for z in range(ZS)] for c in range(CS)]
    places = summed(scattered(parts, "y"))
    got = lax.all_to_all(places, "shard", split_axis=0, concat_axis=0, axis_index_groups=groups, tiled=True)
    return summed([got], "add")


def results_kernel(*refs):
    fc1, fc2, columns = refs[0:4], refs[4:8], refs[8:12]
    g_qkv, g_proj, g_fc1, g_fc2, g_vec, g_bias, fc1_all, fc2_all, cols_all, sems = refs[12:]
    _, _, _, y = place()
    copies = []
    for dy in range(YS):
        yk = near(y, dy, YS)
        copies.append(pltpu.make_async_copy(fc1[dy], fc1_all.at[yk], sems.at[0, dy]))
        copies.append(pltpu.make_async_copy(fc2[dy], fc2_all.at[yk], sems.at[1, dy]))
        copies.append(pltpu.make_async_copy(columns[dy], cols_all.at[yk], sems.at[2, dy]))
    start(copies)
    wait(copies)
    for k in range(YS):
        g_fc1[:, k * 1024 : k * 1024 + 1024] = fc1_all[k].astype(f32)
        g_fc2[k * 64 : k * 64 + 64, :] = fc2_all[k].astype(f32)
    total = lambda rows, low, high: sum(cols_all[k, rows, low:high].astype(f32) for k in range(YS))
    g_qkv[...] = total(slice(0, 64), 0, 3072)
    g_proj[...] = total(slice(0, 64), 3072, 4096)
    g_vec[...] = total(slice(0, 16), 4096, 4224)
    g_bias[...] = total(slice(16, 32), 4096, 4224)


def results(fc1, fc2, columns):
    return call(
        results_kernel,
        [((64, 3072), f32), ((64, 1024), f32), ((64, FF), f32), ((256, D), f32), ((16, 128), f32), ((16, 128), f32)],
        list(fc1) + list(fc2) + list(columns),
        [ANY] * 12,
        scratch=[
            pltpu.VMEM((4, 64, 1024), bf16),
            pltpu.VMEM((4, 64, 1024), bf16),
            pltpu.VMEM((4, 64, QP), bf16),
            pltpu.SemaphoreType.DMA((3, 4)),
        ],
        moved=10 * 2**20,
        name="results",
    )


def gather(w_qkv, w_proj, w_fc1, w_fc2, vectors, fc1_bias):
    twin = lambda v: from_shard(v, dc=1)
    unit, piece = pack(w_qkv, w_proj, w_fc1, w_fc2, vectors, fc1_bias)
    pieces = [
        piece if (dx, dz) == (0, 0) else from_shard(piece, dx=dx, dz=dz) for dx in range(XS) for dz in range(ZS)
    ]
    here = placed_pieces(pieces)
    unit, here = lax.optimization_barrier((unit, here))
    twin_here = twin(here)
    behind = onward(here, "y")
    twin_behind = onward(twin_here, "y")
    opposite = onward(behind, "y")
    rows = [
        [here, behind, twin(twin_behind), opposite],
        [twin_here, twin_behind, twin(behind), twin(opposite)],
    ]
    other = from_shard(unit, dz=1)
    plus = [from_shard(unit, dx=1), from_shard(other, dx=1)]
    minus = [from_shard(unit, dx=3), from_shard(other, dx=3)]
    far = [from_shard(plus[0], dx=1), from_shard(minus[1], dx=3)]
    mine = [[unit, other], plus, far, minus]
    columns = [mine, [[twin(v) for v in pair] for pair in mine]]
    return columns, rows


def shards(edge_inputs, image_counts, w_qkv, w_proj, w_fc1, w_fc2, vectors, fc1_bias):
    section = lax.axis_index("section")
    _, _, _, y = place()
    source = edge_inputs[0, :, 0]
    present = (lax.axis_index("shard") * YS + y < image_counts).astype(f32)
    columns, rows = gather(w_qkv[0], w_proj[0], w_fc1[0], w_fc2[0], vectors[0], fc1_bias[0])
    vec, bias = gathered_vectors(columns)

    own = source.reshape(T, D)
    x1, c = attention_forward(False, own, vec, columns)
    (first_out,) = feed_forward(False, x1, c, vec, bias, columns, rows)
    received = passed_along(first_out, 1)
    inputs = jnp.where(section == 0, own, received)
    a, p, soft, m, o, x1, c = attention_forward(True, inputs, vec, columns)
    u, gp, f, output = feed_forward(True, x1, c, vec, bias, columns, rows)

    twin = lambda v: from_shard(v, dc=1)
    around = lambda v: [v] + [from_replica(v, dy) for dy in range(1, YS)]
    second_scale = vec[9:10, :]
    cotangent = (source.astype(f32) * present[:, None, None]).reshape(T, D)
    df = (second_scale * cotangent).astype(bf16)
    _, dx1, do, small = feed_backward(cotangent, df, f, gp, x1, o, vec, columns, rows)
    _, dx, _ = attention_backward(do, dx1, inputs, p, soft, small, vec, columns, bf16)
    received_grad = passed_along(dx, -1)
    mine, theirs = picked(a, m, c, u)
    received_grad, mine, theirs = lax.optimization_barrier((received_grad, mine, twin(theirs)))

    upstream = jnp.where(section == 1, cotangent, received_grad.astype(f32))
    df = (second_scale * upstream).astype(bf16)
    fc2_parts = fc2_grads(mine, theirs, df, twin(df))
    upstream, df, fc2_parts = lax.optimization_barrier((upstream, df, fc2_parts))
    fc2 = scatter_rows(fc2_parts)
    dh, dx1, do, small = feed_backward(upstream, df, f, gp, x1, o, vec, columns, rows)
    dp, dx, small = attention_backward(do, dx1, inputs, p, soft, small, vec, columns, f32)
    dh, dh2, dp, small = lax.optimization_barrier((dh, twin(dh), dp, small))
    fc1_parts = fc1_grads(mine, theirs, dh, dh2)
    dp, dp2, small, small2, fc1_parts = lax.optimization_barrier((dp, twin(dp), small, twin(small), fc1_parts))
    fc1 = scatter_rows(fc1_parts)
    column = scatter_columns(attention_grads(mine, theirs, dp, dp2, small, small2))
    g_qkv, g_proj, g_fc1, g_fc2, g_vec, g_bias = results(around(fc1), around(fc2), around(column))
    edge_values = jnp.where(section == 0, dx, output).reshape(1, 2, 1, 128, D)
    return (
        edge_values,
        g_qkv[None],
        g_proj[None],
        g_fc1[None],
        g_fc2[None],
        g_vec[None, :10, :64],
        g_bias[:2].reshape(1, 256),
    )


def solution(mesh):
    placed = (
        P("section", None, ("shard", "replica"), None, None),
        P(),
        P("section", "shard", None),
        P("section", "shard", None),
        P("section", "shard", None),
        P("section", "shard", None),
        P("section", None, "shard"),
        P("section", "shard"),
    )
    return jax.shard_map(
        shards,
        mesh=mesh,
        in_specs=placed,
        out_specs=(placed[0],) + placed[2:],
        check_vma=False,
    )
```

```python
import jax
import jax.numpy as jnp
from jax import lax
from jax.experimental import pallas as pl
from jax.experimental.pallas import tpu as pltpu
from jax.sharding import PartitionSpec as P

XS, ZS, CS, YS = 4, 2, 2, 4
T = 256
D, FF = 1024, 4096
GROWS = 32
TAILS = 4 - GROWS // 16
UNIT = 4096 + 1024 * TAILS + 128
QP = 4224
LIMIT = 8
epsilon = 1e-06
bf16, f32 = jnp.bfloat16, jnp.float32
ANY = pl.BlockSpec(memory_space=pl.ANY)
HB = pl.BlockSpec(memory_space=pltpu.HBM)
VM = pl.BlockSpec(memory_space=pltpu.VMEM)
SM = pl.BlockSpec(memory_space=pltpu.SMEM)
NT = (((1,), (1,)), ((), ()))
TN = (((0,), (0,)), ((), ()))


def shard_of(x, z, c):
    return (x % XS) * 4 + (z % ZS) * 2 + (c % CS)


def from_shard(value, dx=0, dz=0, dc=0, name="from_shard"):
    pairs = [
        (shard_of(x + dx, z + dz, c + dc), shard_of(x, z, c))
        for x in range(XS)
        for z in range(ZS)
        for c in range(CS)
    ]
    with jax.named_scope(name):
        return lax.ppermute(value, "shard", pairs)


def from_replica(value, dy):
    return lax.ppermute(value, "replica", [((y + dy) % YS, y) for y in range(YS)])


def onward(value, axis, name="onward"):
    pairs = []
    for x in range(XS):
        for z in range(ZS):
            for c in range(CS):
                for y in range(YS):
                    step = 1 - 2 * c
                    tx, ty = (x + step, y) if axis == "x" else (x, y + step)
                    pairs.append((shard_of(x, z, c) * YS + y, shard_of(tx, z, c) * YS + ty % YS))
    with jax.named_scope(name):
        return lax.ppermute(value, ("shard", "replica"), pairs)


def passed_along(value, steps):
    return lax.ppermute(value, "section", [(0, 1)] if steps == 1 else [(1, 0)])


def place():
    shard = lax.axis_index("shard")
    x = lax.div(shard, jnp.int32(4))
    z = lax.rem(lax.div(shard, jnp.int32(2)), jnp.int32(2))
    c = lax.rem(shard, jnp.int32(2))
    return x, z, c, lax.axis_index("replica")


def near(base, step, size):
    return lax.rem(base + jnp.int32(step), jnp.int32(size))


def call(kernel, outs, args, kinds, scratch=(), flops=0, moved=0, out_kinds=None, name=None, aliases=None, limit=LIMIT):
    return pl.pallas_call(
        kernel,
        out_shape=[jax.ShapeDtypeStruct(s, d) for s, d in outs],
        in_specs=list(kinds),
        out_specs=list(out_kinds or [VM] * len(outs)),
        scratch_shapes=list(scratch),
        compiler_params=pltpu.CompilerParams(vmem_limit_bytes=limit * 2**20),
        cost_estimate=pl.CostEstimate(flops=1, bytes_accessed=1, transcendentals=0),
        name=name,
        input_output_aliases=aliases or {},
    )(*args)


def after(values, token):
    return lax.optimization_barrier((values, token))[0]


def dot(a, b, dims=(((1,), (0,)), ((), ()))):
    return lax.dot_general(a, b, dims, preferred_element_type=f32)


def stats(values):
    average = jnp.mean(values, axis=-1, keepdims=True)
    centered = values - average
    spread = jnp.mean(centered * centered, axis=-1, keepdims=True)
    scale = lax.rsqrt(spread + epsilon)
    return centered * scale, scale


def norm_back(grad, gain, hat, scale):
    d_hat = grad * gain
    d_in = scale * (
        d_hat - jnp.mean(d_hat, axis=-1, keepdims=True) - hat * jnp.mean(d_hat * hat, axis=-1, keepdims=True)
    )
    return d_in, jnp.sum(grad * hat, axis=0, keepdims=True), jnp.sum(grad, axis=0, keepdims=True)


def places(base, c, size):
    step = 1 - 2 * c
    return [near(base + 4, d, size) for d in (2, -step, step, 0)]


def pack_kernel(qkv, proj, fc1, fc2, vectors, bias, unit, pieces, small, sems):
    _, _, _, y = place()
    small[...] = jnp.zeros_like(small)
    small[0:10, 0:64] = vectors[...].astype(f32)
    small[16:17, :] = bias[:, 0:128].astype(f32)
    small[17:18, :] = bias[:, 128:256].astype(f32)
    copies = [pltpu.make_async_copy(qkv, unit.at[:, 0:3072], sems.at[0])]
    copies.append(pltpu.make_async_copy(proj, unit.at[:, 3072:4096], sems.at[1]))
    for n in range(TAILS):
        row, col = 4 * GROWS + 64 * n, 4096 + 1024 * n
        copies.append(
            pltpu.make_async_copy(fc2.at[row : row + 64], unit.at[:, col : col + 1024], sems.at[2 + n])
        )
    block = fc1.at[:, pl.ds(pl.multiple_of(y * 1024, 1024), 1024)]
    rows = fc2.at[pl.ds(pl.multiple_of(y * GROWS, 16), GROWS)]
    for n in range(8):
        at = 2 + TAILS + 2 * n
        copies.append(pltpu.make_async_copy(block, pieces.at[n, 0:64], sems.at[at]))
        copies.append(pltpu.make_async_copy(rows, pieces.at[n, 64 : 64 + GROWS], sems.at[at + 1]))
    start(copies)
    wait(copies)
    unit[:, UNIT - 128 : UNIT] = small[...].astype(bf16)


def pack(w_qkv, w_proj, w_fc1, w_fc2, vectors, fc1_bias):
    return call(
        pack_kernel,
        [((64, UNIT), bf16), ((8, 64 + GROWS, 1024), bf16)],
        (w_qkv, w_proj, w_fc1, w_fc2, vectors, fc1_bias),
        [HB] * 4 + [VM] * 2,
        scratch=[pltpu.VMEM((64, 128), f32), pltpu.SemaphoreType.DMA((18 + TAILS,))],
        moved=4 * 2**20,
        name="pack_parts",
        limit=56,
    )


def start(copies):
    for copy in copies:
        copy.start()


def wait(copies):
    for copy in copies:
        copy.wait()


def columns_kernel(keys, *refs):
    pieces, (qkv, proj, fc2, small), sems = refs, refs[-5:-1], refs[-1]
    x, z, c, _ = place()
    copies = []
    for n, (k, dx, dz, array, row) in enumerate(keys):
        piece = pieces[array] if row is None else pieces[array].at[row]
        xz, ck = near(x, dx, XS) * 2 + near(z, dz, ZS), near(c, k, CS)
        parts = [(0, 3072, qkv.at[xz, ck]), (3072, 4096, proj.at[xz, ck]), (UNIT - 128, UNIT, small.at[xz, ck])]
        for t in range(TAILS):
            first, col = 4 * GROWS + 64 * t, 4096 + 1024 * t
            parts.append((col, col + 1024, fc2.at[xz, ck, first : first + 64]))
        for t, (low, high, target) in enumerate(parts):
            copies.append(pltpu.make_async_copy(piece.at[:, low:high], target, sems.at[n, t]))
    start(copies)
    wait(copies)


def put_columns(weights, keys, arrays):
    held = list(weights or [])
    count = len(arrays)
    return list(
        call(
            lambda *refs: columns_kernel(keys, *refs),
            [((8, 2, 64, 3072), bf16), ((8, 2, 64, 1024), bf16), ((8, 2, 256, 1024), bf16), ((8, 2, 64, 128), bf16)],
            list(arrays) + held,
            [ANY] * count + [VM] * len(held),
            scratch=[pltpu.SemaphoreType.DMA((len(keys), 3 + TAILS))],
            moved=count * 2**20,
            name="put_columns",
            aliases={count + n: n for n in range(len(held))},
        )
    )


def stack_kernel(*refs):
    pieces, out, sems = refs[:-2], refs[-2], refs[-1]
    copies = [pltpu.make_async_copy(piece, out.at[n], sems.at[n]) for n, piece in enumerate(pieces)]
    start(copies)
    wait(copies)


def stacked(pieces):
    return call(
        stack_kernel,
        [((len(pieces),) + pieces[0].shape, bf16)],
        pieces,
        [ANY] * len(pieces),
        scratch=[pltpu.SemaphoreType.DMA((len(pieces),))],
        moved=4 * 2**20,
        name="stacked",
    )[0]


def rows_kernel(keys, *refs):
    count = len(keys)
    pieces, (fc1, fc2), sems = refs[:count], refs[-3:-1], refs[-1]
    _, _, c, y = place()
    copies = []
    for n, (k, kind) in enumerate(keys):
        ck, yk = near(c, k, CS), places(y, c, YS)[kind]
        copies.append(pltpu.make_async_copy(pieces[n].at[:, 0:64], fc1.at[yk, :, ck], sems.at[n, 0]))
        target = fc2.at[:, ck, pl.ds(pl.multiple_of(yk * GROWS, 16), GROWS)]
        copies.append(pltpu.make_async_copy(pieces[n].at[:, 64 : 64 + GROWS], target, sems.at[n, 1]))
    start(copies)
    wait(copies)


def put_rows(fc1, fc2, pieces):
    keys = list(pieces)
    held = [fc1, fc2] if fc1 is not None else [fc2]
    count = len(keys)
    return call(
        lambda *refs: rows_kernel(keys, *refs),
        [((4, 8, 2, 64, 1024), bf16), ((8, 2, 256, 1024), bf16)],
        [pieces[key] for key in keys] + held,
        [ANY] * count + [VM] * len(held),
        scratch=[pltpu.SemaphoreType.DMA((count, 2))],
        moved=2 * count * 2**20,
        name="put_rows",
        aliases={count + n: 2 - len(held) + n for n in range(len(held))},
    )


def vectors_kernel(small, vec, bias):
    lane = lax.broadcasted_iota(jnp.int32, (16, 128), 1)
    for t in range(8):
        a = small[t, 0, 0:16].astype(f32)
        b = small[t, 1, 0:16].astype(f32)
        vec[:, t * 128 : t * 128 + 128] = jnp.where(lane < 64, a, pltpu.roll(b, 64, 1))
    for s in range(16):
        tail = small[s // 2, s % 2, 16:32].astype(f32)
        bias[0:1, s * 256 : s * 256 + 128] = tail[0:1]
        bias[0:1, s * 256 + 128 : s * 256 + 256] = tail[1:2]


def gathered_vectors(small):
    return call(
        vectors_kernel, [((16, 1024), f32), ((1, FF), f32)], [small], [VM], moved=2**20, name="gathered_vectors"
    )


def stacked_heads(pair, lane):
    zero = jnp.zeros_like(pair)
    return jnp.concatenate([jnp.where(lane, pair, zero), jnp.where(lane, zero, pair)], axis=0)


def attention_forward_kernel(keep, x_ref, vec, w_qkv, w_proj, *refs):
    if keep:
        received, x_out, a_out, p_out, soft_out, m_out, o_out, x1_out, c_out = refs
        x_out[...] = jnp.where(lax.axis_index("section") == 0, x_ref[...].astype(f32), received[...].astype(f32)).astype(bf16)
        x = x_out[...].astype(f32)
    else:
        x1_out, c_out, p_out, m_out = refs
        x = x_ref[...].astype(f32)
    hat, _ = stats(x)
    a = (hat * vec[0:1, :] + vec[1:2, :]).astype(bf16)
    if keep:
        a_out[...] = a
    for j in range(6):
        part = dot(a, w_qkv[:, :, :, j * 512 : j * 512 + 512].reshape(D, 512))
        if j < 2:
            part = part + vec[2:3, j * 512 : j * 512 + 512]
        if j >= 4:
            part = part + vec[3:4, j * 512 - 2048 : j * 512 - 1536]
        p_out[:, j * 512 : j * 512 + 512] = part.astype(bf16)
    lane = lax.broadcasted_iota(jnp.int32, (128, 128), 1) < 64

    def unit(u, _):
        i, h = lax.div(u, jnp.int32(8)), lax.rem(u, jnp.int32(8))
        rows = pl.ds(pl.multiple_of(i * 128, 128), 128)
        q, k, v = [p_out[rows, pl.ds(pl.multiple_of(h * 128 + o, 128), 128)] for o in (0, 1024, 2048)]
        s = dot(stacked_heads(q, lane), k, NT) * 0.125
        e = jnp.exp(s - jnp.max(s, axis=-1, keepdims=True))
        soft = e / jnp.sum(e, axis=-1, keepdims=True)
        if keep:
            soft_out[u] = soft
        mixed = dot(soft.astype(bf16), v)
        m_out[rows, pl.ds(pl.multiple_of(h * 128, 128), 128)] = jnp.where(lane, mixed[:128], mixed[128:]).astype(bf16)
        return 0

    lax.fori_loop(0, 16, unit, 0, unroll=16)
    o = dot(m_out[...], w_proj[...].reshape(D, D)) + vec[4:5, :]
    x1 = x + vec[5:6, :] * o
    if keep:
        o_out[...] = o
    x1_out[...] = x1
    hat, _ = stats(x1)
    c_out[...] = (hat * vec[6:7, :] + vec[7:8, :]).astype(bf16)


def attention_forward(keep, x, vec, weights, received=None):
    outs = [((T, D), f32), ((T, D), bf16)]
    scratch = []
    if keep:
        outs = [((T, D), bf16)] * 2 + [((T, 3072), bf16), ((16, 256, 128), f32), ((T, D), bf16), ((T, D), f32)] + outs
    else:
        scratch = [pltpu.VMEM((T, 3072), bf16), pltpu.VMEM((T, D), bf16)]
    return call(
        lambda *refs: attention_forward_kernel(keep, *refs),
        outs,
        [x, vec, weights[0], weights[1]] + ([received] if keep else []),
        [VM] * (5 if keep else 4),
        scratch=scratch,
        flops=2 * T * D * 4 * D,
        moved=14 * 2**20,
        name="attention_forward",
    )


def fc1_tile(w1, t):
    return w1[t // 2, :, :, :, (t % 2) * 512 : (t % 2) * 512 + 512].reshape(D, 512)


def feed_forward_kernel(keep, x1_ref, c_ref, vec, bias, w1, w2, *refs):
    if keep:
        u_out, gp_out, f_out, y_out = refs
    else:
        (y_out,) = refs
    c = c_ref[...]
    total = None
    ahead = dot(c, fc1_tile(w1, 0))
    for t in range(8):
        cols = slice(t * 512, t * 512 + 512)
        h = ahead + bias[0:1, cols]
        if t < 7:
            ahead = dot(c, fc1_tile(w1, t + 1))
        cdf = 0.5 * (1.0 + lax.erf(h * 0.7071067811865476))
        u = (h * cdf).astype(bf16)
        if keep:
            gp = cdf + h * (jnp.exp(-0.5 * h * h) * 0.3989422804014327)
            u_out[:, cols] = u
            gp_out[:, cols] = gp.astype(bf16)
        part = dot(u, w2[t].reshape(512, D))
        total = part if total is None else total + part
    f = total + vec[8:9, :]
    if keep:
        f_out[...] = f
    y_out[...] = (x1_ref[...] + vec[9:10, :] * f).astype(y_out.dtype)


def feed_forward(keep, x1, c, vec, bias, weights):
    outs = [((T, D), f32 if keep else bf16)]
    if keep:
        outs = [((T, FF), bf16), ((T, FF), bf16), ((T, D), f32)] + outs
    return call(
        lambda *refs: feed_forward_kernel(keep, *refs),
        outs,
        [x1, c, vec, bias, weights[2], weights[3]],
        [VM] * 6,
        flops=4 * T * D * FF,
        moved=24 * 2**20,
        name="feed_forward",
    )


def upstream_kernel(first, counts, source, *refs):
    vec, g_out, df_out = refs[-3:]
    image = lax.axis_index("shard") * YS + lax.axis_index("replica")
    for m in range(2):
        rows = slice(m * 128, m * 128 + 128)
        g = source[rows, :].astype(f32) * jnp.where(image < counts[m], 1.0, 0.0)
        if not first:
            g = jnp.where(lax.axis_index("section") == 1, g, refs[0][rows, :].astype(f32))
        g_out[rows, :] = g
        df_out[rows, :] = (vec[9:10, :] * g).astype(bf16)


def upstream(counts, source, vec, received=None):
    extra = [] if received is None else [received]
    return call(
        lambda *refs: upstream_kernel(received is None, *refs),
        [((T, D), f32), ((T, D), bf16)],
        [counts, source] + extra + [vec],
        [SM] + [VM] * (2 + len(extra)),
        moved=2**20,
        name="upstream",
    )


def feed_backward_kernel(g_ref, df_ref, f_ref, gp_ref, x1_ref, o_ref, vec, w1, w2, dh_out, dx1_out, do_out, small):
    g = g_ref[...]
    df = df_ref[...]
    small[8:9, :] = jnp.sum(df.astype(f32), axis=0, keepdims=True)
    small[9:10, :] = jnp.sum(g * f_ref[...], axis=0, keepdims=True)
    small[0:4, :] = jnp.zeros((4, D), f32)
    small[14:16, :] = jnp.zeros((2, D), f32)
    total = None
    ahead = dot(df, w2[0].reshape(512, D), NT)
    for t in range(8):
        y, off = t // 2, (t % 2) * 512
        cols = slice(t * 512, t * 512 + 512)
        du = ahead
        if t < 7:
            ahead = dot(df, w2[t + 1].reshape(512, D), NT)
        dh = (gp_ref[:, cols].astype(f32) * du).astype(bf16)
        dh_out[:, cols] = dh
        small[10 + y : 11 + y, off : off + 512] = jnp.sum(dh.astype(f32), axis=0, keepdims=True)
        part = dot(dh, fc1_tile(w1, t), NT)
        total = part if total is None else total + part
    hat, scale = stats(x1_ref[...])
    d_norm, small[6:7, :], small[7:8, :] = norm_back(total, vec[6:7, :], hat, scale)
    dx1 = g + d_norm
    dx1_out[...] = dx1
    small[5:6, :] = jnp.sum(dx1 * o_ref[...], axis=0, keepdims=True)
    do = (vec[5:6, :] * dx1).astype(bf16)
    do_out[...] = do
    small[4:5, :] = jnp.sum(do.astype(f32), axis=0, keepdims=True)


def feed_backward(g, df, f, gp, x1, o, vec, weights):
    return call(
        feed_backward_kernel,
        [((T, FF), bf16), ((T, D), f32), ((T, D), bf16), ((16, D), f32)],
        [g, df, f, gp, x1, o, vec, weights[2], weights[3]],
        [VM] * 9,
        flops=4 * T * D * FF,
        moved=26 * 2**20,
        name="feed_backward",
    )


def attention_backward_kernel(
    do_ref, dx1_ref, x_ref, p_ref, soft_ref, small_ref, vec, w_qkv, w_proj, *refs
):
    dp_out, dx_out, small, dm_ref = refs[-4:]
    dm_ref[...] = dot(do_ref[...], w_proj[...].reshape(D, D), NT).astype(bf16)
    lane = lax.broadcasted_iota(jnp.int32, (128, 128), 1) < 64

    def unit(u, _):
        i, h = lax.div(u, jnp.int32(8)), lax.rem(u, jnp.int32(8))
        rows = pl.ds(pl.multiple_of(i * 128, 128), 128)
        at = lambda o: pl.ds(pl.multiple_of(h * 128 + o, 128), 128)
        q, k, v = [p_ref[rows, at(o)] for o in (0, 1024, 2048)]
        dm = stacked_heads(dm_ref[rows, at(0)], lane)
        soft = soft_ref[u]
        dp_out[rows, at(2048)] = dot(soft.astype(bf16), dm, TN).astype(bf16)
        dw = dot(dm, v, NT)
        ds = (soft * (dw - jnp.sum(soft * dw, axis=-1, keepdims=True))).astype(bf16)
        dq = dot(ds, k) * 0.125
        dp_out[rows, at(0)] = jnp.where(lane, dq[:128], dq[128:]).astype(bf16)
        dp_out[rows, at(1024)] = (dot(ds, stacked_heads(q, lane), TN) * 0.125).astype(bf16)
        return 0

    lax.fori_loop(0, 16, unit, 0, unroll=16)
    small[2:3, :] = jnp.sum(dp_out[:, 0:1024].astype(f32), axis=0, keepdims=True)
    small[3:4, :] = jnp.sum(dp_out[:, 2048:3072].astype(f32), axis=0, keepdims=True)
    small[4:16, :] = small_ref[4:16, :]
    dp_out[:, 3072:4096] = do_ref[...]
    total = None
    for j in range(6):
        cols = slice(j * 512, j * 512 + 512)
        part = dot(dp_out[:, cols], w_qkv[:, :, :, cols].reshape(D, 512), NT)
        total = part if total is None else total + part
    hat, scale = stats(x_ref[...].astype(f32))
    d_norm, small[0:1, :], small[1:2, :] = norm_back(total, vec[0:1, :], hat, scale)
    dx = dx1_ref[...] + d_norm
    if len(refs) > 4:
        dx = jnp.where(lax.axis_index("section") == 0, dx, refs[0][...])
    dx_out[...] = dx.astype(dx_out.dtype)


def attention_backward(do, dx1, x, p, soft, small, vec, weights, output=None):
    extra = [] if output is None else [output]
    return call(
        attention_backward_kernel,
        [((T, 4096), bf16), ((T, D), f32 if extra else bf16), ((16, D), f32)],
        [do, dx1, x, p, soft, small, vec, weights[0], weights[1]] + extra,
        [VM] * (9 + len(extra)),
        scratch=[pltpu.VMEM((T, D), bf16)],
        flops=2 * T * D * 4 * D,
        moved=18 * 2**20,
        name="attention_backward",
    )


def picked_kernel(a_ref, m_ref, c_ref, u_ref, mine, theirs):
    x, z, c, _ = place()
    row = lax.broadcasted_iota(jnp.int32, (512, D), 0)
    col = lax.broadcasted_iota(jnp.int32, (512, D), 1)
    eye_r = lax.broadcasted_iota(jnp.int32, (256, 256), 0)
    eye = jnp.where(eye_r == lax.broadcasted_iota(jnp.int32, (256, 256), 1), 1.0, 0.0).astype(bf16)
    kind, dz, inner = row >> 7, (row >> 6) & 1, row & 63
    for k, out in enumerate((mine, theirs)):
        ck = near(c, k, CS)
        step = 1 - 2 * ck
        there = jnp.where(kind == 0, 2, jnp.where(kind == 1, 4 - step, jnp.where(kind == 2, 4 + step, 0)))
        there = (((x + there) & 3) << 8) + (((z + dz) & 1) << 7) + inner + ck * 64
        chosen = jnp.where(col == there, 1.0, 0.0).astype(bf16)
        for n, ref in enumerate((a_ref, m_ref)):
            out[n * 512 : n * 512 + 512, :] = dot(chosen, ref[...], NT).astype(bf16)
        there = ((row >> 6) << 7) + inner + ck * 64
        chosen = jnp.where(col == there, 1.0, 0.0).astype(bf16)
        out[1024:1536, :] = dot(chosen, c_ref[...], NT).astype(bf16)
        for j in range(8):
            block = u_ref[:, pl.ds(pl.multiple_of((2 * j + ck) * 256, 256), 256)]
            turned = dot(eye, block, NT).astype(bf16)
            for k2 in range(YS):
                out[1536 + k2 * 512 + j * 64 : 1600 + k2 * 512 + j * 64, :] = turned[k2 * 64 : k2 * 64 + 64]


def picked(a, m, c, u):
    return call(
        picked_kernel,
        [((3584, T), bf16)] * 2,
        [a, m, c, u],
        [VM] * 4,
        flops=2 * 10**9,
        moved=8 * 2**20,
        name="transposed_acts",
    )


def fc2_grads_kernel(mine, theirs, df, df2, *outs):
    _, _, c, y = place()
    for n, yk in enumerate(places(y, c, YS)):
        rows = pl.ds(pl.multiple_of(1536 + yk * 512, 512), 512)
        grad = dot(mine[rows, :], df[...]) + dot(theirs[rows, :], df2[...])
        outs[n][...] = grad.astype(bf16).reshape(8, 64, 1024)


def fc1_grads_kernel(mine, theirs, dh, dh2, *outs):
    _, _, c, y = place()
    for n, yk in enumerate(places(y, c, YS)):
        cols = pl.ds(pl.multiple_of(yk * 1024, 1024), 1024)
        grad = dot(mine[1024:1536, :], dh[:, cols]) + dot(theirs[1024:1536, :], dh2[:, cols])
        outs[n][...] = grad.astype(bf16).reshape(8, 64, 1024)


def feed_grads(kernel, name, mine, theirs, given, given2):
    return call(
        kernel,
        [((8, 64, 1024), bf16)] * 4,
        [mine, theirs, given, given2],
        [VM] * 4,
        flops=4 * T * D * FF,
        moved=12 * 2**20,
        name=name,
    )


def attention_grads_kernel(mine, theirs, dp, dp2, small, small2, *refs):
    outs, total = refs[:4], refs[4]
    x, z, c, _ = place()
    total[...] = small[...] + small2[...]
    vec = total[...].astype(bf16)
    row = lax.broadcasted_iota(jnp.int32, (D, 128), 0)
    col = lax.broadcasted_iota(jnp.int32, (D, 128), 1)
    line = lax.broadcasted_iota(jnp.int32, (16, 128), 0)
    for n, x_there in enumerate(places(x, c, XS)):
        for dz in range(ZS):
            inner = near(z, dz, ZS) * 2 + c
            chosen = jnp.where((row == col + x_there * 256 + inner * 64) & (col < 64), 1.0, 0.0).astype(bf16)
            outs[n][dz, 32:64, 4096:4224] = jnp.zeros((32, 128), bf16)
            outs[n][dz, 0:16, 4096:4224] = dot(vec, chosen).astype(bf16)
            there = total[pl.ds(10 + x_there, 1), pl.ds(pl.multiple_of(inner * 256, 256), 256)]
            a, b = there[:, 0:128], there[:, 128:256]
            outs[n][dz, 16:32, 4096:4224] = jnp.where(line == 0, a, jnp.where(line == 1, b, 0.0)).astype(bf16)
    for t in range(8):
        low = 0 if t < 6 else 512
        cols = slice(t * 512, t * 512 + 512)
        grad = dot(mine[low : low + 512, :], dp[:, cols]) + dot(theirs[low : low + 512, :], dp2[:, cols])
        grad = grad.astype(bf16)
        for n in range(4):
            outs[n][:, :, cols] = grad[n * 128 : n * 128 + 128].reshape(2, 64, 512)


def attention_grads(mine, theirs, dp, dp2, small, small2):
    return call(
        attention_grads_kernel,
        [((2, 64, QP), bf16)] * 4,
        [mine, theirs, dp, dp2, small, small2],
        [VM] * 6,
        scratch=[pltpu.VMEM((16, D), f32)],
        flops=8 * T * D * 2 * D,
        moved=16 * 2**20,
        name="attention_grads",
    )


def sum_kernel(count, axis, *refs):
    total = refs[0][...].astype(f32)
    for ref in refs[1:count]:
        total = total + ref[...].astype(f32)
    outs = refs[count:]
    if axis == "add":
        outs[0][...] = jnp.sum(total, axis=0).astype(bf16)
    elif axis == "split":
        for n, out in enumerate(outs):
            out[...] = total[n].astype(bf16)
    elif axis == "quarters":
        outs, held = outs[:4], outs[4]
        held[...] = total
        _, _, _, y = place()
        for dy, out in enumerate(outs):
            out[...] = held[pl.ds(pl.multiple_of(near(y, dy, YS) * 16, 16), 16), :].astype(bf16)
    else:
        outs[0][...] = total.astype(bf16)


def summed(parts, axis=None):
    shape = parts[0].shape
    scratch = []
    if axis == "split":
        outs = [(shape[1:], bf16)] * shape[0]
    elif axis == "quarters":
        outs = [((16,) + shape[1:], bf16)] * 4
        scratch = [pltpu.VMEM(shape, f32)]
    else:
        outs = [(shape[1:] if axis else shape, bf16)]
    size = 1
    for n in shape:
        size *= n
    out = call(
        lambda *refs: sum_kernel(len(parts), axis, *refs),
        outs,
        parts,
        [VM] * len(parts),
        scratch=scratch,
        flops=size * len(parts),
        moved=2 * size * (len(parts) + 1),
        name="summed",
    )
    return out if len(outs) > 1 else out[0]


def results_kernel(*refs):
    fc1, fc2, columns = refs[0:4], refs[4:8], refs[8:12]
    g_qkv, g_proj, g_fc1, g_fc2, g_vec, g_bias, fc1_all, fc2_all, cols_all, sems = refs[12:]
    _, _, _, y = place()
    copies = []
    for dy in range(YS):
        yk = near(y, dy, YS)
        copies.append(pltpu.make_async_copy(fc1[dy], fc1_all.at[yk], sems.at[0, dy]))
        copies.append(pltpu.make_async_copy(fc2[dy], fc2_all.at[yk], sems.at[1, dy]))
        copies.append(pltpu.make_async_copy(columns[dy], cols_all.at[yk], sems.at[2, dy]))
    start(copies)
    wait(copies)
    for k in range(YS):
        g_fc1[:, k * 1024 : k * 1024 + 1024] = fc1_all[k].astype(f32)
        g_fc2[k * 64 : k * 64 + 64, :] = fc2_all[k].astype(f32)
        line = slice(k * 16, k * 16 + 16)
        g_qkv[line, :] = cols_all[k, :, 0:3072].astype(f32)
        g_proj[line, :] = cols_all[k, :, 3072:4096].astype(f32)
    g_vec[...] = cols_all[0, 0:10, 4096:4160].astype(f32)
    g_bias[...] = cols_all[1, 0:2, 4096:4224].astype(f32)


def results(fc1, fc2, columns):
    return call(
        results_kernel,
        [((64, 3072), f32), ((64, 1024), f32), ((64, FF), f32), ((256, D), f32), ((10, 64), f32), ((2, 128), f32)],
        list(fc1) + list(fc2) + list(columns),
        [ANY] * 12,
        scratch=[
            pltpu.VMEM((4, 64, 1024), bf16),
            pltpu.VMEM((4, 64, 1024), bf16),
            pltpu.VMEM((4, 16, QP), bf16),
            pltpu.SemaphoreType.DMA((3, 4)),
        ],
        moved=10 * 2**20,
        name="results",
    )


def twin(value, name="twin"):
    with jax.named_scope(name):
        return from_shard(value, dc=1)


def around(value, name):
    with jax.named_scope(name):
        return [value] + [from_replica(value, dy) for dy in range(1, YS)]


def swap(value, name):
    groups = [[shard_of(x, z, c) for x in range(XS) for z in range(ZS)] for c in range(CS)]
    with jax.named_scope(name):
        return lax.all_to_all(value, "shard", split_axis=0, concat_axis=0, axis_index_groups=groups, tiled=True)


def gather(w_qkv, w_proj, w_fc1, w_fc2, vectors, fc1_bias):
    hold = lax.optimization_barrier
    unit, pieces = pack(w_qkv, w_proj, w_fc1, w_fc2, vectors, fc1_bias)
    here, twin_unit = swap(pieces, "here"), twin(unit, "twin_unit")
    unit, here, twin_unit = hold((unit, here, twin_unit))
    behind, twin_here = onward(here, "y", "behind"), twin(here, "twin_here")
    other = from_shard(unit, dz=1, name="other")
    plus, minus = from_shard(unit, dx=1, name="plus"), from_shard(unit, dx=3, name="minus")
    behind, twin_here, other, plus, minus = hold((behind, twin_here, other, plus, minus))
    twin_behind = onward(twin_here, "y", "twin_behind")
    minus_other, plus_other = from_shard(other, dx=3, name="minus_other"), from_shard(plus, dz=1, name="plus_other")
    far = from_shard(plus, dx=1, name="far")
    first = stacked([other, plus, minus])
    twins = twin(first, "twin_first")
    weights = put_columns(None, [(0, 0, 0, 0, None), (1, 0, 0, 1, None)], [unit, twin_unit])
    fc1, weights[2] = put_rows(None, weights[2], {(0, 3): here, (1, 3): twin_here})
    held = hold((twin_behind, minus_other, plus_other, far, first, twins, fc1, weights))
    twin_behind, minus_other, plus_other, far, first, twins, fc1, weights = held
    opposite = onward(behind, "y", "opposite")
    far_other = from_shard(far, dz=1, name="far_other")
    ahead, twin_ahead = twin(twin_behind, "ahead"), twin(behind, "twin_ahead")
    second = stacked([minus_other, plus_other, far])
    second_twins = twin(second, "twin_second")
    order = [(0, 1), (1, 0), (3, 0)]
    weights = put_columns(weights, [(k, dx, dz, k, n) for k in range(2) for n, (dx, dz) in enumerate(order)], [first, twins])
    fc1, weights[2] = put_rows(fc1, weights[2], {(0, 1): behind, (1, 1): twin_behind})
    held = hold((opposite, far_other, ahead, twin_ahead, second, second_twins, fc1, weights))
    opposite, far_other, ahead, twin_ahead, second, second_twins, fc1, weights = held
    twin_opposite, twin_far_other = twin(opposite, "twin_opposite"), twin(far_other, "twin_far_other")
    order = [(3, 1), (1, 1), (2, 0)]
    keys = [(k, dx, dz, k, n) for k in range(2) for n, (dx, dz) in enumerate(order)]
    weights = put_columns(weights, keys, [second, second_twins])
    fc1, weights[2] = put_rows(fc1, weights[2], {(0, 2): ahead, (1, 2): twin_ahead})
    weights = put_columns(weights, [(0, 2, 1, 0, None), (1, 2, 1, 1, None)], [far_other, twin_far_other])
    fc1, weights[2] = put_rows(fc1, weights[2], {(0, 0): opposite, (1, 0): twin_opposite})
    vec, bias = gathered_vectors(weights[3])
    return (weights[0], weights[1], fc1, weights[2]), vec, bias


def shards(edge_inputs, image_counts, w_qkv, w_proj, w_fc1, w_fc2, vectors, fc1_bias):
    source = edge_inputs[0, :, 0].reshape(T, D)
    weights, vec, bias = gather(w_qkv[0], w_proj[0], w_fc1[0], w_fc2[0], vectors[0], fc1_bias)

    x1, c = attention_forward(False, source, vec, weights)
    (first_out,) = feed_forward(False, x1, c, vec, bias, weights)
    received = passed_along(first_out, 1)
    inputs, a, p, soft, m, o, x1, c = attention_forward(True, source, vec, weights, received)
    u, gp, f, output = feed_forward(True, x1, c, vec, bias, weights)

    g, df = upstream(image_counts, source, vec)
    _, dx1, do, small = feed_backward(g, df, f, gp, x1, o, vec, weights)
    _, dx, _ = attention_backward(do, dx1, inputs, p, soft, small, vec, weights)
    received_grad = passed_along(dx, -1)
    mine, theirs = picked(a, m, c, u)
    received_grad, mine, theirs = lax.optimization_barrier((received_grad, mine, twin(theirs)))

    hold = lax.optimization_barrier
    g, df = upstream(image_counts, source, vec, received_grad)
    opposite, behind, ahead_2, here_2 = feed_grads(fc2_grads_kernel, "fc2_grads", mine, theirs, df, twin(df, "twin_df"))
    far_2, given_2 = onward(opposite, "y", "far_2"), onward(twin(behind, "behind_2"), "y", "given_2")
    g = after(g, opposite)
    dh, dx1, do, small = feed_backward(g, df, f, gp, x1, o, vec, weights)
    dh2 = twin(dh, "twin_dh")
    dp, edge, small = attention_backward(do, dx1, inputs, p, soft, small, vec, weights, output)
    dh, dh2, dp, far_2 = hold((dh, dh2, dp, far_2))
    dp2, small2 = twin(dp, "twin_dp"), twin(small, "twin_small")
    ahead_2 = summed([ahead_2, far_2])
    own_2 = onward(ahead_2, "y", "own_2")
    parts_1 = feed_grads(fc1_grads_kernel, "fc1_grads", mine, theirs, after(dh, ahead_2), dh2)
    opposite, behind, ahead_1, here_1 = parts_1
    far_1, given_1 = onward(opposite, "y", "far_1"), onward(twin(behind, "behind_1"), "y", "given_1")
    parts_c = attention_grads(mine, theirs, after(dp, here_1), dp2, small, small2)
    opposite, behind, ahead_c, here_c = parts_c
    far_c, given_c = onward(opposite, "x", "far_c"), onward(twin(behind, "behind_c"), "x", "given_c")

    ahead_c = summed([ahead_c, far_c])
    own_c = onward(ahead_c, "x", "own_c")
    sum_2 = summed([after(here_2, ahead_c), own_2, twin(given_2, "twin_given_2")])
    got_2 = swap(sum_2, "swap_2")
    ahead_1 = summed([after(ahead_1, sum_2), far_1])
    own_1 = onward(ahead_1, "y", "own_1")
    fc2 = summed([after(got_2, ahead_1)], "add")
    same, other = summed([after(here_c, fc2), own_c, twin(given_c, "twin_given_c")], "split")
    fc2 = around(fc2, "around_fc2")
    with jax.named_scope("other_z"):
        other = from_shard(other, dz=1)
    quarters = summed([same, other], "quarters")
    with jax.named_scope("quarters"):
        quarters = [quarters[0]] + [from_replica(quarters[dy], YS - dy) for dy in range(1, YS)]
    sum_1 = summed([after(here_1, quarters[0]), own_1, twin(given_1, "twin_given_1")])
    got_1 = swap(sum_1, "swap_1")
    quarters[0] = after(quarters[0], sum_1)
    column = around(summed(quarters), "around_c")
    fc1 = around(summed([got_1], "add"), "around_fc1")
    g_qkv, g_proj, g_fc1, g_fc2, g_vec, g_bias = results(fc1, fc2, column)
    return (
        edge.reshape(1, 2, 1, 128, D),
        g_qkv[None],
        g_proj[None],
        g_fc1[None],
        g_fc2[None],
        g_vec[None],
        g_bias.reshape(1, 256),
    )


def solution(mesh):
    placed = (
        P("section", None, ("shard", "replica"), None, None),
        P(),
        P("section", "shard", None),
        P("section", "shard", None),
        P("section", "shard", None),
        P("section", "shard", None),
        P("section", None, "shard"),
        P("section", "shard"),
    )
    return jax.shard_map(
        shards,
        mesh=mesh,
        in_specs=placed,
        out_specs=(placed[0],) + placed[2:],
        check_vma=False,
    )
```

```python
import jax
import jax.numpy as jnp
from jax import lax
from jax.experimental import pallas as pl
from jax.experimental.pallas import tpu as pltpu
from jax.sharding import PartitionSpec as P

XS, ZS, CS, YS = 4, 2, 2, 4
T = 256
D, FF = 1024, 4096
GROWS = 32
TAILS = 4 - GROWS // 16
UNIT = 4096 + 1024 * TAILS + 128
QP = 4224
LIMIT = 8
HEAVY = ('attention_backward',)
epsilon = 1e-06
bf16, f32 = jnp.bfloat16, jnp.float32
ANY = pl.BlockSpec(memory_space=pl.ANY)
HB = pl.BlockSpec(memory_space=pltpu.HBM)
VM = pl.BlockSpec(memory_space=pltpu.VMEM)
SM = pl.BlockSpec(memory_space=pltpu.SMEM)
NT = (((1,), (1,)), ((), ()))
TN = (((0,), (0,)), ((), ()))


def shard_of(x, z, c):
    return (x % XS) * 4 + (z % ZS) * 2 + (c % CS)


def from_shard(value, dx=0, dz=0, dc=0, name="from_shard"):
    pairs = [
        (shard_of(x + dx, z + dz, c + dc), shard_of(x, z, c))
        for x in range(XS)
        for z in range(ZS)
        for c in range(CS)
    ]
    with jax.named_scope(name):
        return lax.ppermute(value, "shard", pairs)


def from_replica(value, dy):
    return lax.ppermute(value, "replica", [((y + dy) % YS, y) for y in range(YS)])


def onward(value, axis, name="onward"):
    pairs = []
    for x in range(XS):
        for z in range(ZS):
            for c in range(CS):
                for y in range(YS):
                    step = 1 - 2 * c
                    tx, ty = (x + step, y) if axis == "x" else (x, y + step)
                    pairs.append((shard_of(x, z, c) * YS + y, shard_of(tx, z, c) * YS + ty % YS))
    with jax.named_scope(name):
        return lax.ppermute(value, ("shard", "replica"), pairs)


def passed_along(value, steps):
    return lax.ppermute(value, "section", [(0, 1)] if steps == 1 else [(1, 0)])


def place():
    shard = lax.axis_index("shard")
    x = lax.div(shard, jnp.int32(4))
    z = lax.rem(lax.div(shard, jnp.int32(2)), jnp.int32(2))
    c = lax.rem(shard, jnp.int32(2))
    return x, z, c, lax.axis_index("replica")


def near(base, step, size):
    return lax.rem(base + jnp.int32(step), jnp.int32(size))


def call(kernel, outs, args, kinds, scratch=(), flops=0, moved=0, out_kinds=None, name=None, aliases=None, limit=LIMIT):
    return pl.pallas_call(
        kernel,
        out_shape=[jax.ShapeDtypeStruct(s, d) for s, d in outs],
        in_specs=list(kinds),
        out_specs=list(out_kinds or [VM] * len(outs)),
        scratch_shapes=list(scratch),
        compiler_params=pltpu.CompilerParams(vmem_limit_bytes=limit * 2**20),
        cost_estimate=pl.CostEstimate(flops=3 * 10**10 if name in HEAVY else 1, bytes_accessed=1, transcendentals=0),
        name=name,
        input_output_aliases=aliases or {},
    )(*args)


def after(values, token):
    return lax.optimization_barrier((values, token))[0]


def dot(a, b, dims=(((1,), (0,)), ((), ()))):
    return lax.dot_general(a, b, dims, preferred_element_type=f32)


def stats(values):
    average = jnp.mean(values, axis=-1, keepdims=True)
    centered = values - average
    spread = jnp.mean(centered * centered, axis=-1, keepdims=True)
    scale = lax.rsqrt(spread + epsilon)
    return centered * scale, scale


def norm_back(grad, gain, hat, scale):
    d_hat = grad * gain
    d_in = scale * (
        d_hat - jnp.mean(d_hat, axis=-1, keepdims=True) - hat * jnp.mean(d_hat * hat, axis=-1, keepdims=True)
    )
    return d_in, jnp.sum(grad * hat, axis=0, keepdims=True), jnp.sum(grad, axis=0, keepdims=True)


def places(base, c, size):
    step = 1 - 2 * c
    return [near(base + 4, d, size) for d in (2, -step, step, 0)]


def pieces_kernel(fc1, fc2, pieces, sems):
    _, _, _, y = place()
    block = fc1.at[:, pl.ds(pl.multiple_of(y * 1024, 1024), 1024)]
    rows = fc2.at[pl.ds(pl.multiple_of(y * GROWS, 16), GROWS)]
    copies = []
    for n in range(8):
        copies.append(pltpu.make_async_copy(block, pieces.at[n, 0:64], sems.at[2 * n]))
        copies.append(pltpu.make_async_copy(rows, pieces.at[n, 64 : 64 + GROWS], sems.at[2 * n + 1]))
    start(copies)
    wait(copies)


def own_pieces(w_fc1, w_fc2):
    return call(
        pieces_kernel,
        [((8, 64 + GROWS, 1024), bf16)],
        (w_fc1, w_fc2),
        [HB] * 2,
        scratch=[pltpu.SemaphoreType.DMA((16,))],
        moved=4 * 2**20,
        name="own_pieces",
        limit=56,
    )[0]


def unit_kernel(qkv, proj, fc2, vectors, bias, unit, small, sems):
    copies = [pltpu.make_async_copy(qkv, unit.at[:, 0:3072], sems.at[0])]
    copies.append(pltpu.make_async_copy(proj, unit.at[:, 3072:4096], sems.at[1]))
    for n in range(TAILS):
        row, col = 4 * GROWS + 64 * n, 4096 + 1024 * n
        copies.append(
            pltpu.make_async_copy(fc2.at[row : row + 64], unit.at[:, col : col + 1024], sems.at[2 + n])
        )
    start(copies)
    small[...] = jnp.zeros_like(small)
    small[0:10, 0:64] = vectors[...].astype(f32)
    small[16:17, :] = bias[:, 0:128].astype(f32)
    small[17:18, :] = bias[:, 128:256].astype(f32)
    wait(copies)
    unit[:, UNIT - 128 : UNIT] = small[...].astype(bf16)


def own_unit(w_qkv, w_proj, w_fc2, vectors, fc1_bias):
    return call(
        unit_kernel,
        [((64, UNIT), bf16)],
        (w_qkv, w_proj, w_fc2, vectors, fc1_bias),
        [HB] * 3 + [VM] * 2,
        scratch=[pltpu.VMEM((64, 128), f32), pltpu.SemaphoreType.DMA((2 + TAILS,))],
        moved=4 * 2**20,
        name="own_unit",
        limit=56,
    )[0]


def start(copies):
    for copy in copies:
        copy.start()


def wait(copies):
    for copy in copies:
        copy.wait()


def columns_kernel(keys, *refs):
    pieces, (qkv, proj, fc2, small), sems = refs, refs[-5:-1], refs[-1]
    x, z, c, _ = place()
    copies = []
    for n, (k, dx, dz, array, row) in enumerate(keys):
        piece = pieces[array] if row is None else pieces[array].at[row]
        xz, ck = near(x, dx, XS) * 2 + near(z, dz, ZS), near(c, k, CS)
        parts = [(0, 3072, qkv.at[xz, ck]), (3072, 4096, proj.at[xz, ck]), (UNIT - 128, UNIT, small.at[xz, ck])]
        for t in range(TAILS):
            first, col = 4 * GROWS + 64 * t, 4096 + 1024 * t
            parts.append((col, col + 1024, fc2.at[xz, ck, first : first + 64]))
        for t, (low, high, target) in enumerate(parts):
            copies.append(pltpu.make_async_copy(piece.at[:, low:high], target, sems.at[n, t]))
    start(copies)
    wait(copies)


def put_columns(weights, keys, arrays):
    held = list(weights or [])
    count = len(arrays)
    return list(
        call(
            lambda *refs: columns_kernel(keys, *refs),
            [((8, 2, 64, 3072), bf16), ((8, 2, 64, 1024), bf16), ((8, 2, 256, 1024), bf16), ((8, 2, 64, 128), bf16)],
            list(arrays) + held,
            [ANY] * count + [VM] * len(held),
            scratch=[pltpu.SemaphoreType.DMA((len(keys), 3 + TAILS))],
            moved=count * 2**20,
            name="put_columns",
            aliases={count + n: n for n in range(len(held))},
        )
    )


def stack_kernel(*refs):
    pieces, out, sems = refs[:-2], refs[-2], refs[-1]
    copies = [pltpu.make_async_copy(piece, out.at[n], sems.at[n]) for n, piece in enumerate(pieces)]
    start(copies)
    wait(copies)


def stacked(pieces):
    return call(
        stack_kernel,
        [((len(pieces),) + pieces[0].shape, bf16)],
        pieces,
        [ANY] * len(pieces),
        scratch=[pltpu.SemaphoreType.DMA((len(pieces),))],
        moved=4 * 2**20,
        name="stacked",
    )[0]


def rows_kernel(keys, *refs):
    count = len(keys)
    pieces, (fc1, fc2), sems = refs[:count], refs[-3:-1], refs[-1]
    _, _, c, y = place()
    copies = []
    for n, (k, kind) in enumerate(keys):
        ck, yk = near(c, k, CS), places(y, c, YS)[kind]
        copies.append(pltpu.make_async_copy(pieces[n].at[:, 0:64], fc1.at[yk, :, ck], sems.at[n, 0]))
        target = fc2.at[:, ck, pl.ds(pl.multiple_of(yk * GROWS, 16), GROWS)]
        copies.append(pltpu.make_async_copy(pieces[n].at[:, 64 : 64 + GROWS], target, sems.at[n, 1]))
    start(copies)
    wait(copies)


def put_rows(fc1, fc2, pieces):
    keys = list(pieces)
    held = [fc1, fc2] if fc1 is not None else [fc2]
    count = len(keys)
    return call(
        lambda *refs: rows_kernel(keys, *refs),
        [((4, 8, 2, 64, 1024), bf16), ((8, 2, 256, 1024), bf16)],
        [pieces[key] for key in keys] + held,
        [ANY] * count + [VM] * len(held),
        scratch=[pltpu.SemaphoreType.DMA((count, 2))],
        moved=2 * count * 2**20,
        name="put_rows",
        aliases={count + n: 2 - len(held) + n for n in range(len(held))},
    )


def vectors_kernel(small, vec, bias):
    lane = lax.broadcasted_iota(jnp.int32, (16, 128), 1)
    for t in range(8):
        a = small[t, 0, 0:16].astype(f32)
        b = small[t, 1, 0:16].astype(f32)
        vec[:, t * 128 : t * 128 + 128] = jnp.where(lane < 64, a, pltpu.roll(b, 64, 1))
    for s in range(16):
        tail = small[s // 2, s % 2, 16:32].astype(f32)
        bias[0:1, s * 256 : s * 256 + 128] = tail[0:1]
        bias[0:1, s * 256 + 128 : s * 256 + 256] = tail[1:2]


def gathered_vectors(small):
    return call(
        vectors_kernel, [((16, 1024), f32), ((1, FF), f32)], [small], [VM], moved=2**20, name="gathered_vectors"
    )


def stacked_heads(pair, lane):
    zero = jnp.zeros_like(pair)
    return jnp.concatenate([jnp.where(lane, pair, zero), jnp.where(lane, zero, pair)], axis=0)


def attention_forward_kernel(keep, x_ref, vec, w_qkv, w_proj, *refs):
    if keep:
        received, x_out, a_out, p_out, soft_out, m_out, o_out, x1_out, c_out = refs
        x_out[...] = jnp.where(lax.axis_index("section") == 0, x_ref[...].astype(f32), received[...].astype(f32)).astype(bf16)
        x = x_out[...].astype(f32)
    else:
        x1_out, c_out, p_out, m_out = refs
        x = x_ref[...].astype(f32)
    hat, _ = stats(x)
    a = (hat * vec[0:1, :] + vec[1:2, :]).astype(bf16)
    if keep:
        a_out[...] = a
    for j in range(6):
        part = dot(a, w_qkv[:, :, :, j * 512 : j * 512 + 512].reshape(D, 512))
        if j < 2:
            part = part + vec[2:3, j * 512 : j * 512 + 512]
        if j >= 4:
            part = part + vec[3:4, j * 512 - 2048 : j * 512 - 1536]
        p_out[:, j * 512 : j * 512 + 512] = part.astype(bf16)
    lane = lax.broadcasted_iota(jnp.int32, (128, 128), 1) < 64

    def unit(u, _):
        i, h = lax.div(u, jnp.int32(8)), lax.rem(u, jnp.int32(8))
        rows = pl.ds(pl.multiple_of(i * 128, 128), 128)
        q, k, v = [p_out[rows, pl.ds(pl.multiple_of(h * 128 + o, 128), 128)] for o in (0, 1024, 2048)]
        s = dot(stacked_heads(q, lane), k, NT) * 0.125
        e = jnp.exp(s - jnp.max(s, axis=-1, keepdims=True))
        soft = (e / jnp.sum(e, axis=-1, keepdims=True)).astype(bf16)
        if keep:
            soft_out[u] = soft
        mixed = dot(soft, v)
        m_out[rows, pl.ds(pl.multiple_of(h * 128, 128), 128)] = jnp.where(lane, mixed[:128], mixed[128:]).astype(bf16)
        return 0

    lax.fori_loop(0, 16, unit, 0, unroll=16)
    o = dot(m_out[...], w_proj[...].reshape(D, D)) + vec[4:5, :]
    x1 = x + vec[5:6, :] * o
    if keep:
        o_out[...] = o.astype(bf16)
    x1_out[...] = x1
    hat, _ = stats(x1)
    c_out[...] = (hat * vec[6:7, :] + vec[7:8, :]).astype(bf16)


def attention_forward(keep, x, vec, weights, received=None):
    outs = [((T, D), f32), ((T, D), bf16)]
    scratch = []
    if keep:
        outs = [((T, D), bf16)] * 2 + [((T, 3072), bf16), ((16, 256, 128), bf16), ((T, D), bf16), ((T, D), bf16)] + outs
    else:
        scratch = [pltpu.VMEM((T, 3072), bf16), pltpu.VMEM((T, D), bf16)]
    return call(
        lambda *refs: attention_forward_kernel(keep, *refs),
        outs,
        [x, vec, weights[0], weights[1]] + ([received] if keep else []),
        [VM] * (5 if keep else 4),
        scratch=scratch,
        flops=2 * T * D * 4 * D,
        moved=14 * 2**20,
        name="attention_forward",
        limit=6,
    )


def fc1_tile(w1, t):
    return w1[t // 2, :, :, :, (t % 2) * 512 : (t % 2) * 512 + 512].reshape(D, 512)


def feed_forward_kernel(keep, x1_ref, c_ref, vec, bias, w1, w2, *refs):
    if keep:
        u_out, gp_out, f_out, y_out = refs
    else:
        (y_out,) = refs
    c = c_ref[...]
    total = None
    ahead = dot(c, fc1_tile(w1, 0))
    for t in range(8):
        cols = slice(t * 512, t * 512 + 512)
        h = ahead + bias[0:1, cols]
        if t < 7:
            ahead = dot(c, fc1_tile(w1, t + 1))
        cdf = 0.5 * (1.0 + lax.erf(h * 0.7071067811865476))
        u = (h * cdf).astype(bf16)
        if keep:
            gp = cdf + h * (jnp.exp(-0.5 * h * h) * 0.3989422804014327)
            u_out[:, cols] = u
            gp_out[:, cols] = gp.astype(bf16)
        part = dot(u, w2[t].reshape(512, D))
        total = part if total is None else total + part
    f = total + vec[8:9, :]
    if keep:
        f_out[...] = f.astype(bf16)
    y_out[...] = (x1_ref[...] + vec[9:10, :] * f).astype(y_out.dtype)


def feed_forward(keep, x1, c, vec, bias, weights):
    outs = [((T, D), f32 if keep else bf16)]
    if keep:
        outs = [((T, FF), bf16), ((T, FF), bf16), ((T, D), bf16)] + outs
    return call(
        lambda *refs: feed_forward_kernel(keep, *refs),
        outs,
        [x1, c, vec, bias, weights[2], weights[3]],
        [VM] * 6,
        flops=4 * T * D * FF,
        moved=24 * 2**20,
        name="feed_forward",
        limit=6,
    )


def upstream_kernel(first, counts, source, *refs):
    vec, g_out, df_out = refs[-3:]
    image = lax.axis_index("shard") * YS + lax.axis_index("replica")
    for m in range(2):
        rows = slice(m * 128, m * 128 + 128)
        g = source[rows, :].astype(f32) * jnp.where(image < counts[m], 1.0, 0.0)
        if not first:
            g = jnp.where(lax.axis_index("section") == 1, g, refs[0][rows, :].astype(f32))
        g_out[rows, :] = g
        df_out[rows, :] = (vec[9:10, :] * g).astype(bf16)


def upstream(counts, source, vec, received=None):
    extra = [] if received is None else [received]
    return call(
        lambda *refs: upstream_kernel(received is None, *refs),
        [((T, D), f32), ((T, D), bf16)],
        [counts, source] + extra + [vec],
        [SM] + [VM] * (2 + len(extra)),
        moved=2**20,
        name="upstream",
    )


def feed_backward_kernel(g_ref, df_ref, f_ref, gp_ref, x1_ref, o_ref, vec, w1, w2, dh_out, dx1_out, do_out, small):
    g = g_ref[...]
    df = df_ref[...]
    small[8:9, :] = jnp.sum(df.astype(f32), axis=0, keepdims=True)
    small[9:10, :] = jnp.sum(g * f_ref[...].astype(f32), axis=0, keepdims=True)
    small[0:4, :] = jnp.zeros((4, D), f32)
    small[14:16, :] = jnp.zeros((2, D), f32)
    total = None
    ahead = dot(df, w2[0].reshape(512, D), NT)
    for t in range(8):
        y, off = t // 2, (t % 2) * 512
        cols = slice(t * 512, t * 512 + 512)
        du = ahead
        if t < 7:
            ahead = dot(df, w2[t + 1].reshape(512, D), NT)
        dh = (gp_ref[:, cols].astype(f32) * du).astype(bf16)
        dh_out[:, cols] = dh
        small[10 + y : 11 + y, off : off + 512] = jnp.sum(dh.astype(f32), axis=0, keepdims=True)
        part = dot(dh, fc1_tile(w1, t), NT)
        total = part if total is None else total + part
    hat, scale = stats(x1_ref[...])
    d_norm, small[6:7, :], small[7:8, :] = norm_back(total, vec[6:7, :], hat, scale)
    dx1 = g + d_norm
    dx1_out[...] = dx1
    small[5:6, :] = jnp.sum(dx1 * o_ref[...].astype(f32), axis=0, keepdims=True)
    do = (vec[5:6, :] * dx1).astype(bf16)
    do_out[...] = do
    small[4:5, :] = jnp.sum(do.astype(f32), axis=0, keepdims=True)


def feed_backward(g, df, f, gp, x1, o, vec, weights):
    return call(
        feed_backward_kernel,
        [((T, FF), bf16), ((T, D), f32), ((T, D), bf16), ((16, D), f32)],
        [g, df, f, gp, x1, o, vec, weights[2], weights[3]],
        [VM] * 9,
        flops=4 * T * D * FF,
        moved=26 * 2**20,
        name="feed_backward",
        limit=6,
    )


def attention_backward_kernel(
    do_ref, dx1_ref, x_ref, p_ref, soft_ref, small_ref, vec, w_qkv, w_proj, *refs
):
    dp_out, dx_out, small, dm_ref = refs[-4:]
    dm_ref[...] = dot(do_ref[...], w_proj[...].reshape(D, D), NT).astype(bf16)
    lane = lax.broadcasted_iota(jnp.int32, (128, 128), 1) < 64

    def unit(u, _):
        i, h = lax.div(u, jnp.int32(8)), lax.rem(u, jnp.int32(8))
        rows = pl.ds(pl.multiple_of(i * 128, 128), 128)
        at = lambda o: pl.ds(pl.multiple_of(h * 128 + o, 128), 128)
        q, k, v = [p_ref[rows, at(o)] for o in (0, 1024, 2048)]
        dm = stacked_heads(dm_ref[rows, at(0)], lane)
        low = soft_ref[u]
        soft = low.astype(f32)
        dp_out[rows, at(2048)] = dot(low, dm, TN).astype(bf16)
        dw = dot(dm, v, NT)
        ds = (soft * (dw - jnp.sum(soft * dw, axis=-1, keepdims=True))).astype(bf16)
        dq = dot(ds, k) * 0.125
        dp_out[rows, at(0)] = jnp.where(lane, dq[:128], dq[128:]).astype(bf16)
        dp_out[rows, at(1024)] = (dot(ds, stacked_heads(q, lane), TN) * 0.125).astype(bf16)
        return 0

    lax.fori_loop(0, 16, unit, 0, unroll=16)
    small[2:3, :] = jnp.sum(dp_out[:, 0:1024].astype(f32), axis=0, keepdims=True)
    small[3:4, :] = jnp.sum(dp_out[:, 2048:3072].astype(f32), axis=0, keepdims=True)
    small[4:16, :] = small_ref[4:16, :]
    dp_out[:, 3072:4096] = do_ref[...]
    total = None
    for j in range(6):
        cols = slice(j * 512, j * 512 + 512)
        part = dot(dp_out[:, cols], w_qkv[:, :, :, cols].reshape(D, 512), NT)
        total = part if total is None else total + part
    hat, scale = stats(x_ref[...].astype(f32))
    d_norm, small[0:1, :], small[1:2, :] = norm_back(total, vec[0:1, :], hat, scale)
    dx = dx1_ref[...] + d_norm
    if len(refs) > 4:
        dx = jnp.where(lax.axis_index("section") == 0, dx, refs[0][...])
    dx_out[...] = dx.astype(dx_out.dtype)


def attention_backward(do, dx1, x, p, soft, small, vec, weights, output=None):
    extra = [] if output is None else [output]
    return call(
        attention_backward_kernel,
        [((T, 4096), bf16), ((T, D), f32 if extra else bf16), ((16, D), f32)],
        [do, dx1, x, p, soft, small, vec, weights[0], weights[1]] + extra,
        [VM] * (9 + len(extra)),
        scratch=[pltpu.VMEM((T, D), bf16)],
        flops=2 * T * D * 4 * D,
        moved=18 * 2**20,
        name="attention_backward",
        limit=6,
    )


def picked_kernel(a_ref, m_ref, c_ref, u_ref, mine, theirs):
    x, z, c, _ = place()
    row = lax.broadcasted_iota(jnp.int32, (512, D), 0)
    col = lax.broadcasted_iota(jnp.int32, (512, D), 1)
    eye_r = lax.broadcasted_iota(jnp.int32, (256, 256), 0)
    eye = jnp.where(eye_r == lax.broadcasted_iota(jnp.int32, (256, 256), 1), 1.0, 0.0).astype(bf16)
    kind, dz, inner = row >> 7, (row >> 6) & 1, row & 63
    for k, out in enumerate((mine, theirs)):
        ck = near(c, k, CS)
        step = 1 - 2 * ck
        there = jnp.where(kind == 0, 2, jnp.where(kind == 1, 4 - step, jnp.where(kind == 2, 4 + step, 0)))
        there = (((x + there) & 3) << 8) + (((z + dz) & 1) << 7) + inner + ck * 64
        chosen = jnp.where(col == there, 1.0, 0.0).astype(bf16)
        for n, ref in enumerate((a_ref, m_ref)):
            out[n * 512 : n * 512 + 512, :] = dot(chosen, ref[...], NT).astype(bf16)
        there = ((row >> 6) << 7) + inner + ck * 64
        chosen = jnp.where(col == there, 1.0, 0.0).astype(bf16)
        out[1024:1536, :] = dot(chosen, c_ref[...], NT).astype(bf16)
        for j in range(8):
            block = u_ref[:, pl.ds(pl.multiple_of((2 * j + ck) * 256, 256), 256)]
            turned = dot(eye, block, NT).astype(bf16)
            for k2 in range(YS):
                out[1536 + k2 * 512 + j * 64 : 1600 + k2 * 512 + j * 64, :] = turned[k2 * 64 : k2 * 64 + 64]


def picked(a, m, c, u):
    return call(
        picked_kernel,
        [((3584, T), bf16)] * 2,
        [a, m, c, u],
        [VM] * 4,
        flops=2 * 10**9,
        moved=8 * 2**20,
        name="transposed_acts",
    )


def fc2_grads_kernel(mine, theirs, df, df2, *outs):
    _, _, c, y = place()
    for n, yk in enumerate(places(y, c, YS)):
        rows = pl.ds(pl.multiple_of(1536 + yk * 512, 512), 512)
        grad = dot(mine[rows, :], df[...]) + dot(theirs[rows, :], df2[...])
        outs[n][...] = grad.astype(bf16).reshape(8, 64, 1024)


def fc1_grads_kernel(mine, theirs, dh, dh2, *outs):
    _, _, c, y = place()
    for n, yk in enumerate(places(y, c, YS)):
        cols = pl.ds(pl.multiple_of(yk * 1024, 1024), 1024)
        grad = dot(mine[1024:1536, :], dh[:, cols]) + dot(theirs[1024:1536, :], dh2[:, cols])
        outs[n][...] = grad.astype(bf16).reshape(8, 64, 1024)


def feed_grads(kernel, name, mine, theirs, given, given2):
    return call(
        kernel,
        [((8, 64, 1024), bf16)] * 4,
        [mine, theirs, given, given2],
        [VM] * 4,
        flops=4 * T * D * FF,
        moved=12 * 2**20,
        name=name,
    )


def attention_grads_kernel(mine, theirs, dp, dp2, small, small2, *refs):
    outs, total = refs[:4], refs[4]
    x, z, c, _ = place()
    total[...] = small[...] + small2[...]
    vec = total[...].astype(bf16)
    row = lax.broadcasted_iota(jnp.int32, (D, 128), 0)
    col = lax.broadcasted_iota(jnp.int32, (D, 128), 1)
    line = lax.broadcasted_iota(jnp.int32, (16, 128), 0)
    for n, x_there in enumerate(places(x, c, XS)):
        for dz in range(ZS):
            inner = near(z, dz, ZS) * 2 + c
            chosen = jnp.where((row == col + x_there * 256 + inner * 64) & (col < 64), 1.0, 0.0).astype(bf16)
            outs[n][dz, 32:64, 4096:4224] = jnp.zeros((32, 128), bf16)
            outs[n][dz, 0:16, 4096:4224] = dot(vec, chosen).astype(bf16)
            there = total[pl.ds(10 + x_there, 1), pl.ds(pl.multiple_of(inner * 256, 256), 256)]
            a, b = there[:, 0:128], there[:, 128:256]
            outs[n][dz, 16:32, 4096:4224] = jnp.where(line == 0, a, jnp.where(line == 1, b, 0.0)).astype(bf16)
    for t in range(8):
        low = 0 if t < 6 else 512
        cols = slice(t * 512, t * 512 + 512)
        grad = dot(mine[low : low + 512, :], dp[:, cols]) + dot(theirs[low : low + 512, :], dp2[:, cols])
        grad = grad.astype(bf16)
        for n in range(4):
            outs[n][:, :, cols] = grad[n * 128 : n * 128 + 128].reshape(2, 64, 512)


def attention_grads(mine, theirs, dp, dp2, small, small2):
    return call(
        attention_grads_kernel,
        [((2, 64, QP), bf16)] * 4,
        [mine, theirs, dp, dp2, small, small2],
        [VM] * 6,
        scratch=[pltpu.VMEM((16, D), f32)],
        flops=8 * T * D * 2 * D,
        moved=16 * 2**20,
        name="attention_grads",
    )


def sum_kernel(count, axis, *refs):
    total = refs[0][...].astype(f32)
    for ref in refs[1:count]:
        total = total + ref[...].astype(f32)
    outs = refs[count:]
    if axis == "add":
        outs[0][...] = jnp.sum(total, axis=0).astype(bf16)
    elif axis == "split":
        for n, out in enumerate(outs):
            out[...] = total[n].astype(bf16)
    elif axis == "quarters":
        outs, held = outs[:4], outs[4]
        held[...] = total
        _, _, _, y = place()
        for dy, out in enumerate(outs):
            out[...] = held[pl.ds(pl.multiple_of(near(y, dy, YS) * 16, 16), 16), :].astype(bf16)
    else:
        outs[0][...] = total.astype(bf16)


def summed(parts, axis=None):
    shape = parts[0].shape
    scratch = []
    if axis == "split":
        outs = [(shape[1:], bf16)] * shape[0]
    elif axis == "quarters":
        outs = [((16,) + shape[1:], bf16)] * 4
        scratch = [pltpu.VMEM(shape, f32)]
    else:
        outs = [(shape[1:] if axis else shape, bf16)]
    size = 1
    for n in shape:
        size *= n
    out = call(
        lambda *refs: sum_kernel(len(parts), axis, *refs),
        outs,
        parts,
        [VM] * len(parts),
        scratch=scratch,
        flops=size * len(parts),
        moved=2 * size * (len(parts) + 1),
        name="summed",
    )
    return out if len(outs) > 1 else out[0]


def gathered_copies(parts, target, sems):
    y = place()[3]
    copies = [pltpu.make_async_copy(part, target.at[near(y, dy, YS)], sems.at[dy]) for dy, part in enumerate(parts)]
    start(copies)
    return copies


def fc1_results_kernel(a, b, c, d, out, held, sems):
    wait(gathered_copies((a, b, c, d), held, sems))
    for k in range(YS):
        out[:, k * 1024 : k * 1024 + 1024] = held[k].astype(f32)


def fc2_results_kernel(a, b, c, d, out, held, sems):
    wait(gathered_copies((a, b, c, d), held, sems))
    for k in range(YS):
        out[k * 64 : k * 64 + 64, :] = held[k].astype(f32)


def column_results_kernel(a, b, c, d, qkv, proj, vec, bias, held, sems):
    wait(gathered_copies((a, b, c, d), held, sems))
    for k in range(YS):
        line = slice(k * 16, k * 16 + 16)
        qkv[line, :] = held[k, :, 0:3072].astype(f32)
        proj[line, :] = held[k, :, 3072:4096].astype(f32)
    vec[...] = held[0, 0:10, 4096:4160].astype(f32)
    tail = held[1, 0:16, 4096:4224].astype(f32)
    bias[:, 0:128] = tail[0:1]
    bias[:, 128:256] = tail[1:2]


def results(kernel, shapes, parts, name):
    return call(
        kernel,
        [(shape, f32) for shape in shapes],
        parts,
        [ANY] * 4,
        scratch=[pltpu.VMEM((4,) + parts[0].shape, bf16), pltpu.SemaphoreType.DMA((4,))],
        moved=10 * 2**20,
        name=name,
    )


def twin(value, name="twin"):
    with jax.named_scope(name):
        return from_shard(value, dc=1)


def around(value, name):
    with jax.named_scope(name):
        return [value] + [from_replica(value, dy) for dy in range(1, YS)]


def swap(value, name):
    groups = [[shard_of(x, z, c) for x in range(XS) for z in range(ZS)] for c in range(CS)]
    with jax.named_scope(name):
        return lax.all_to_all(value, "shard", split_axis=0, concat_axis=0, axis_index_groups=groups, tiled=True)


def gather(w_qkv, w_proj, w_fc1, w_fc2, vectors, fc1_bias):
    hold = lax.optimization_barrier
    here = swap(own_pieces(w_fc1, w_fc2), "here")
    unit = own_unit(w_qkv, w_proj, w_fc2, vectors, fc1_bias)
    twin_unit = twin(unit, "twin_unit")
    unit, here, twin_unit = hold((unit, here, twin_unit))
    behind, twin_here = onward(here, "y", "behind"), twin(here, "twin_here")
    other = from_shard(unit, dz=1, name="other")
    plus, minus = from_shard(unit, dx=1, name="plus"), from_shard(unit, dx=3, name="minus")
    behind, twin_here, other, plus, minus = hold((behind, twin_here, other, plus, minus))
    twin_behind = onward(twin_here, "y", "twin_behind")
    minus_other, plus_other = from_shard(other, dx=3, name="minus_other"), from_shard(plus, dz=1, name="plus_other")
    far = from_shard(plus, dx=1, name="far")
    first = stacked([other, plus, minus])
    twins = twin(first, "twin_first")
    weights = put_columns(None, [(0, 0, 0, 0, None), (1, 0, 0, 1, None)], [unit, twin_unit])
    fc1, weights[2] = put_rows(None, weights[2], {(0, 3): here, (1, 3): twin_here})
    held = hold((twin_behind, minus_other, plus_other, far, first, twins, fc1, weights))
    twin_behind, minus_other, plus_other, far, first, twins, fc1, weights = held
    opposite = onward(behind, "y", "opposite")
    far_other = from_shard(far, dz=1, name="far_other")
    ahead, twin_ahead = twin(twin_behind, "ahead"), twin(behind, "twin_ahead")
    second = stacked([minus_other, plus_other, far])
    second_twins = twin(second, "twin_second")
    order = [(0, 1), (1, 0), (3, 0)]
    weights = put_columns(weights, [(k, dx, dz, k, n) for k in range(2) for n, (dx, dz) in enumerate(order)], [first, twins])
    fc1, weights[2] = put_rows(fc1, weights[2], {(0, 1): behind, (1, 1): twin_behind})
    held = hold((opposite, far_other, ahead, twin_ahead, second, second_twins, fc1, weights))
    opposite, far_other, ahead, twin_ahead, second, second_twins, fc1, weights = held
    twin_opposite, twin_far_other = twin(opposite, "twin_opposite"), twin(far_other, "twin_far_other")
    order = [(3, 1), (1, 1), (2, 0)]
    keys = [(k, dx, dz, k, n) for k in range(2) for n, (dx, dz) in enumerate(order)]
    weights = put_columns(weights, keys, [second, second_twins])
    fc1, weights[2] = put_rows(fc1, weights[2], {(0, 2): ahead, (1, 2): twin_ahead})
    weights = put_columns(weights, [(0, 2, 1, 0, None), (1, 2, 1, 1, None)], [far_other, twin_far_other])
    fc1, weights[2] = put_rows(fc1, weights[2], {(0, 0): opposite, (1, 0): twin_opposite})
    vec, bias = gathered_vectors(weights[3])
    return (weights[0], weights[1], fc1, weights[2]), vec, bias


def shards(edge_inputs, image_counts, w_qkv, w_proj, w_fc1, w_fc2, vectors, fc1_bias):
    source = edge_inputs[0, :, 0].reshape(T, D)
    weights, vec, bias = gather(w_qkv[0], w_proj[0], w_fc1[0], w_fc2[0], vectors[0], fc1_bias)

    x1, c = attention_forward(False, source, vec, weights)
    (first_out,) = feed_forward(False, x1, c, vec, bias, weights)
    received = passed_along(first_out, 1)
    inputs, a, p, soft, m, o, x1, c = attention_forward(True, source, vec, weights, received)
    u, gp, f, output = feed_forward(True, x1, c, vec, bias, weights)

    g, df = upstream(image_counts, source, vec)
    _, dx1, do, small = feed_backward(g, df, f, gp, x1, o, vec, weights)
    _, dx, _ = attention_backward(do, dx1, inputs, p, soft, small, vec, weights)
    received_grad = passed_along(dx, -1)
    mine, theirs = picked(a, m, c, u)
    received_grad, mine, theirs = lax.optimization_barrier((received_grad, mine, twin(theirs)))

    hold = lax.optimization_barrier
    g, df = upstream(image_counts, source, vec, received_grad)
    opposite, behind, ahead_2, here_2 = feed_grads(fc2_grads_kernel, "fc2_grads", mine, theirs, df, twin(df, "twin_df"))
    far_2, given_2 = onward(opposite, "y", "far_2"), onward(twin(behind, "behind_2"), "y", "given_2")
    g = after(g, opposite)
    dh, dx1, do, small = feed_backward(g, df, f, gp, x1, o, vec, weights)
    dh2 = twin(dh, "twin_dh")
    dp, edge, small = attention_backward(do, dx1, inputs, p, soft, small, vec, weights, output)
    dh, dh2, dp, far_2 = hold((dh, dh2, dp, far_2))
    dp2, small2 = twin(dp, "twin_dp"), twin(small, "twin_small")
    ahead_2 = summed([ahead_2, far_2])
    own_2 = onward(ahead_2, "y", "own_2")
    parts_1 = feed_grads(fc1_grads_kernel, "fc1_grads", mine, theirs, after(dh, ahead_2), dh2)
    opposite, behind, ahead_1, here_1 = parts_1
    far_1, given_1 = onward(opposite, "y", "far_1"), onward(twin(behind, "behind_1"), "y", "given_1")
    parts_c = attention_grads(mine, theirs, after(dp, here_1), dp2, small, small2)
    opposite, behind, ahead_c, here_c = parts_c
    far_c, given_c = onward(opposite, "x", "far_c"), onward(twin(behind, "behind_c"), "x", "given_c")

    ahead_c = summed([ahead_c, far_c])
    own_c = onward(ahead_c, "x", "own_c")
    sum_2 = summed([after(here_2, ahead_c), own_2, twin(given_2, "twin_given_2")])
    got_2 = swap(sum_2, "swap_2")
    ahead_1 = summed([after(ahead_1, sum_2), far_1])
    own_1 = onward(ahead_1, "y", "own_1")
    fc2 = summed([after(got_2, ahead_1)], "add")
    same, other = summed([after(here_c, fc2), own_c, twin(given_c, "twin_given_c")], "split")
    fc2 = around(fc2, "around_fc2")
    with jax.named_scope("other_z"):
        other = from_shard(other, dz=1)
    quarters = summed([same, other], "quarters")
    with jax.named_scope("quarters"):
        quarters = [quarters[0]] + [from_replica(quarters[dy], YS - dy) for dy in range(1, YS)]
    sum_1 = summed([after(here_1, quarters[0]), own_1, twin(given_1, "twin_given_1")])
    got_1 = swap(sum_1, "swap_1")
    quarters[0] = after(quarters[0], sum_1)
    column = around(summed(quarters), "around_c")
    fc1 = around(summed([got_1], "add"), "around_fc1")
    (g_fc2,) = results(fc2_results_kernel, [(256, D)], fc2, "fc2_results")
    g_qkv, g_proj, g_vec, g_bias = results(
        column_results_kernel, [(64, 3072), (64, 1024), (10, 64), (1, 256)], column, "column_results"
    )
    (g_fc1,) = results(fc1_results_kernel, [(64, FF)], fc1, "fc1_results")
    return (
        edge.reshape(1, 2, 1, 128, D),
        g_qkv[None],
        g_proj[None],
        g_fc1[None],
        g_fc2[None],
        g_vec[None],
        g_bias,
    )


def solution(mesh):
    placed = (
        P("section", None, ("shard", "replica"), None, None),
        P(),
        P("section", "shard", None),
        P("section", "shard", None),
        P("section", "shard", None),
        P("section", "shard", None),
        P("section", None, "shard"),
        P("section", "shard"),
    )
    return jax.shard_map(
        shards,
        mesh=mesh,
        in_specs=placed,
        out_specs=(placed[0],) + placed[2:],
        check_vma=False,
    )
```

```python
import jax
import jax.numpy as jnp
from jax import lax
from jax.experimental import pallas as pl
from jax.experimental.pallas import tpu as pltpu
from jax.sharding import PartitionSpec as P

XS, ZS, CS, YS = 4, 2, 2, 4
T = 256
D, FF = 1024, 4096
GROWS = 32
TAILS = 4 - GROWS // 16
UNIT = 4096 + 1024 * TAILS + 128
QP = 4224
LIMIT = 8
HEAVY = ('attention_backward', 'attention_input_grad', 'transposed_acts')
epsilon = 1e-06
bf16, f32 = jnp.bfloat16, jnp.float32
ANY = pl.BlockSpec(memory_space=pl.ANY)
HB = pl.BlockSpec(memory_space=pltpu.HBM)
VM = pl.BlockSpec(memory_space=pltpu.VMEM)
SM = pl.BlockSpec(memory_space=pltpu.SMEM)
NT = (((1,), (1,)), ((), ()))
TN = (((0,), (0,)), ((), ()))


def shard_of(x, z, c):
    return (x % XS) * 4 + (z % ZS) * 2 + (c % CS)


def from_shard(value, dx=0, dz=0, dc=0, name="from_shard"):
    pairs = [
        (shard_of(x + dx, z + dz, c + dc), shard_of(x, z, c))
        for x in range(XS)
        for z in range(ZS)
        for c in range(CS)
    ]
    with jax.named_scope(name):
        return lax.ppermute(value, "shard", pairs)


def from_replica(value, dy):
    return lax.ppermute(value, "replica", [((y + dy) % YS, y) for y in range(YS)])


def onward(value, axis, name="onward", way=1):
    pairs = []
    for x in range(XS):
        for z in range(ZS):
            for c in range(CS):
                for y in range(YS):
                    step = way * (1 - 2 * c)
                    tx, ty = (x + step, y) if axis == "x" else (x, y + step)
                    pairs.append((shard_of(x, z, c) * YS + y, shard_of(tx, z, c) * YS + ty % YS))
    with jax.named_scope(name):
        return lax.ppermute(value, ("shard", "replica"), pairs)


def passed_along(value, steps):
    return lax.ppermute(value, "section", [(0, 1)] if steps == 1 else [(1, 0)])


def place():
    shard = lax.axis_index("shard")
    x = lax.div(shard, jnp.int32(4))
    z = lax.rem(lax.div(shard, jnp.int32(2)), jnp.int32(2))
    c = lax.rem(shard, jnp.int32(2))
    return x, z, c, lax.axis_index("replica")


def near(base, step, size):
    return lax.rem(base + jnp.int32(step), jnp.int32(size))


def call(kernel, outs, args, kinds, scratch=(), flops=0, moved=0, out_kinds=None, name=None, aliases=None, limit=LIMIT):
    return pl.pallas_call(
        kernel,
        out_shape=[jax.ShapeDtypeStruct(s, d) for s, d in outs],
        in_specs=list(kinds),
        out_specs=list(out_kinds or [VM] * len(outs)),
        scratch_shapes=list(scratch),
        compiler_params=pltpu.CompilerParams(vmem_limit_bytes=limit * 2**20),
        cost_estimate=pl.CostEstimate(flops=3 * 10**10 if name in HEAVY else 1, bytes_accessed=1, transcendentals=0),
        name=name,
        input_output_aliases=aliases or {},
    )(*args)


def after(values, token):
    return lax.optimization_barrier((values, token))[0]


def dot(a, b, dims=(((1,), (0,)), ((), ()))):
    return lax.dot_general(a, b, dims, preferred_element_type=f32)


def stats(values):
    average = jnp.mean(values, axis=-1, keepdims=True)
    centered = values - average
    spread = jnp.mean(centered * centered, axis=-1, keepdims=True)
    scale = lax.rsqrt(spread + epsilon)
    return centered * scale, scale


def norm_back(grad, gain, hat, scale):
    d_hat = grad * gain
    d_in = scale * (
        d_hat - jnp.mean(d_hat, axis=-1, keepdims=True) - hat * jnp.mean(d_hat * hat, axis=-1, keepdims=True)
    )
    return d_in, jnp.sum(grad * hat, axis=0, keepdims=True), jnp.sum(grad, axis=0, keepdims=True)


def places(base, c, size):
    step = 1 - 2 * c
    return [near(base + 4, d, size) for d in (2, -step, step, 0)]


def pieces_kernel(fc1, fc2, pieces, sems):
    _, _, _, y = place()
    block = fc1.at[:, pl.ds(pl.multiple_of(y * 1024, 1024), 1024)]
    rows = fc2.at[pl.ds(pl.multiple_of(y * GROWS, 16), GROWS)]
    copies = []
    for n in range(8):
        copies.append(pltpu.make_async_copy(block, pieces.at[n, 0:64], sems.at[2 * n]))
        copies.append(pltpu.make_async_copy(rows, pieces.at[n, 64 : 64 + GROWS], sems.at[2 * n + 1]))
    start(copies)
    wait(copies)


def own_pieces(w_fc1, w_fc2):
    return call(
        pieces_kernel,
        [((8, 64 + GROWS, 1024), bf16)],
        (w_fc1, w_fc2),
        [HB] * 2,
        scratch=[pltpu.SemaphoreType.DMA((16,))],
        moved=4 * 2**20,
        name="own_pieces",
        limit=56,
    )[0]


def unit_kernel(qkv, proj, fc2, vectors, bias, unit, small, sems):
    copies = [pltpu.make_async_copy(qkv, unit.at[:, 0:3072], sems.at[0])]
    copies.append(pltpu.make_async_copy(proj, unit.at[:, 3072:4096], sems.at[1]))
    for n in range(TAILS):
        row, col = 4 * GROWS + 64 * n, 4096 + 1024 * n
        copies.append(
            pltpu.make_async_copy(fc2.at[row : row + 64], unit.at[:, col : col + 1024], sems.at[2 + n])
        )
    start(copies)
    small[...] = jnp.zeros_like(small)
    small[0:10, 0:64] = vectors[...].astype(f32)
    small[16:17, :] = bias[:, 0:128].astype(f32)
    small[17:18, :] = bias[:, 128:256].astype(f32)
    wait(copies)
    unit[:, UNIT - 128 : UNIT] = small[...].astype(bf16)


def own_unit(w_qkv, w_proj, w_fc2, vectors, fc1_bias):
    return call(
        unit_kernel,
        [((64, UNIT), bf16)],
        (w_qkv, w_proj, w_fc2, vectors, fc1_bias),
        [HB] * 3 + [VM] * 2,
        scratch=[pltpu.VMEM((64, 128), f32), pltpu.SemaphoreType.DMA((2 + TAILS,))],
        moved=4 * 2**20,
        name="own_unit",
        limit=56,
    )[0]


def start(copies):
    for copy in copies:
        copy.start()


def wait(copies):
    for copy in copies:
        copy.wait()


def columns_kernel(keys, *refs):
    pieces, (qkv, proj, fc2, small), sems = refs, refs[-5:-1], refs[-1]
    x, z, c, _ = place()
    copies = []
    for n, (k, dx, dz, array, row) in enumerate(keys):
        piece = pieces[array] if row is None else pieces[array].at[row]
        xz, ck = near(x, dx, XS) * 2 + near(z, dz, ZS), near(c, k, CS)
        parts = [(0, 3072, qkv.at[xz, ck]), (3072, 4096, proj.at[xz, ck]), (UNIT - 128, UNIT, small.at[xz, ck])]
        for t in range(TAILS):
            first, col = 4 * GROWS + 64 * t, 4096 + 1024 * t
            parts.append((col, col + 1024, fc2.at[xz, ck, first : first + 64]))
        for t, (low, high, target) in enumerate(parts):
            copies.append(pltpu.make_async_copy(piece.at[:, low:high], target, sems.at[n, t]))
    start(copies)
    wait(copies)


def put_columns(weights, keys, arrays):
    held = list(weights or [])
    count = len(arrays)
    return list(
        call(
            lambda *refs: columns_kernel(keys, *refs),
            [((8, 2, 64, 3072), bf16), ((8, 2, 64, 1024), bf16), ((8, 2, 256, 1024), bf16), ((8, 2, 64, 128), bf16)],
            list(arrays) + held,
            [ANY] * count + [VM] * len(held),
            scratch=[pltpu.SemaphoreType.DMA((len(keys), 3 + TAILS))],
            moved=count * 2**20,
            name="put_columns",
            aliases={count + n: n for n in range(len(held))},
        )
    )


def stack_kernel(*refs):
    pieces, out, sems = refs[:-2], refs[-2], refs[-1]
    copies = [pltpu.make_async_copy(piece, out.at[n], sems.at[n]) for n, piece in enumerate(pieces)]
    start(copies)
    wait(copies)


def stacked(pieces):
    return call(
        stack_kernel,
        [((len(pieces),) + pieces[0].shape, bf16)],
        pieces,
        [ANY] * len(pieces),
        scratch=[pltpu.SemaphoreType.DMA((len(pieces),))],
        moved=4 * 2**20,
        name="stacked",
    )[0]


def rows_kernel(keys, *refs):
    count = len(keys)
    pieces, (fc1, fc2), sems = refs[:count], refs[-3:-1], refs[-1]
    _, _, c, y = place()
    copies = []
    for n, (k, kind) in enumerate(keys):
        ck, yk = near(c, k, CS), places(y, c, YS)[kind]
        copies.append(pltpu.make_async_copy(pieces[n].at[:, 0:64], fc1.at[yk, :, ck], sems.at[n, 0]))
        target = fc2.at[:, ck, pl.ds(pl.multiple_of(yk * GROWS, 16), GROWS)]
        copies.append(pltpu.make_async_copy(pieces[n].at[:, 64 : 64 + GROWS], target, sems.at[n, 1]))
    start(copies)
    wait(copies)


def put_rows(fc1, fc2, pieces):
    keys = list(pieces)
    held = [fc1, fc2] if fc1 is not None else [fc2]
    count = len(keys)
    return call(
        lambda *refs: rows_kernel(keys, *refs),
        [((4, 8, 2, 64, 1024), bf16), ((8, 2, 256, 1024), bf16)],
        [pieces[key] for key in keys] + held,
        [ANY] * count + [VM] * len(held),
        scratch=[pltpu.SemaphoreType.DMA((count, 2))],
        moved=2 * count * 2**20,
        name="put_rows",
        aliases={count + n: 2 - len(held) + n for n in range(len(held))},
    )


def vectors_kernel(small, vec, bias):
    lane = lax.broadcasted_iota(jnp.int32, (16, 128), 1)
    for t in range(8):
        a = small[t, 0, 0:16].astype(f32)
        b = small[t, 1, 0:16].astype(f32)
        vec[:, t * 128 : t * 128 + 128] = jnp.where(lane < 64, a, pltpu.roll(b, 64, 1))
    for s in range(16):
        tail = small[s // 2, s % 2, 16:32].astype(f32)
        bias[0:1, s * 256 : s * 256 + 128] = tail[0:1]
        bias[0:1, s * 256 + 128 : s * 256 + 256] = tail[1:2]


def gathered_vectors(small):
    return call(
        vectors_kernel, [((16, 1024), f32), ((1, FF), f32)], [small], [VM], moved=2**20, name="gathered_vectors"
    )


def stacked_heads(pair, lane):
    zero = jnp.zeros_like(pair)
    return jnp.concatenate([jnp.where(lane, pair, zero), jnp.where(lane, zero, pair)], axis=0)


def attention_forward_kernel(keep, x_ref, vec, w_qkv, w_proj, *refs):
    if keep:
        received, x_out, a_out, p_out, soft_out, m_out, o_out, x1_out, c_out = refs
        x_out[...] = jnp.where(lax.axis_index("section") == 0, x_ref[...].astype(f32), received[...].astype(f32)).astype(bf16)
        x = x_out[...].astype(f32)
    else:
        x1_out, c_out, p_out, m_out = refs
        x = x_ref[...].astype(f32)
    hat, _ = stats(x)
    a = (hat * vec[0:1, :] + vec[1:2, :]).astype(bf16)
    if keep:
        a_out[...] = a
    for j in range(6):
        part = dot(a, w_qkv[:, :, :, j * 512 : j * 512 + 512].reshape(D, 512))
        if j < 2:
            part = part + vec[2:3, j * 512 : j * 512 + 512]
        if j >= 4:
            part = part + vec[3:4, j * 512 - 2048 : j * 512 - 1536]
        p_out[:, j * 512 : j * 512 + 512] = part.astype(bf16)
    lane = lax.broadcasted_iota(jnp.int32, (128, 128), 1) < 64

    def unit(u, _):
        i, h = lax.div(u, jnp.int32(8)), lax.rem(u, jnp.int32(8))
        rows = pl.ds(pl.multiple_of(i * 128, 128), 128)
        q, k, v = [p_out[rows, pl.ds(pl.multiple_of(h * 128 + o, 128), 128)] for o in (0, 1024, 2048)]
        s = dot(stacked_heads(q, lane), k, NT) * 0.125
        e = jnp.exp(s - jnp.max(s, axis=-1, keepdims=True))
        soft = (e / jnp.sum(e, axis=-1, keepdims=True)).astype(bf16)
        if keep:
            soft_out[u] = soft
        mixed = dot(soft, v)
        m_out[rows, pl.ds(pl.multiple_of(h * 128, 128), 128)] = jnp.where(lane, mixed[:128], mixed[128:]).astype(bf16)
        return 0

    lax.fori_loop(0, 16, unit, 0, unroll=16)
    o = dot(m_out[...], w_proj[...].reshape(D, D)) + vec[4:5, :]
    x1 = x + vec[5:6, :] * o
    if keep:
        o_out[...] = o.astype(bf16)
    x1_out[...] = x1
    hat, _ = stats(x1)
    c_out[...] = (hat * vec[6:7, :] + vec[7:8, :]).astype(bf16)


def attention_forward(keep, x, vec, weights, received=None):
    outs = [((T, D), f32), ((T, D), bf16)]
    scratch = []
    if keep:
        outs = [((T, D), bf16)] * 2 + [((T, 3072), bf16), ((16, 256, 128), bf16), ((T, D), bf16), ((T, D), bf16)] + outs
    else:
        scratch = [pltpu.VMEM((T, 3072), bf16), pltpu.VMEM((T, D), bf16)]
    return call(
        lambda *refs: attention_forward_kernel(keep, *refs),
        outs,
        [x, vec, weights[0], weights[1]] + ([received] if keep else []),
        [VM] * (5 if keep else 4),
        scratch=scratch,
        flops=2 * T * D * 4 * D,
        moved=14 * 2**20,
        name="attention_forward",
        limit=6,
    )


def fc1_tile(w1, t):
    return w1[t // 2, :, :, :, (t % 2) * 512 : (t % 2) * 512 + 512].reshape(D, 512)


def feed_forward_kernel(keep, x1_ref, c_ref, vec, bias, w1, w2, *refs):
    if keep:
        u_out, gp_out, f_out, y_out = refs
    else:
        (y_out,) = refs
    c = c_ref[...]
    total = None
    ahead = dot(c, fc1_tile(w1, 0))
    for t in range(8):
        cols = slice(t * 512, t * 512 + 512)
        h = ahead + bias[0:1, cols]
        if t < 7:
            ahead = dot(c, fc1_tile(w1, t + 1))
        cdf = 0.5 * (1.0 + lax.erf(h * 0.7071067811865476))
        u = (h * cdf).astype(bf16)
        if keep:
            gp = cdf + h * (jnp.exp(-0.5 * h * h) * 0.3989422804014327)
            u_out[:, cols] = u
            gp_out[:, cols] = gp.astype(bf16)
        part = dot(u, w2[t].reshape(512, D))
        total = part if total is None else total + part
    f = total + vec[8:9, :]
    if keep:
        f_out[...] = f.astype(bf16)
    y_out[...] = (x1_ref[...] + vec[9:10, :] * f).astype(y_out.dtype)


def feed_forward(keep, x1, c, vec, bias, weights):
    outs = [((T, D), f32 if keep else bf16)]
    if keep:
        outs = [((T, FF), bf16), ((T, FF), bf16), ((T, D), bf16)] + outs
    return call(
        lambda *refs: feed_forward_kernel(keep, *refs),
        outs,
        [x1, c, vec, bias, weights[2], weights[3]],
        [VM] * 6,
        flops=4 * T * D * FF,
        moved=24 * 2**20,
        name="feed_forward",
        limit=6,
    )


def upstream_kernel(first, counts, source, *refs):
    vec, g_out, df_out = refs[-3:]
    image = lax.axis_index("shard") * YS + lax.axis_index("replica")
    for m in range(2):
        rows = slice(m * 128, m * 128 + 128)
        g = source[rows, :].astype(f32) * jnp.where(image < counts[m], 1.0, 0.0)
        if not first:
            g = jnp.where(lax.axis_index("section") == 1, g, refs[m][...].astype(f32))
        g_out[rows, :] = g
        df_out[rows, :] = (vec[9:10, :] * g).astype(bf16)


def upstream(counts, source, vec, received=None):
    extra = [] if received is None else list(received)
    return call(
        lambda *refs: upstream_kernel(received is None, *refs),
        [((T, D), f32), ((T, D), bf16)],
        [counts, source] + extra + [vec],
        [SM] + [VM] * (2 + len(extra)),
        moved=2**20,
        name="upstream",
    )


def feed_backward_kernel(keep, g_ref, df_ref, f_ref, gp_ref, x1_ref, o_ref, vec, w1, w2, dx1_out, do_out, *refs):
    g = g_ref[...]
    df = df_ref[...]
    if keep:
        dh_out, small = refs
        small[8:9, :] = jnp.sum(df.astype(f32), axis=0, keepdims=True)
        small[9:10, :] = jnp.sum(g * f_ref[...].astype(f32), axis=0, keepdims=True)
        small[0:4, :] = jnp.zeros((4, D), f32)
        small[14:16, :] = jnp.zeros((2, D), f32)
    total = None
    ahead = dot(df, w2[0].reshape(512, D), NT)
    for t in range(8):
        y, off = t // 2, (t % 2) * 512
        cols = slice(t * 512, t * 512 + 512)
        du = ahead
        if t < 7:
            ahead = dot(df, w2[t + 1].reshape(512, D), NT)
        dh = (gp_ref[:, cols].astype(f32) * du).astype(bf16)
        if keep:
            dh_out[:, cols] = dh
            small[10 + y : 11 + y, off : off + 512] = jnp.sum(dh.astype(f32), axis=0, keepdims=True)
        part = dot(dh, fc1_tile(w1, t), NT)
        total = part if total is None else total + part
    hat, scale = stats(x1_ref[...])
    d_norm, d_gain, d_shift = norm_back(total, vec[6:7, :], hat, scale)
    dx1 = g + d_norm
    dx1_out[...] = dx1
    do = (vec[5:6, :] * dx1).astype(bf16)
    do_out[...] = do
    if keep:
        small[4:5, :] = jnp.sum(do.astype(f32), axis=0, keepdims=True)
        small[5:6, :] = jnp.sum(dx1 * o_ref[...].astype(f32), axis=0, keepdims=True)
        small[6:7, :] = d_gain
        small[7:8, :] = d_shift


def feed_backward(keep, g, df, f, gp, x1, o, vec, weights):
    outs = [((T, D), f32), ((T, D), bf16)]
    if keep:
        outs += [((T, FF), bf16), ((16, D), f32)]
    return call(
        lambda *refs: feed_backward_kernel(keep, *refs),
        outs,
        [g, df, f, gp, x1, o, vec, weights[2], weights[3]],
        [VM] * 9,
        flops=4 * T * D * FF,
        moved=26 * 2**20,
        name="feed_backward",
        limit=6,
    )


def attention_backward_kernel(
    do_ref, dx1_ref, x_ref, p_ref, soft_ref, small_ref, vec, w_qkv, w_proj, *refs
):
    dp_out, dx_out, small, dm_ref = refs[-4:]
    dm_ref[...] = dot(do_ref[...], w_proj[...].reshape(D, D), NT).astype(bf16)
    lane = lax.broadcasted_iota(jnp.int32, (128, 128), 1) < 64

    def unit(u, _):
        i, h = lax.div(u, jnp.int32(8)), lax.rem(u, jnp.int32(8))
        rows = pl.ds(pl.multiple_of(i * 128, 128), 128)
        at = lambda o: pl.ds(pl.multiple_of(h * 128 + o, 128), 128)
        q, k, v = [p_ref[rows, at(o)] for o in (0, 1024, 2048)]
        dm = stacked_heads(dm_ref[rows, at(0)], lane)
        low = soft_ref[u]
        soft = low.astype(f32)
        dp_out[rows, at(2048)] = dot(low, dm, TN).astype(bf16)
        dw = dot(dm, v, NT)
        ds = (soft * (dw - jnp.sum(soft * dw, axis=-1, keepdims=True))).astype(bf16)
        dq = dot(ds, k) * 0.125
        dp_out[rows, at(0)] = jnp.where(lane, dq[:128], dq[128:]).astype(bf16)
        dp_out[rows, at(1024)] = (dot(ds, stacked_heads(q, lane), TN) * 0.125).astype(bf16)
        return 0

    lax.fori_loop(0, 16, unit, 0, unroll=16)
    small[2:3, :] = jnp.sum(dp_out[:, 0:1024].astype(f32), axis=0, keepdims=True)
    small[3:4, :] = jnp.sum(dp_out[:, 2048:3072].astype(f32), axis=0, keepdims=True)
    small[4:16, :] = small_ref[4:16, :]
    dp_out[:, 3072:4096] = do_ref[...]
    total = None
    for j in range(6):
        cols = slice(j * 512, j * 512 + 512)
        part = dot(dp_out[:, cols], w_qkv[:, :, :, cols].reshape(D, 512), NT)
        total = part if total is None else total + part
    hat, scale = stats(x_ref[...].astype(f32))
    d_norm, small[0:1, :], small[1:2, :] = norm_back(total, vec[0:1, :], hat, scale)
    dx = dx1_ref[...] + d_norm
    if len(refs) > 4:
        dx = jnp.where(lax.axis_index("section") == 0, dx, refs[0][...])
    dx_out[...] = dx.astype(dx_out.dtype)


def attention_input_grad_kernel(image, do_ref, dx1_ref, x_ref, p_ref, soft_ref, vec, w_qkv, w_proj, dx_out, dm_ref, dp_ref):
    rows = slice(image * 128, image * 128 + 128)
    dm_ref[...] = dot(do_ref[rows, :], w_proj[...].reshape(D, D), NT).astype(bf16)
    lane = lax.broadcasted_iota(jnp.int32, (128, 128), 1) < 64

    def unit(h, _):
        at = lambda o: pl.ds(pl.multiple_of(h * 128 + o, 128), 128)
        q, k, v = [p_ref[rows, at(o)] for o in (0, 1024, 2048)]
        dm = stacked_heads(dm_ref[:, at(0)], lane)
        low = soft_ref[image * 8 + h]
        soft = low.astype(f32)
        dp_ref[:, at(2048)] = dot(low, dm, TN).astype(bf16)
        dw = dot(dm, v, NT)
        ds = (soft * (dw - jnp.sum(soft * dw, axis=-1, keepdims=True))).astype(bf16)
        dq = dot(ds, k) * 0.125
        dp_ref[:, at(0)] = jnp.where(lane, dq[:128], dq[128:]).astype(bf16)
        dp_ref[:, at(1024)] = (dot(ds, stacked_heads(q, lane), TN) * 0.125).astype(bf16)
        return 0

    lax.fori_loop(0, 8, unit, 0, unroll=8)
    total = None
    for j in range(6):
        cols = slice(j * 512, j * 512 + 512)
        part = dot(dp_ref[:, cols], w_qkv[:, :, :, cols].reshape(D, 512), NT)
        total = part if total is None else total + part
    hat, scale = stats(x_ref[rows, :].astype(f32))
    d_norm, _, _ = norm_back(total, vec[0:1, :], hat, scale)
    dx_out[...] = (dx1_ref[rows, :] + d_norm).astype(bf16)


def attention_input_grad(image, do, dx1, x, p, soft, vec, weights):
    return call(
        lambda *refs: attention_input_grad_kernel(image, *refs),
        [((128, D), bf16)],
        [do, dx1, x, p, soft, vec, weights[0], weights[1]],
        [VM] * 8,
        scratch=[pltpu.VMEM((128, D), bf16), pltpu.VMEM((128, 3072), bf16)],
        flops=T * D * 4 * D,
        moved=10 * 2**20,
        name="attention_input_grad",
        limit=6,
    )[0]


def attention_backward(do, dx1, x, p, soft, small, vec, weights, output=None):
    extra = [] if output is None else [output]
    return call(
        attention_backward_kernel,
        [((T, 4096), bf16), ((T, D), f32 if extra else bf16), ((16, D), f32)],
        [do, dx1, x, p, soft, small, vec, weights[0], weights[1]] + extra,
        [VM] * (9 + len(extra)),
        scratch=[pltpu.VMEM((T, D), bf16)],
        flops=2 * T * D * 4 * D,
        moved=18 * 2**20,
        name="attention_backward",
        limit=6,
    )


def picked_kernel(a_ref, m_ref, c_ref, u_ref, mine, theirs):
    x, z, c, _ = place()
    row = lax.broadcasted_iota(jnp.int32, (512, D), 0)
    col = lax.broadcasted_iota(jnp.int32, (512, D), 1)
    eye_r = lax.broadcasted_iota(jnp.int32, (256, 256), 0)
    eye = jnp.where(eye_r == lax.broadcasted_iota(jnp.int32, (256, 256), 1), 1.0, 0.0).astype(bf16)
    kind, dz, inner = row >> 7, (row >> 6) & 1, row & 63
    for k, out in enumerate((mine, theirs)):
        ck = near(c, k, CS)
        step = 1 - 2 * ck
        there = jnp.where(kind == 0, 2, jnp.where(kind == 1, 4 - step, jnp.where(kind == 2, 4 + step, 0)))
        there = (((x + there) & 3) << 8) + (((z + dz) & 1) << 7) + inner + ck * 64
        chosen = jnp.where(col == there, 1.0, 0.0).astype(bf16)
        for n, ref in enumerate((a_ref, m_ref)):
            out[n * 512 : n * 512 + 512, :] = dot(chosen, ref[...], NT).astype(bf16)
        there = ((row >> 6) << 7) + inner + ck * 64
        chosen = jnp.where(col == there, 1.0, 0.0).astype(bf16)
        out[1024:1536, :] = dot(chosen, c_ref[...], NT).astype(bf16)
        for j in range(8):
            chip = near(x, j % 4, XS) * 2 + near(z, j // 4, ZS)
            block = u_ref[:, pl.ds(pl.multiple_of((2 * chip + ck) * 256, 256), 256)]
            turned = dot(eye, block, NT).astype(bf16)
            for k2 in range(YS):
                out[1536 + k2 * 512 + j * 64 : 1600 + k2 * 512 + j * 64, :] = turned[k2 * 64 : k2 * 64 + 64]


def picked(a, m, c, u):
    return call(
        picked_kernel,
        [((3584, T), bf16)] * 2,
        [a, m, c, u],
        [VM] * 4,
        flops=2 * 10**9,
        moved=8 * 2**20,
        name="transposed_acts",
    )


def fc2_grads_kernel(mine, theirs, df, df2, *outs):
    _, _, c, y = place()
    for n, yk in enumerate(places(y, c, YS)):
        rows = pl.ds(pl.multiple_of(1536 + yk * 512, 512), 512)
        grad = dot(mine[rows, :], df[...]) + dot(theirs[rows, :], df2[...])
        outs[n][...] = grad.astype(bf16).reshape(8, 64, 1024)


def fc1_grads_kernel(mine, theirs, dh, dh2, *outs):
    _, _, c, y = place()
    for n, yk in enumerate(places(y, c, YS)):
        cols = pl.ds(pl.multiple_of(yk * 1024, 1024), 1024)
        grad = dot(mine[1024:1536, :], dh[:, cols]) + dot(theirs[1024:1536, :], dh2[:, cols])
        outs[n][...] = grad.astype(bf16).reshape(8, 64, 1024)


def feed_grads(kernel, name, mine, theirs, given, given2):
    return call(
        kernel,
        [((8, 64, 1024), bf16)] * 4,
        [mine, theirs, given, given2],
        [VM] * 4,
        flops=4 * T * D * FF,
        moved=12 * 2**20,
        name=name,
    )


def attention_grads_kernel(mine, theirs, dp, dp2, small, small2, *refs):
    outs, total = refs[:4], refs[4]
    x, z, c, _ = place()
    total[...] = small[...] + small2[...]
    vec = total[...].astype(bf16)
    row = lax.broadcasted_iota(jnp.int32, (D, 128), 0)
    col = lax.broadcasted_iota(jnp.int32, (D, 128), 1)
    line = lax.broadcasted_iota(jnp.int32, (16, 128), 0)
    for n, x_there in enumerate(places(x, c, XS)):
        for dz in range(ZS):
            inner = near(z, dz, ZS) * 2 + c
            chosen = jnp.where((row == col + x_there * 256 + inner * 64) & (col < 64), 1.0, 0.0).astype(bf16)
            outs[n][dz, 32:64, 4096:4224] = jnp.zeros((32, 128), bf16)
            outs[n][dz, 0:16, 4096:4224] = dot(vec, chosen).astype(bf16)
            there = total[pl.ds(10 + x_there, 1), pl.ds(pl.multiple_of(inner * 256, 256), 256)]
            a, b = there[:, 0:128], there[:, 128:256]
            outs[n][dz, 16:32, 4096:4224] = jnp.where(line == 0, a, jnp.where(line == 1, b, 0.0)).astype(bf16)
    for t in range(8):
        low = 0 if t < 6 else 512
        cols = slice(t * 512, t * 512 + 512)
        grad = dot(mine[low : low + 512, :], dp[:, cols]) + dot(theirs[low : low + 512, :], dp2[:, cols])
        grad = grad.astype(bf16)
        for n in range(4):
            outs[n][:, :, cols] = grad[n * 128 : n * 128 + 128].reshape(2, 64, 512)


def attention_grads(mine, theirs, dp, dp2, small, small2):
    return call(
        attention_grads_kernel,
        [((2, 64, QP), bf16)] * 4,
        [mine, theirs, dp, dp2, small, small2],
        [VM] * 6,
        scratch=[pltpu.VMEM((16, D), f32)],
        flops=8 * T * D * 2 * D,
        moved=16 * 2**20,
        name="attention_grads",
    )


def sum_kernel(count, axis, *refs):
    total = refs[0][...].astype(f32)
    for ref in refs[1:count]:
        total = total + ref[...].astype(f32)
    outs = refs[count:]
    if axis == "add":
        outs[0][...] = jnp.sum(total, axis=0).astype(bf16)
    elif axis == "split":
        for n, out in enumerate(outs):
            out[...] = total[n].astype(bf16)
    elif axis == "halves":
        count = total.shape[0] // 2
        outs[0][...] = total[:count].astype(bf16)
        outs[1][...] = total[count:].astype(bf16)
    elif axis == "quarters":
        outs, held = outs[:4], outs[4]
        held[...] = total
        _, _, _, y = place()
        for dy, out in enumerate(outs):
            out[...] = held[pl.ds(pl.multiple_of(near(y, dy, YS) * 16, 16), 16), :].astype(bf16)
    else:
        outs[0][...] = total.astype(bf16)


def summed(parts, axis=None):
    shape = parts[0].shape
    scratch = []
    if axis == "split":
        outs = [(shape[1:], bf16)] * shape[0]
    elif axis == "halves":
        outs = [((shape[0] // 2,) + shape[1:], bf16)] * 2
    elif axis == "quarters":
        outs = [((16,) + shape[1:], bf16)] * 4
        scratch = [pltpu.VMEM(shape, f32)]
    else:
        outs = [(shape[1:] if axis else shape, bf16)]
    size = 1
    for n in shape:
        size *= n
    out = call(
        lambda *refs: sum_kernel(len(parts), axis, *refs),
        outs,
        parts,
        [VM] * len(parts),
        scratch=scratch,
        flops=size * len(parts),
        moved=2 * size * (len(parts) + 1),
        name="summed",
    )
    return out if len(outs) > 1 else out[0]


def gathered_copies(parts, target, sems):
    y = place()[3]
    copies = [pltpu.make_async_copy(part, target.at[near(y, dy, YS)], sems.at[dy]) for dy, part in enumerate(parts)]
    start(copies)
    return copies


def fc1_results_kernel(a, b, c, d, out, held, sems):
    wait(gathered_copies((a, b, c, d), held, sems))
    for k in range(YS):
        out[:, k * 1024 : k * 1024 + 1024] = held[k].astype(f32)


def fc2_results_kernel(a, b, c, d, out, held, sems):
    wait(gathered_copies((a, b, c, d), held, sems))
    for k in range(YS):
        out[k * 64 : k * 64 + 64, :] = held[k].astype(f32)


def column_results_kernel(a, b, c, d, qkv, proj, vec, bias, held, sems):
    wait(gathered_copies((a, b, c, d), held, sems))
    for k in range(YS):
        line = slice(k * 16, k * 16 + 16)
        qkv[line, :] = held[k, :, 0:3072].astype(f32)
        proj[line, :] = held[k, :, 3072:4096].astype(f32)
    vec[...] = held[0, 0:10, 4096:4160].astype(f32)
    tail = held[1, 0:16, 4096:4224].astype(f32)
    bias[:, 0:128] = tail[0:1]
    bias[:, 128:256] = tail[1:2]


def results(kernel, shapes, parts, name):
    return call(
        kernel,
        [(shape, f32) for shape in shapes],
        parts,
        [ANY] * 4,
        scratch=[pltpu.VMEM((4,) + parts[0].shape, bf16), pltpu.SemaphoreType.DMA((4,))],
        moved=10 * 2**20,
        name=name,
    )


def twin(value, name="twin"):
    with jax.named_scope(name):
        return from_shard(value, dc=1)


def around(value, name):
    with jax.named_scope(name):
        return [value] + [from_replica(value, dy) for dy in range(1, YS)]


def swap(value, name):
    groups = [[shard_of(x, z, c) for x in range(XS) for z in range(ZS)] for c in range(CS)]
    with jax.named_scope(name):
        return lax.all_to_all(value, "shard", split_axis=0, concat_axis=0, axis_index_groups=groups, tiled=True)


def gather(w_qkv, w_proj, w_fc1, w_fc2, vectors, fc1_bias):
    hold = lax.optimization_barrier
    here = swap(own_pieces(w_fc1, w_fc2), "here")
    unit = own_unit(w_qkv, w_proj, w_fc2, vectors, fc1_bias)
    twin_unit = twin(unit, "twin_unit")
    unit, here, twin_unit = hold((unit, here, twin_unit))
    behind, twin_here = onward(here, "y", "behind"), twin(here, "twin_here")
    other = from_shard(unit, dz=1, name="other")
    plus, minus = from_shard(unit, dx=1, name="plus"), from_shard(unit, dx=3, name="minus")
    behind, twin_here, other, plus, minus = hold((behind, twin_here, other, plus, minus))
    twin_behind = onward(twin_here, "y", "twin_behind")
    minus_other, plus_other = from_shard(other, dx=3, name="minus_other"), from_shard(plus, dz=1, name="plus_other")
    far = from_shard(plus, dx=1, name="far")
    first = stacked([other, plus, minus])
    twins = twin(first, "twin_first")
    weights = put_columns(None, [(0, 0, 0, 0, None), (1, 0, 0, 1, None)], [unit, twin_unit])
    fc1, weights[2] = put_rows(None, weights[2], {(0, 3): here, (1, 3): twin_here})
    held = hold((twin_behind, minus_other, plus_other, far, first, twins, fc1, weights))
    twin_behind, minus_other, plus_other, far, first, twins, fc1, weights = held
    opposite = onward(behind, "y", "opposite")
    far_other = from_shard(far, dz=1, name="far_other")
    ahead, twin_ahead = twin(twin_behind, "ahead"), twin(behind, "twin_ahead")
    second = stacked([minus_other, plus_other, far])
    second_twins = twin(second, "twin_second")
    order = [(0, 1), (1, 0), (3, 0)]
    weights = put_columns(weights, [(k, dx, dz, k, n) for k in range(2) for n, (dx, dz) in enumerate(order)], [first, twins])
    fc1, weights[2] = put_rows(fc1, weights[2], {(0, 1): behind, (1, 1): twin_behind})
    held = hold((opposite, far_other, ahead, twin_ahead, second, second_twins, fc1, weights))
    opposite, far_other, ahead, twin_ahead, second, second_twins, fc1, weights = held
    twin_opposite, twin_far_other = twin(opposite, "twin_opposite"), twin(far_other, "twin_far_other")
    order = [(3, 1), (1, 1), (2, 0)]
    keys = [(k, dx, dz, k, n) for k in range(2) for n, (dx, dz) in enumerate(order)]
    weights = put_columns(weights, keys, [second, second_twins])
    fc1, weights[2] = put_rows(fc1, weights[2], {(0, 2): ahead, (1, 2): twin_ahead})
    weights = put_columns(weights, [(0, 2, 1, 0, None), (1, 2, 1, 1, None)], [far_other, twin_far_other])
    fc1, weights[2] = put_rows(fc1, weights[2], {(0, 0): opposite, (1, 0): twin_opposite})
    vec, bias = gathered_vectors(weights[3])
    return (weights[0], weights[1], fc1, weights[2]), vec, bias


def shards(edge_inputs, image_counts, w_qkv, w_proj, w_fc1, w_fc2, vectors, fc1_bias):
    source = edge_inputs[0, :, 0].reshape(T, D)
    weights, vec, bias = gather(w_qkv[0], w_proj[0], w_fc1[0], w_fc2[0], vectors[0], fc1_bias)

    x1, c = attention_forward(False, source, vec, weights)
    (first_out,) = feed_forward(False, x1, c, vec, bias, weights)
    received = passed_along(first_out, 1)
    inputs, a, p, soft, m, o, x1, c = attention_forward(True, source, vec, weights, received)
    u, gp, f, output = feed_forward(True, x1, c, vec, bias, weights)

    g, df = upstream(image_counts, source, vec)
    dx1, do = feed_backward(False, g, df, f, gp, x1, o, vec, weights)
    halves = [attention_input_grad(m, do, dx1, inputs, p, soft, vec, weights) for m in range(2)]
    received_grad = [passed_along(half, -1) for half in halves]
    mine, theirs = picked(after(a, halves[1]), m, c, u)
    received_grad, mine, theirs = lax.optimization_barrier((received_grad, mine, twin(theirs)))

    hold = lax.optimization_barrier
    g, df = upstream(image_counts, source, vec, received_grad)
    parts_2 = feed_grads(fc2_grads_kernel, "fc2_grads", mine, theirs, df, twin(df, "twin_df"))
    far_2 = onward(parts_2[0], "y", "far_2")
    g = after(g, parts_2[0])
    dx1, do, dh, small = feed_backward(True, g, df, f, gp, x1, o, vec, weights)
    dh2 = twin(dh, "twin_dh")
    dp, edge, small = attention_backward(do, dx1, inputs, p, soft, small, vec, weights, output)
    dh, dh2, dp, far_2 = hold((dh, dh2, dp, far_2))
    dp2, small2 = twin(dp, "twin_dp"), twin(small, "twin_small")
    relay_2 = summed([parts_2[2], far_2])
    own_2, given_2 = onward(relay_2, "y", "own_2"), onward(after(parts_2[1], relay_2), "y", "given_2", -1)
    parts_1 = feed_grads(fc1_grads_kernel, "fc1_grads", mine, theirs, after(dh, relay_2), dh2)
    parts_c = attention_grads(mine, theirs, after(dp, parts_1[3]), dp2, small, small2)
    far_c, given_c = onward(parts_c[0], "x", "far_c"), onward(parts_c[1], "x", "given_c", -1)
    parts_1, own_2, given_2, last = hold((parts_1, own_2, given_2, parts_c[3]))
    far_1, given_1 = onward(parts_1[0], "y", "far_1"), onward(parts_1[1], "y", "given_1", -1)

    same_2, other_2 = summed([parts_2[3], own_2, given_2], "halves")
    with jax.named_scope("other_2"):
        other_2 = from_shard(other_2, dz=1)
    far_c, given_c = hold((far_c, given_c))
    relay_c = summed([after(parts_c[2], same_2), far_c])
    own_c = onward(relay_c, "x", "own_c")
    along = summed([after(same_2, relay_c), other_2], "split")
    with jax.named_scope("along_2"):
        along = [along[0]] + [from_shard(along[dx], dx=XS - dx) for dx in range(1, XS)]
    far_1, given_1 = hold((far_1, given_1))
    relay_1 = summed([after(parts_1[2], along[0]), far_1])
    own_1 = onward(relay_1, "y", "own_1")
    same, other = summed([after(last, relay_1), own_c, given_c], "split")
    fc2 = summed([after(along[0], same)] + along[1:])
    with jax.named_scope("other_z"):
        other = from_shard(other, dz=1)
    quarters = summed([after(same, fc2), other], "quarters")
    sum_1 = summed([after(parts_1[3], quarters[0]), own_1, given_1])
    with jax.named_scope("quarters"):
        quarters = [quarters[0]] + [from_replica(quarters[dy], YS - dy) for dy in range(1, YS)]
    fc2 = around(fc2, "around_fc2")
    got_1 = swap(sum_1, "swap_1")
    column = around(summed(quarters), "around_c")
    fc1 = around(summed([got_1], "add"), "around_fc1")
    (g_fc2,) = results(fc2_results_kernel, [(256, D)], fc2, "fc2_results")
    g_qkv, g_proj, g_vec, g_bias = results(
        column_results_kernel, [(64, 3072), (64, 1024), (10, 64), (1, 256)], column, "column_results"
    )
    (g_fc1,) = results(fc1_results_kernel, [(64, FF)], fc1, "fc1_results")
    return (
        edge.reshape(1, 2, 1, 128, D),
        g_qkv[None],
        g_proj[None],
        g_fc1[None],
        g_fc2[None],
        g_vec[None],
        g_bias,
    )


def solution(mesh):
    placed = (
        P("section", None, ("shard", "replica"), None, None),
        P(),
        P("section", "shard", None),
        P("section", "shard", None),
        P("section", "shard", None),
        P("section", "shard", None),
        P("section", None, "shard"),
        P("section", "shard"),
    )
    return jax.shard_map(
        shards,
        mesh=mesh,
        in_specs=placed,
        out_specs=(placed[0],) + placed[2:],
        check_vma=False,
    )
```

```python
import jax
import jax.numpy as jnp
from jax import lax
from jax.experimental import pallas as pl
from jax.experimental.pallas import tpu as pltpu
from jax.sharding import PartitionSpec as P

XS, ZS, CS, YS = 4, 2, 2, 4
T = 256
D, FF = 1024, 4096
GROWS = 32
TAILS = 4 - GROWS // 16
UNIT = 4096 + 1024 * TAILS + 128
QP = 4224
LIMIT = 8
HEAVY = ('first_attention', 'attention_backward', 'attention_input_grad', 'transposed_acts')
epsilon = 1e-06
bf16, f32 = jnp.bfloat16, jnp.float32
ANY = pl.BlockSpec(memory_space=pl.ANY)
HB = pl.BlockSpec(memory_space=pltpu.HBM)
VM = pl.BlockSpec(memory_space=pltpu.VMEM)
SM = pl.BlockSpec(memory_space=pltpu.SMEM)
NT = (((1,), (1,)), ((), ()))
TN = (((0,), (0,)), ((), ()))


def shard_of(x, z, c):
    return (x % XS) * 4 + (z % ZS) * 2 + (c % CS)


def from_shard(value, dx=0, dz=0, dc=0, name="from_shard"):
    pairs = [
        (shard_of(x + dx, z + dz, c + dc), shard_of(x, z, c))
        for x in range(XS)
        for z in range(ZS)
        for c in range(CS)
    ]
    with jax.named_scope(name):
        return lax.ppermute(value, "shard", pairs)


def from_replica(value, dy):
    return lax.ppermute(value, "replica", [((y + dy) % YS, y) for y in range(YS)])


def onward(value, axis, name="onward", way=1):
    pairs = []
    for x in range(XS):
        for z in range(ZS):
            for c in range(CS):
                for y in range(YS):
                    step = way * (1 - 2 * c)
                    tx, ty = (x + step, y) if axis == "x" else (x, y + step)
                    pairs.append((shard_of(x, z, c) * YS + y, shard_of(tx, z, c) * YS + ty % YS))
    with jax.named_scope(name):
        return lax.ppermute(value, ("shard", "replica"), pairs)


def passed_along(value, steps):
    return lax.ppermute(value, "section", [(0, 1)] if steps == 1 else [(1, 0)])


def place():
    shard = lax.axis_index("shard")
    x = lax.div(shard, jnp.int32(4))
    z = lax.rem(lax.div(shard, jnp.int32(2)), jnp.int32(2))
    c = lax.rem(shard, jnp.int32(2))
    return x, z, c, lax.axis_index("replica")


def near(base, step, size):
    return lax.rem(base + jnp.int32(step), jnp.int32(size))


def call(kernel, outs, args, kinds, scratch=(), flops=0, moved=0, out_kinds=None, name=None, aliases=None, limit=LIMIT):
    return pl.pallas_call(
        kernel,
        out_shape=[jax.ShapeDtypeStruct(s, d) for s, d in outs],
        in_specs=list(kinds),
        out_specs=list(out_kinds or [VM] * len(outs)),
        scratch_shapes=list(scratch),
        compiler_params=pltpu.CompilerParams(vmem_limit_bytes=limit * 2**20),
        cost_estimate=pl.CostEstimate(flops=3 * 10**10 if name in HEAVY else 1, bytes_accessed=1, transcendentals=0),
        name=name,
        input_output_aliases=aliases or {},
    )(*args)


def after(values, token):
    return lax.optimization_barrier((values, token))[0]


def dot(a, b, dims=(((1,), (0,)), ((), ()))):
    return lax.dot_general(a, b, dims, preferred_element_type=f32)


def stats(values):
    average = jnp.mean(values, axis=-1, keepdims=True)
    centered = values - average
    spread = jnp.mean(centered * centered, axis=-1, keepdims=True)
    scale = lax.rsqrt(spread + epsilon)
    return centered * scale, scale


def norm_back(grad, gain, hat, scale):
    d_hat = grad * gain
    d_in = scale * (
        d_hat - jnp.mean(d_hat, axis=-1, keepdims=True) - hat * jnp.mean(d_hat * hat, axis=-1, keepdims=True)
    )
    return d_in, jnp.sum(grad * hat, axis=0, keepdims=True), jnp.sum(grad, axis=0, keepdims=True)


def places(base, c, size):
    step = 1 - 2 * c
    return [near(base + 4, d, size) for d in (2, -step, step, 0)]


def pieces_kernel(fc1, fc2, pieces, sems):
    _, _, _, y = place()
    block = fc1.at[:, pl.ds(pl.multiple_of(y * 1024, 1024), 1024)]
    rows = fc2.at[pl.ds(pl.multiple_of(y * GROWS, 16), GROWS)]
    copies = []
    for n in range(8):
        copies.append(pltpu.make_async_copy(block, pieces.at[n, 0:64], sems.at[2 * n]))
        copies.append(pltpu.make_async_copy(rows, pieces.at[n, 64 : 64 + GROWS], sems.at[2 * n + 1]))
    start(copies)
    wait(copies)


def own_pieces(w_fc1, w_fc2):
    return call(
        pieces_kernel,
        [((8, 64 + GROWS, 1024), bf16)],
        (w_fc1, w_fc2),
        [HB] * 2,
        scratch=[pltpu.SemaphoreType.DMA((16,))],
        moved=4 * 2**20,
        name="own_pieces",
        limit=56,
    )[0]


def unit_kernel(qkv, proj, fc2, vectors, bias, unit, small, sems):
    copies = [pltpu.make_async_copy(qkv, unit.at[:, 0:3072], sems.at[0])]
    copies.append(pltpu.make_async_copy(proj, unit.at[:, 3072:4096], sems.at[1]))
    for n in range(TAILS):
        row, col = 4 * GROWS + 64 * n, QP + 1024 * n
        copies.append(
            pltpu.make_async_copy(fc2.at[row : row + 64], unit.at[:, col : col + 1024], sems.at[2 + n])
        )
    start(copies)
    small[...] = jnp.zeros_like(small)
    small[0:10, 0:64] = vectors[...].astype(f32)
    small[16:17, :] = bias[:, 0:128].astype(f32)
    small[17:18, :] = bias[:, 128:256].astype(f32)
    wait(copies)
    unit[:, 4096:QP] = small[...].astype(bf16)


def own_unit(w_qkv, w_proj, w_fc2, vectors, fc1_bias):
    return call(
        unit_kernel,
        [((64, UNIT), bf16)],
        (w_qkv, w_proj, w_fc2, vectors, fc1_bias),
        [HB] * 3 + [VM] * 2,
        scratch=[pltpu.VMEM((64, 128), f32), pltpu.SemaphoreType.DMA((2 + TAILS,))],
        moved=4 * 2**20,
        name="own_unit",
        limit=56,
    )[0]


def start(copies):
    for copy in copies:
        copy.start()


def wait(copies):
    for copy in copies:
        copy.wait()


def columns_kernel(keys, *refs):
    pieces, (qkv, proj, fc2, small), sems = refs, refs[-5:-1], refs[-1]
    x, z, c, _ = place()
    copies = []
    for n, (k, dx, dz, array, row) in enumerate(keys):
        piece = pieces[array] if row is None else pieces[array].at[row]
        width = piece.shape[-1]
        xz, ck = near(x, dx, XS) * 2 + near(z, dz, ZS), near(c, k, CS)
        parts = []
        if width != UNIT - QP:
            parts = [(0, 3072, qkv.at[xz, ck]), (3072, 4096, proj.at[xz, ck]), (4096, QP, small.at[xz, ck])]
        if width != QP:
            for t in range(TAILS):
                first, col = 4 * GROWS + 64 * t, width - 1024 * (TAILS - t)
                parts.append((col, col + 1024, fc2.at[xz, ck, first : first + 64]))
        for t, (low, high, target) in enumerate(parts):
            copies.append(pltpu.make_async_copy(piece.at[:, low:high], target, sems.at[n, t]))
    start(copies)
    wait(copies)


def put_columns(weights, keys, arrays):
    held = list(weights or [])
    count = len(arrays)
    return list(
        call(
            lambda *refs: columns_kernel(keys, *refs),
            [((8, 2, 64, 3072), bf16), ((8, 2, 64, 1024), bf16), ((8, 2, 256, 1024), bf16), ((8, 2, 64, 128), bf16)],
            list(arrays) + held,
            [ANY] * count + [VM] * len(held),
            scratch=[pltpu.SemaphoreType.DMA((len(keys), 3 + TAILS))],
            moved=count * 2**20,
            name="put_columns",
            aliases={count + n: n for n in range(len(held))},
        )
    )


def rest_kernel(mine, other, held, fc2, sems):
    x, z, c, _ = place()
    xz = near(x, 2, XS) * 2 + near(z, 1, ZS)
    copies = []
    for k, piece in enumerate((mine, other)):
        for t in range(TAILS):
            first = 4 * GROWS + 64 * t
            target = fc2.at[xz, near(c, k, CS), first : first + 64]
            copies.append(pltpu.make_async_copy(piece.at[:, 1024 * t : 1024 * t + 1024], target, sems.at[k, t]))
    start(copies)
    wait(copies)


def put_rest(fc2, mine, other):
    return call(
        rest_kernel,
        [((8, 2, 256, 1024), bf16)],
        [mine, other, fc2],
        [ANY, ANY, VM],
        scratch=[pltpu.SemaphoreType.DMA((2, TAILS))],
        moved=2**20,
        name="put_rest",
        aliases={2: 0},
    )[0]


def parted_kernel(a, b, first, rest, sems):
    copies = [pltpu.make_async_copy(a.at[:, 0:QP], first, sems.at[0])]
    copies.append(pltpu.make_async_copy(b.at[:, QP:UNIT], rest, sems.at[1]))
    start(copies)
    wait(copies)


def parted(a, b):
    return call(
        parted_kernel,
        [((64, QP), bf16), ((64, UNIT - QP), bf16)],
        [a, b],
        [ANY] * 2,
        scratch=[pltpu.SemaphoreType.DMA((2,))],
        moved=2**20,
        name="parted",
    )


def stack_kernel(*refs):
    pieces, out, sems = refs[:-2], refs[-2], refs[-1]
    copies = [pltpu.make_async_copy(piece, out.at[n], sems.at[n]) for n, piece in enumerate(pieces)]
    start(copies)
    wait(copies)


def stacked(pieces):
    return call(
        stack_kernel,
        [((len(pieces),) + pieces[0].shape, bf16)],
        pieces,
        [ANY] * len(pieces),
        scratch=[pltpu.SemaphoreType.DMA((len(pieces),))],
        moved=4 * 2**20,
        name="stacked",
    )[0]


def rows_kernel(keys, *refs):
    count = len(keys)
    pieces, (fc1, fc2), sems = refs[:count], refs[-3:-1], refs[-1]
    _, _, c, y = place()
    copies = []
    for n, (k, kind) in enumerate(keys):
        ck, yk = near(c, k, CS), places(y, c, YS)[kind]
        copies.append(pltpu.make_async_copy(pieces[n].at[:, 0:64], fc1.at[yk, :, ck], sems.at[n, 0]))
        target = fc2.at[:, ck, pl.ds(pl.multiple_of(yk * GROWS, 16), GROWS)]
        copies.append(pltpu.make_async_copy(pieces[n].at[:, 64 : 64 + GROWS], target, sems.at[n, 1]))
    start(copies)
    wait(copies)


def put_rows(fc1, fc2, pieces):
    keys = list(pieces)
    held = [fc1, fc2] if fc1 is not None else [fc2]
    count = len(keys)
    return call(
        lambda *refs: rows_kernel(keys, *refs),
        [((4, 8, 2, 64, 1024), bf16), ((8, 2, 256, 1024), bf16)],
        [pieces[key] for key in keys] + held,
        [ANY] * count + [VM] * len(held),
        scratch=[pltpu.SemaphoreType.DMA((count, 2))],
        moved=2 * count * 2**20,
        name="put_rows",
        aliases={count + n: 2 - len(held) + n for n in range(len(held))},
    )


def vectors_kernel(small, vec, bias):
    lane = lax.broadcasted_iota(jnp.int32, (16, 128), 1)
    for t in range(8):
        a = small[t, 0, 0:16].astype(f32)
        b = small[t, 1, 0:16].astype(f32)
        vec[:, t * 128 : t * 128 + 128] = jnp.where(lane < 64, a, pltpu.roll(b, 64, 1))
    for s in range(16):
        tail = small[s // 2, s % 2, 16:32].astype(f32)
        bias[0:1, s * 256 : s * 256 + 128] = tail[0:1]
        bias[0:1, s * 256 + 128 : s * 256 + 256] = tail[1:2]


def gathered_vectors(small):
    return call(
        vectors_kernel, [((16, 1024), f32), ((1, FF), f32)], [small], [VM], moved=2**20, name="gathered_vectors"
    )


def stacked_heads(pair, lane):
    zero = jnp.zeros_like(pair)
    return jnp.concatenate([jnp.where(lane, pair, zero), jnp.where(lane, zero, pair)], axis=0)


def attention_forward_kernel(keep, x_ref, vec, w_qkv, w_proj, *refs):
    if keep:
        received, x_out, a_out, p_out, soft_out, m_out, o_out, x1_out, c_out = refs
        x_out[...] = jnp.where(lax.axis_index("section") == 0, x_ref[...].astype(f32), received[...].astype(f32)).astype(bf16)
        x = x_out[...].astype(f32)
    else:
        x1_out, c_out, p_out, m_out = refs
        x = x_ref[...].astype(f32)
    hat, _ = stats(x)
    a = (hat * vec[0:1, :] + vec[1:2, :]).astype(bf16)
    if keep:
        a_out[...] = a
    for j in range(6):
        part = dot(a, w_qkv[:, :, :, j * 512 : j * 512 + 512].reshape(D, 512))
        if j < 2:
            part = part + vec[2:3, j * 512 : j * 512 + 512]
        if j >= 4:
            part = part + vec[3:4, j * 512 - 2048 : j * 512 - 1536]
        p_out[:, j * 512 : j * 512 + 512] = part.astype(bf16)
    lane = lax.broadcasted_iota(jnp.int32, (128, 128), 1) < 64

    def unit(u, _):
        i, h = lax.div(u, jnp.int32(8)), lax.rem(u, jnp.int32(8))
        rows = pl.ds(pl.multiple_of(i * 128, 128), 128)
        q, k, v = [p_out[rows, pl.ds(pl.multiple_of(h * 128 + o, 128), 128)] for o in (0, 1024, 2048)]
        s = dot(stacked_heads(q, lane), k, NT) * 0.125
        e = jnp.exp(s - jnp.max(s, axis=-1, keepdims=True))
        soft = (e / jnp.sum(e, axis=-1, keepdims=True)).astype(bf16)
        if keep:
            soft_out[u] = soft
        mixed = dot(soft, v)
        m_out[rows, pl.ds(pl.multiple_of(h * 128, 128), 128)] = jnp.where(lane, mixed[:128], mixed[128:]).astype(bf16)
        return 0

    lax.fori_loop(0, 16, unit, 0, unroll=16)
    o = dot(m_out[...], w_proj[...].reshape(D, D)) + vec[4:5, :]
    x1 = x + vec[5:6, :] * o
    if keep:
        o_out[...] = o.astype(bf16)
    x1_out[...] = x1
    hat, _ = stats(x1)
    c_out[...] = (hat * vec[6:7, :] + vec[7:8, :]).astype(bf16)


def attention_forward(keep, x, vec, weights, received=None):
    outs = [((T, D), f32), ((T, D), bf16)]
    scratch = []
    if keep:
        outs = [((T, D), bf16)] * 2 + [((T, 3072), bf16), ((16, 256, 128), bf16), ((T, D), bf16), ((T, D), bf16)] + outs
    else:
        scratch = [pltpu.VMEM((T, 3072), bf16), pltpu.VMEM((T, D), bf16)]
    return call(
        lambda *refs: attention_forward_kernel(keep, *refs),
        outs,
        [x, vec, weights[0], weights[1]] + ([received] if keep else []),
        [VM] * (5 if keep else 4),
        scratch=scratch,
        flops=2 * T * D * 4 * D,
        moved=14 * 2**20,
        name="attention_forward" if keep else "first_attention",
        limit=6,
    )


def fc1_tile(w1, t):
    return w1[t // 2, :, :, :, (t % 2) * 512 : (t % 2) * 512 + 512].reshape(D, 512)


def feed_forward_kernel(keep, x1_ref, c_ref, vec, bias, w1, w2, *refs):
    if keep:
        u_out, gp_out, f_out, y_out = refs
    else:
        (y_out,) = refs
    c = c_ref[...]
    total = None
    ahead = dot(c, fc1_tile(w1, 0))
    for t in range(8):
        cols = slice(t * 512, t * 512 + 512)
        h = ahead + bias[0:1, cols]
        if t < 7:
            ahead = dot(c, fc1_tile(w1, t + 1))
        cdf = 0.5 * (1.0 + lax.erf(h * 0.7071067811865476))
        u = (h * cdf).astype(bf16)
        if keep:
            gp = cdf + h * (jnp.exp(-0.5 * h * h) * 0.3989422804014327)
            u_out[:, cols] = u
            gp_out[:, cols] = gp.astype(bf16)
        part = dot(u, w2[t].reshape(512, D))
        total = part if total is None else total + part
    f = total + vec[8:9, :]
    if keep:
        f_out[...] = f.astype(bf16)
    y_out[...] = (x1_ref[...] + vec[9:10, :] * f).astype(y_out.dtype)


def feed_forward(keep, x1, c, vec, bias, weights):
    outs = [((T, D), f32 if keep else bf16)]
    if keep:
        outs = [((T, FF), bf16), ((T, FF), bf16), ((T, D), bf16)] + outs
    return call(
        lambda *refs: feed_forward_kernel(keep, *refs),
        outs,
        [x1, c, vec, bias, weights[2], weights[3]],
        [VM] * 6,
        flops=4 * T * D * FF,
        moved=24 * 2**20,
        name="feed_forward",
        limit=6,
    )


def upstream_kernel(first, counts, source, *refs):
    vec, g_out, df_out = refs[-3:]
    image = lax.axis_index("shard") * YS + lax.axis_index("replica")
    for m in range(2):
        rows = slice(m * 128, m * 128 + 128)
        g = source[rows, :].astype(f32) * jnp.where(image < counts[m], 1.0, 0.0)
        if not first:
            g = jnp.where(lax.axis_index("section") == 1, g, refs[m][...].astype(f32))
        g_out[rows, :] = g
        df_out[rows, :] = (vec[9:10, :] * g).astype(bf16)


def upstream(counts, source, vec, received=None):
    extra = [] if received is None else list(received)
    return call(
        lambda *refs: upstream_kernel(received is None, *refs),
        [((T, D), f32), ((T, D), bf16)],
        [counts, source] + extra + [vec],
        [SM] + [VM] * (2 + len(extra)),
        moved=2**20,
        name="upstream",
    )


def feed_backward_kernel(keep, g_ref, df_ref, f_ref, gp_ref, x1_ref, o_ref, vec, w1, w2, dx1_out, do_out, *refs):
    g = g_ref[...]
    df = df_ref[...]
    if keep:
        dh_out, small = refs
        small[8:9, :] = jnp.sum(df.astype(f32), axis=0, keepdims=True)
        small[9:10, :] = jnp.sum(g * f_ref[...].astype(f32), axis=0, keepdims=True)
        small[0:4, :] = jnp.zeros((4, D), f32)
        small[14:16, :] = jnp.zeros((2, D), f32)
    total = None
    ahead = dot(df, w2[0].reshape(512, D), NT)
    for t in range(8):
        y, off = t // 2, (t % 2) * 512
        cols = slice(t * 512, t * 512 + 512)
        du = ahead
        if t < 7:
            ahead = dot(df, w2[t + 1].reshape(512, D), NT)
        dh = (gp_ref[:, cols].astype(f32) * du).astype(bf16)
        if keep:
            dh_out[:, cols] = dh
            small[10 + y : 11 + y, off : off + 512] = jnp.sum(dh.astype(f32), axis=0, keepdims=True)
        part = dot(dh, fc1_tile(w1, t), NT)
        total = part if total is None else total + part
    hat, scale = stats(x1_ref[...])
    d_norm, d_gain, d_shift = norm_back(total, vec[6:7, :], hat, scale)
    dx1 = g + d_norm
    dx1_out[...] = dx1
    do = (vec[5:6, :] * dx1).astype(bf16)
    do_out[...] = do
    if keep:
        small[4:5, :] = jnp.sum(do.astype(f32), axis=0, keepdims=True)
        small[5:6, :] = jnp.sum(dx1 * o_ref[...].astype(f32), axis=0, keepdims=True)
        small[6:7, :] = d_gain
        small[7:8, :] = d_shift


def feed_backward(keep, g, df, f, gp, x1, o, vec, weights):
    outs = [((T, D), f32), ((T, D), bf16)]
    if keep:
        outs += [((T, FF), bf16), ((16, D), f32)]
    return call(
        lambda *refs: feed_backward_kernel(keep, *refs),
        outs,
        [g, df, f, gp, x1, o, vec, weights[2], weights[3]],
        [VM] * 9,
        flops=4 * T * D * FF,
        moved=26 * 2**20,
        name="feed_backward",
        limit=6,
    )


def attention_backward_kernel(
    do_ref, dx1_ref, x_ref, p_ref, soft_ref, small_ref, vec, w_qkv, w_proj, *refs
):
    dp_out, dx_out, small, dm_ref = refs[-4:]
    dm_ref[...] = dot(do_ref[...], w_proj[...].reshape(D, D), NT).astype(bf16)
    lane = lax.broadcasted_iota(jnp.int32, (128, 128), 1) < 64

    def unit(u, _):
        i, h = lax.div(u, jnp.int32(8)), lax.rem(u, jnp.int32(8))
        rows = pl.ds(pl.multiple_of(i * 128, 128), 128)
        at = lambda o: pl.ds(pl.multiple_of(h * 128 + o, 128), 128)
        q, k, v = [p_ref[rows, at(o)] for o in (0, 1024, 2048)]
        dm = stacked_heads(dm_ref[rows, at(0)], lane)
        low = soft_ref[u]
        soft = low.astype(f32)
        dp_out[rows, at(2048)] = dot(low, dm, TN).astype(bf16)
        dw = dot(dm, v, NT)
        ds = (soft * (dw - jnp.sum(soft * dw, axis=-1, keepdims=True))).astype(bf16)
        dq = dot(ds, k) * 0.125
        dp_out[rows, at(0)] = jnp.where(lane, dq[:128], dq[128:]).astype(bf16)
        dp_out[rows, at(1024)] = (dot(ds, stacked_heads(q, lane), TN) * 0.125).astype(bf16)
        return 0

    lax.fori_loop(0, 16, unit, 0, unroll=16)
    small[2:3, :] = jnp.sum(dp_out[:, 0:1024].astype(f32), axis=0, keepdims=True)
    small[3:4, :] = jnp.sum(dp_out[:, 2048:3072].astype(f32), axis=0, keepdims=True)
    small[4:16, :] = small_ref[4:16, :]
    dp_out[:, 3072:4096] = do_ref[...]
    total = None
    for j in range(6):
        cols = slice(j * 512, j * 512 + 512)
        part = dot(dp_out[:, cols], w_qkv[:, :, :, cols].reshape(D, 512), NT)
        total = part if total is None else total + part
    hat, scale = stats(x_ref[...].astype(f32))
    d_norm, small[0:1, :], small[1:2, :] = norm_back(total, vec[0:1, :], hat, scale)
    dx = dx1_ref[...] + d_norm
    if len(refs) > 4:
        dx = jnp.where(lax.axis_index("section") == 0, dx, refs[0][...])
    dx_out[...] = dx.astype(dx_out.dtype)


def attention_input_grad_kernel(image, do_ref, dx1_ref, x_ref, p_ref, soft_ref, vec, w_qkv, w_proj, dx_out, dm_ref, dp_ref):
    rows = slice(image * 128, image * 128 + 128)
    dm_ref[...] = dot(do_ref[rows, :], w_proj[...].reshape(D, D), NT).astype(bf16)
    lane = lax.broadcasted_iota(jnp.int32, (128, 128), 1) < 64

    def unit(h, _):
        at = lambda o: pl.ds(pl.multiple_of(h * 128 + o, 128), 128)
        q, k, v = [p_ref[rows, at(o)] for o in (0, 1024, 2048)]
        dm = stacked_heads(dm_ref[:, at(0)], lane)
        low = soft_ref[image * 8 + h]
        soft = low.astype(f32)
        dp_ref[:, at(2048)] = dot(low, dm, TN).astype(bf16)
        dw = dot(dm, v, NT)
        ds = (soft * (dw - jnp.sum(soft * dw, axis=-1, keepdims=True))).astype(bf16)
        dq = dot(ds, k) * 0.125
        dp_ref[:, at(0)] = jnp.where(lane, dq[:128], dq[128:]).astype(bf16)
        dp_ref[:, at(1024)] = (dot(ds, stacked_heads(q, lane), TN) * 0.125).astype(bf16)
        return 0

    lax.fori_loop(0, 8, unit, 0, unroll=8)
    total = None
    for j in range(6):
        cols = slice(j * 512, j * 512 + 512)
        part = dot(dp_ref[:, cols], w_qkv[:, :, :, cols].reshape(D, 512), NT)
        total = part if total is None else total + part
    hat, scale = stats(x_ref[rows, :].astype(f32))
    d_norm, _, _ = norm_back(total, vec[0:1, :], hat, scale)
    dx_out[...] = (dx1_ref[rows, :] + d_norm).astype(bf16)


def attention_input_grad(image, do, dx1, x, p, soft, vec, weights):
    return call(
        lambda *refs: attention_input_grad_kernel(image, *refs),
        [((128, D), bf16)],
        [do, dx1, x, p, soft, vec, weights[0], weights[1]],
        [VM] * 8,
        scratch=[pltpu.VMEM((128, D), bf16), pltpu.VMEM((128, 3072), bf16)],
        flops=T * D * 4 * D,
        moved=10 * 2**20,
        name="attention_input_grad",
        limit=6,
    )[0]


def attention_backward(do, dx1, x, p, soft, small, vec, weights, output=None):
    extra = [] if output is None else [output]
    return call(
        attention_backward_kernel,
        [((T, 4096), bf16), ((T, D), f32 if extra else bf16), ((16, D), f32)],
        [do, dx1, x, p, soft, small, vec, weights[0], weights[1]] + extra,
        [VM] * (9 + len(extra)),
        scratch=[pltpu.VMEM((T, D), bf16)],
        flops=2 * T * D * 4 * D,
        moved=18 * 2**20,
        name="attention_backward",
        limit=6,
    )


def picked_kernel(a_ref, m_ref, c_ref, u_ref, mine, theirs):
    x, z, c, _ = place()
    row = lax.broadcasted_iota(jnp.int32, (512, D), 0)
    col = lax.broadcasted_iota(jnp.int32, (512, D), 1)
    eye_r = lax.broadcasted_iota(jnp.int32, (256, 256), 0)
    eye = jnp.where(eye_r == lax.broadcasted_iota(jnp.int32, (256, 256), 1), 1.0, 0.0).astype(bf16)
    kind, dz, inner = row >> 7, (row >> 6) & 1, row & 63
    for k, out in enumerate((mine, theirs)):
        ck = near(c, k, CS)
        step = 1 - 2 * ck
        there = jnp.where(kind == 0, 2, jnp.where(kind == 1, 4 - step, jnp.where(kind == 2, 4 + step, 0)))
        there = (((x + there) & 3) << 8) + (((z + dz) & 1) << 7) + inner + ck * 64
        chosen = jnp.where(col == there, 1.0, 0.0).astype(bf16)
        for n, ref in enumerate((a_ref, m_ref)):
            out[n * 512 : n * 512 + 512, :] = dot(chosen, ref[...], NT).astype(bf16)
        there = ((row >> 6) << 7) + inner + ck * 64
        chosen = jnp.where(col == there, 1.0, 0.0).astype(bf16)
        out[1024:1536, :] = dot(chosen, c_ref[...], NT).astype(bf16)
        for j in range(8):
            chip = near(x, j % 4, XS) * 2 + near(z, j // 4, ZS)
            block = u_ref[:, pl.ds(pl.multiple_of((2 * chip + ck) * 256, 256), 256)]
            turned = dot(eye, block, NT).astype(bf16)
            for k2 in range(YS):
                out[1536 + k2 * 512 + j * 64 : 1600 + k2 * 512 + j * 64, :] = turned[k2 * 64 : k2 * 64 + 64]


def picked(a, m, c, u):
    return call(
        picked_kernel,
        [((3584, T), bf16)] * 2,
        [a, m, c, u],
        [VM] * 4,
        flops=2 * 10**9,
        moved=8 * 2**20,
        name="transposed_acts",
    )


def fc2_grads_kernel(mine, theirs, df, df2, *outs):
    _, _, c, y = place()
    for n, yk in enumerate(places(y, c, YS)):
        rows = pl.ds(pl.multiple_of(1536 + yk * 512, 512), 512)
        grad = dot(mine[rows, :], df[...]) + dot(theirs[rows, :], df2[...])
        outs[n][...] = grad.astype(bf16).reshape(8, 64, 1024)


def fc1_grads_kernel(mine, theirs, dh, dh2, *outs):
    _, _, c, y = place()
    for n, yk in enumerate(places(y, c, YS)):
        cols = pl.ds(pl.multiple_of(yk * 1024, 1024), 1024)
        grad = dot(mine[1024:1536, :], dh[:, cols]) + dot(theirs[1024:1536, :], dh2[:, cols])
        outs[n][...] = grad.astype(bf16).reshape(8, 64, 1024)


def feed_grads(kernel, name, mine, theirs, given, given2):
    return call(
        kernel,
        [((8, 64, 1024), bf16)] * 4,
        [mine, theirs, given, given2],
        [VM] * 4,
        flops=4 * T * D * FF,
        moved=12 * 2**20,
        name=name,
    )


def attention_grads_kernel(mine, theirs, dp, dp2, small, small2, *refs):
    outs, total = refs[:4], refs[4]
    x, z, c, _ = place()
    total[...] = small[...] + small2[...]
    vec = total[...].astype(bf16)
    row = lax.broadcasted_iota(jnp.int32, (D, 128), 0)
    col = lax.broadcasted_iota(jnp.int32, (D, 128), 1)
    line = lax.broadcasted_iota(jnp.int32, (16, 128), 0)
    for n, x_there in enumerate(places(x, c, XS)):
        for dz in range(ZS):
            inner = near(z, dz, ZS) * 2 + c
            chosen = jnp.where((row == col + x_there * 256 + inner * 64) & (col < 64), 1.0, 0.0).astype(bf16)
            outs[n][dz, 32:64, 4096:4224] = jnp.zeros((32, 128), bf16)
            outs[n][dz, 0:16, 4096:4224] = dot(vec, chosen).astype(bf16)
            there = total[pl.ds(10 + x_there, 1), pl.ds(pl.multiple_of(inner * 256, 256), 256)]
            a, b = there[:, 0:128], there[:, 128:256]
            outs[n][dz, 16:32, 4096:4224] = jnp.where(line == 0, a, jnp.where(line == 1, b, 0.0)).astype(bf16)
    for t in range(8):
        low = 0 if t < 6 else 512
        cols = slice(t * 512, t * 512 + 512)
        grad = dot(mine[low : low + 512, :], dp[:, cols]) + dot(theirs[low : low + 512, :], dp2[:, cols])
        grad = grad.astype(bf16)
        for n in range(4):
            outs[n][:, :, cols] = grad[n * 128 : n * 128 + 128].reshape(2, 64, 512)


def attention_grads(mine, theirs, dp, dp2, small, small2):
    return call(
        attention_grads_kernel,
        [((2, 64, QP), bf16)] * 4,
        [mine, theirs, dp, dp2, small, small2],
        [VM] * 6,
        scratch=[pltpu.VMEM((16, D), f32)],
        flops=8 * T * D * 2 * D,
        moved=16 * 2**20,
        name="attention_grads",
    )


def sum_kernel(count, axis, *refs):
    total = refs[0][...].astype(f32)
    for ref in refs[1:count]:
        total = total + ref[...].astype(f32)
    outs = refs[count:]
    if axis == "add":
        outs[0][...] = jnp.sum(total, axis=0).astype(bf16)
    elif axis == "split":
        for n, out in enumerate(outs):
            out[...] = total[n].astype(bf16)
    elif axis == "halves":
        count = total.shape[0] // 2
        outs[0][...] = total[:count].astype(bf16)
        outs[1][...] = total[count:].astype(bf16)
    elif axis == "quarters":
        outs, held = outs[:4], outs[4]
        held[...] = total
        _, _, _, y = place()
        for dy, out in enumerate(outs):
            out[...] = held[pl.ds(pl.multiple_of(near(y, dy, YS) * 16, 16), 16), :].astype(bf16)
    else:
        outs[0][...] = total.astype(bf16)


def summed(parts, axis=None):
    shape = parts[0].shape
    scratch = []
    if axis == "split":
        outs = [(shape[1:], bf16)] * shape[0]
    elif axis == "halves":
        outs = [((shape[0] // 2,) + shape[1:], bf16)] * 2
    elif axis == "quarters":
        outs = [((16,) + shape[1:], bf16)] * 4
        scratch = [pltpu.VMEM(shape, f32)]
    else:
        outs = [(shape[1:] if axis else shape, bf16)]
    size = 1
    for n in shape:
        size *= n
    out = call(
        lambda *refs: sum_kernel(len(parts), axis, *refs),
        outs,
        parts,
        [VM] * len(parts),
        scratch=scratch,
        flops=size * len(parts),
        moved=2 * size * (len(parts) + 1),
        name="summed",
    )
    return out if len(outs) > 1 else out[0]


def gathered_copies(parts, target, sems):
    y = place()[3]
    copies = [pltpu.make_async_copy(part, target.at[near(y, dy, YS)], sems.at[dy]) for dy, part in enumerate(parts)]
    start(copies)
    return copies


def fc1_results_kernel(a, b, c, d, out, held, sems):
    wait(gathered_copies((a, b, c, d), held, sems))
    for k in range(YS):
        out[:, k * 1024 : k * 1024 + 1024] = held[k].astype(f32)


def fc2_results_kernel(a, b, c, d, out, held, sems):
    wait(gathered_copies((a, b, c, d), held, sems))
    for k in range(YS):
        out[k * 64 : k * 64 + 64, :] = held[k].astype(f32)


def column_results_kernel(a, b, c, d, qkv, proj, vec, bias, held, sems):
    wait(gathered_copies((a, b, c, d), held, sems))
    for k in range(YS):
        line = slice(k * 16, k * 16 + 16)
        qkv[line, :] = held[k, :, 0:3072].astype(f32)
        proj[line, :] = held[k, :, 3072:4096].astype(f32)
    vec[...] = held[0, 0:10, 4096:4160].astype(f32)
    tail = held[1, 0:16, 4096:4224].astype(f32)
    bias[:, 0:128] = tail[0:1]
    bias[:, 128:256] = tail[1:2]


def results(kernel, shapes, parts, name):
    return call(
        kernel,
        [(shape, f32) for shape in shapes],
        parts,
        [ANY] * 4,
        scratch=[pltpu.VMEM((4,) + parts[0].shape, bf16), pltpu.SemaphoreType.DMA((4,))],
        moved=10 * 2**20,
        name=name,
    )


def twin(value, name="twin"):
    with jax.named_scope(name):
        return from_shard(value, dc=1)


def around(value, name):
    with jax.named_scope(name):
        return [value] + [from_replica(value, dy) for dy in range(1, YS)]


def swap(value, name):
    groups = [[shard_of(x, z, c) for x in range(XS) for z in range(ZS)] for c in range(CS)]
    with jax.named_scope(name):
        return lax.all_to_all(value, "shard", split_axis=0, concat_axis=0, axis_index_groups=groups, tiled=True)


def gather(w_qkv, w_proj, w_fc1, w_fc2, vectors, fc1_bias):
    hold = lax.optimization_barrier
    here = swap(own_pieces(w_fc1, w_fc2), "here")
    unit = own_unit(w_qkv, w_proj, w_fc2, vectors, fc1_bias)
    twin_unit = twin(unit, "twin_unit")
    unit, here, twin_unit = hold((unit, here, twin_unit))
    behind, twin_here = onward(here, "y", "behind"), twin(here, "twin_here")
    other = from_shard(unit, dz=1, name="other")
    plus, minus = from_shard(unit, dx=1, name="plus"), from_shard(unit, dx=3, name="minus")
    behind, twin_here, other, plus, minus = hold((behind, twin_here, other, plus, minus))
    twin_behind = onward(twin_here, "y", "twin_behind")
    minus_other, plus_other = from_shard(other, dx=3, name="minus_other"), from_shard(plus, dz=1, name="plus_other")
    far = from_shard(plus, dx=1, name="far")
    first = stacked([other, plus, minus])
    twins = twin(first, "twin_first")
    weights = put_columns(None, [(0, 0, 0, 0, None), (1, 0, 0, 1, None)], [unit, twin_unit])
    fc1, weights[2] = put_rows(None, weights[2], {(0, 3): here, (1, 3): twin_here})
    held = hold((twin_behind, minus_other, plus_other, far, first, twins, fc1, weights))
    twin_behind, minus_other, plus_other, far, first, twins, fc1, weights = held
    far_first, far_rest = parted(far, minus_other)
    opposite = onward(after(behind, far_first), "y", "opposite")
    far_first, far_rest = from_shard(far_first, dz=1, name="far_first"), from_shard(far_rest, dx=3, name="far_rest")
    ahead, twin_ahead = twin(twin_behind, "ahead"), twin(behind, "twin_ahead")
    second = stacked([minus_other, plus_other, far])
    second_twins = twin(second, "twin_second")
    order = [(0, 1), (1, 0), (3, 0)]
    weights = put_columns(weights, [(k, dx, dz, k, n) for k in range(2) for n, (dx, dz) in enumerate(order)], [first, twins])
    fc1, weights[2] = put_rows(fc1, weights[2], {(0, 1): behind, (1, 1): twin_behind})
    held = hold((far_first, far_rest, ahead, twin_ahead, second, second_twins, fc1, weights))
    far_first, far_rest, ahead, twin_ahead, second, second_twins, fc1, weights = held
    order = [(3, 1), (1, 1), (2, 0)]
    keys = [(k, dx, dz, k, n) for k in range(2) for n, (dx, dz) in enumerate(order)]
    weights = put_columns(weights, keys, [second, second_twins])
    weights = put_columns(weights, [(0, 2, 1, 0, None), (1, 2, 1, 1, None)], [far_first, twin(far_first, "twin_far_first")])
    vec, bias = gathered_vectors(weights[3])
    fc1, fc2 = put_rows(fc1, weights[2], {(0, 2): ahead, (1, 2): twin_ahead})
    fc2 = put_rest(fc2, far_rest, twin(far_rest, "twin_far_rest"))
    opposite, fc2, vec = hold((opposite, fc2, vec))
    return [weights[0], weights[1], fc2], fc1, opposite, vec, bias


def put_last(weights, fc1, opposite):
    fc1, fc2 = put_rows(fc1, weights[2], {(0, 0): opposite, (1, 0): twin(opposite, "twin_opposite")})
    return weights[0], weights[1], fc1, fc2


def shards(edge_inputs, image_counts, w_qkv, w_proj, w_fc1, w_fc2, vectors, fc1_bias):
    source = edge_inputs[0, :, 0].reshape(T, D)
    weights, fc1, opposite, vec, bias = gather(w_qkv[0], w_proj[0], w_fc1[0], w_fc2[0], vectors[0], fc1_bias)
    hold = lax.optimization_barrier

    x1, c = attention_forward(False, source, vec, weights)
    weights = put_last(weights, fc1, opposite)
    (first_out,) = feed_forward(False, x1, c, vec, bias, weights)
    received = passed_along(first_out, 1)
    inputs, a, p, soft, m, o, x1, c = attention_forward(True, source, vec, weights, received)
    u, gp, f, output = feed_forward(True, x1, c, vec, bias, weights)

    g, df = upstream(image_counts, source, vec)
    dx1, do = feed_backward(False, g, df, f, gp, x1, o, vec, weights)
    halves = [attention_input_grad(m, do, dx1, inputs, p, soft, vec, weights) for m in range(2)]
    received_grad = [passed_along(half, -1) for half in halves]
    mine, theirs = picked(after(a, halves[1]), m, c, u)
    received_grad, mine, theirs = lax.optimization_barrier((received_grad, mine, twin(theirs)))

    hold = lax.optimization_barrier
    g, df = upstream(image_counts, source, vec, received_grad)
    parts_2 = feed_grads(fc2_grads_kernel, "fc2_grads", mine, theirs, df, twin(df, "twin_df"))
    far_2 = onward(parts_2[0], "y", "far_2")
    g = after(g, parts_2[0])
    dx1, do, dh, small = feed_backward(True, g, df, f, gp, x1, o, vec, weights)
    dh2 = twin(dh, "twin_dh")
    dp, edge, small = attention_backward(do, dx1, inputs, p, soft, small, vec, weights, output)
    dh, dh2, dp, far_2 = hold((dh, dh2, dp, far_2))
    dp2, small2 = twin(dp, "twin_dp"), twin(small, "twin_small")
    relay_2 = summed([parts_2[2], far_2])
    own_2, given_2 = onward(relay_2, "y", "own_2"), onward(after(parts_2[1], relay_2), "y", "given_2", -1)
    parts_1 = feed_grads(fc1_grads_kernel, "fc1_grads", mine, theirs, after(dh, relay_2), dh2)
    parts_c = attention_grads(mine, theirs, after(dp, parts_1[3]), dp2, small, small2)
    far_c, given_c = onward(parts_c[0], "x", "far_c"), onward(parts_c[1], "x", "given_c", -1)
    parts_1, own_2, given_2, last = hold((parts_1, own_2, given_2, parts_c[3]))
    far_1, given_1 = onward(parts_1[0], "y", "far_1"), onward(parts_1[1], "y", "given_1", -1)

    same_2, other_2 = summed([parts_2[3], own_2, given_2], "halves")
    with jax.named_scope("other_2"):
        other_2 = from_shard(other_2, dz=1)
    far_c, given_c = hold((far_c, given_c))
    relay_c = summed([after(parts_c[2], same_2), far_c])
    own_c = onward(relay_c, "x", "own_c")
    along = summed([after(same_2, relay_c), other_2], "split")
    with jax.named_scope("along_2"):
        along = [along[0]] + [from_shard(along[dx], dx=XS - dx) for dx in range(1, XS)]
    far_1, given_1 = hold((far_1, given_1))
    relay_1 = summed([after(parts_1[2], along[0]), far_1])
    own_1 = onward(relay_1, "y", "own_1")
    same, other = summed([after(last, relay_1), own_c, given_c], "split")
    fc2 = summed([after(along[0], same)] + along[1:])
    with jax.named_scope("other_z"):
        other = from_shard(other, dz=1)
    quarters = summed([after(same, fc2), other], "quarters")
    sum_1 = summed([after(parts_1[3], quarters[0]), own_1, given_1])
    with jax.named_scope("quarters"):
        quarters = [quarters[0]] + [from_replica(quarters[dy], YS - dy) for dy in range(1, YS)]
    got_1 = swap(sum_1, "swap_1")
    (g_fc2,) = results(fc2_results_kernel, [(256, D)], around(fc2, "around_fc2"), "fc2_results")
    column = around(summed([after(quarters[0], g_fc2)] + quarters[1:]), "around_c")
    fc1 = around(summed([got_1], "add"), "around_fc1")
    g_qkv, g_proj, g_vec, g_bias = results(
        column_results_kernel, [(64, 3072), (64, 1024), (10, 64), (1, 256)], column, "column_results"
    )
    (g_fc1,) = results(fc1_results_kernel, [(64, FF)], fc1, "fc1_results")
    return (
        edge.reshape(1, 2, 1, 128, D),
        g_qkv[None],
        g_proj[None],
        g_fc1[None],
        g_fc2[None],
        g_vec[None],
        g_bias,
    )


def solution(mesh):
    placed = (
        P("section", None, ("shard", "replica"), None, None),
        P(),
        P("section", "shard", None),
        P("section", "shard", None),
        P("section", "shard", None),
        P("section", "shard", None),
        P("section", None, "shard"),
        P("section", "shard"),
    )
    return jax.shard_map(
        shards,
        mesh=mesh,
        in_specs=placed,
        out_specs=(placed[0],) + placed[2:],
        check_vma=False,
    )
```

```python
import jax
import jax.numpy as jnp
from jax import lax
from jax.experimental import pallas as pl
from jax.experimental.pallas import tpu as pltpu
from jax.sharding import PartitionSpec as P

XS, ZS, CS, YS = 4, 2, 2, 4
T = 256
D, FF = 1024, 4096
GROWS = 32
TAILS = 4 - GROWS // 16
UNIT = 4096 + 1024 * TAILS + 128
QP = 4224
LIMIT = 8
HEAVY = ('first_attention', 'feed_backward', 'attention_backward', 'attention_input_grad', 'transposed_acts')
epsilon = 1e-06
bf16, f32 = jnp.bfloat16, jnp.float32
ANY = pl.BlockSpec(memory_space=pl.ANY)
HB = pl.BlockSpec(memory_space=pltpu.HBM)
VM = pl.BlockSpec(memory_space=pltpu.VMEM)
SM = pl.BlockSpec(memory_space=pltpu.SMEM)
NT = (((1,), (1,)), ((), ()))
TN = (((0,), (0,)), ((), ()))


def shard_of(x, z, c):
    return (x % XS) * 4 + (z % ZS) * 2 + (c % CS)


def from_shard(value, dx=0, dz=0, dc=0, name="from_shard"):
    pairs = [
        (shard_of(x + dx, z + dz, c + dc), shard_of(x, z, c))
        for x in range(XS)
        for z in range(ZS)
        for c in range(CS)
    ]
    with jax.named_scope(name):
        return lax.ppermute(value, "shard", pairs)


def from_replica(value, dy):
    return lax.ppermute(value, "replica", [((y + dy) % YS, y) for y in range(YS)])


def onward(value, axis, name="onward", way=1):
    pairs = []
    for x in range(XS):
        for z in range(ZS):
            for c in range(CS):
                for y in range(YS):
                    step = way * (1 - 2 * c)
                    tx, ty = (x + step, y) if axis == "x" else (x, y + step)
                    pairs.append((shard_of(x, z, c) * YS + y, shard_of(tx, z, c) * YS + ty % YS))
    with jax.named_scope(name):
        return lax.ppermute(value, ("shard", "replica"), pairs)


def passed_along(value, steps):
    return lax.ppermute(value, "section", [(0, 1)] if steps == 1 else [(1, 0)])


def place():
    shard = lax.axis_index("shard")
    x = lax.div(shard, jnp.int32(4))
    z = lax.rem(lax.div(shard, jnp.int32(2)), jnp.int32(2))
    c = lax.rem(shard, jnp.int32(2))
    return x, z, c, lax.axis_index("replica")


def near(base, step, size):
    return lax.rem(base + jnp.int32(step), jnp.int32(size))


def call(kernel, outs, args, kinds, scratch=(), flops=0, moved=0, out_kinds=None, name=None, aliases=None, limit=LIMIT):
    return pl.pallas_call(
        kernel,
        out_shape=[jax.ShapeDtypeStruct(s, d) for s, d in outs],
        in_specs=list(kinds),
        out_specs=list(out_kinds or [VM] * len(outs)),
        scratch_shapes=list(scratch),
        compiler_params=pltpu.CompilerParams(vmem_limit_bytes=limit * 2**20),
        cost_estimate=pl.CostEstimate(flops=3 * 10**10 if name in HEAVY else 1, bytes_accessed=1, transcendentals=0),
        name=name,
        input_output_aliases=aliases or {},
    )(*args)


def after(values, token):
    return lax.optimization_barrier((values, token))[0]


def dot(a, b, dims=(((1,), (0,)), ((), ()))):
    return lax.dot_general(a, b, dims, preferred_element_type=f32)


def stats(values):
    average = jnp.mean(values, axis=-1, keepdims=True)
    centered = values - average
    spread = jnp.mean(centered * centered, axis=-1, keepdims=True)
    scale = lax.rsqrt(spread + epsilon)
    return centered * scale, scale


def norm_back(grad, gain, hat, scale):
    d_hat = grad * gain
    d_in = scale * (
        d_hat - jnp.mean(d_hat, axis=-1, keepdims=True) - hat * jnp.mean(d_hat * hat, axis=-1, keepdims=True)
    )
    return d_in, jnp.sum(grad * hat, axis=0, keepdims=True), jnp.sum(grad, axis=0, keepdims=True)


def places(base, c, size):
    step = 1 - 2 * c
    return [near(base + 4, d, size) for d in (2, -step, step, 0)]


def pieces_kernel(fc1, fc2, pieces, sems):
    _, _, _, y = place()
    block = fc1.at[:, pl.ds(pl.multiple_of(y * 1024, 1024), 1024)]
    rows = fc2.at[pl.ds(pl.multiple_of(y * GROWS, 16), GROWS)]
    copies = []
    for n in range(8):
        copies.append(pltpu.make_async_copy(block, pieces.at[n, 0:64], sems.at[2 * n]))
        copies.append(pltpu.make_async_copy(rows, pieces.at[n, 64 : 64 + GROWS], sems.at[2 * n + 1]))
    start(copies)
    wait(copies)


def own_pieces(w_fc1, w_fc2):
    return call(
        pieces_kernel,
        [((8, 64 + GROWS, 1024), bf16)],
        (w_fc1, w_fc2),
        [HB] * 2,
        scratch=[pltpu.SemaphoreType.DMA((16,))],
        moved=4 * 2**20,
        name="own_pieces",
        limit=56,
    )[0]


def unit_kernel(qkv, proj, fc2, vectors, bias, unit, small, sems):
    copies = [pltpu.make_async_copy(qkv, unit.at[:, 0:3072], sems.at[0])]
    copies.append(pltpu.make_async_copy(proj, unit.at[:, 3072:4096], sems.at[1]))
    for n in range(TAILS):
        row, col = 4 * GROWS + 64 * n, QP + 1024 * n
        copies.append(
            pltpu.make_async_copy(fc2.at[row : row + 64], unit.at[:, col : col + 1024], sems.at[2 + n])
        )
    start(copies)
    small[...] = jnp.zeros_like(small)
    small[0:10, 0:64] = vectors[...].astype(f32)
    small[16:17, :] = bias[:, 0:128].astype(f32)
    small[17:18, :] = bias[:, 128:256].astype(f32)
    wait(copies)
    unit[:, 4096:QP] = small[...].astype(bf16)


def own_unit(w_qkv, w_proj, w_fc2, vectors, fc1_bias):
    return call(
        unit_kernel,
        [((64, UNIT), bf16)],
        (w_qkv, w_proj, w_fc2, vectors, fc1_bias),
        [HB] * 3 + [VM] * 2,
        scratch=[pltpu.VMEM((64, 128), f32), pltpu.SemaphoreType.DMA((2 + TAILS,))],
        moved=4 * 2**20,
        name="own_unit",
        limit=56,
    )[0]


def start(copies):
    for copy in copies:
        copy.start()


def wait(copies):
    for copy in copies:
        copy.wait()


def columns_kernel(keys, *refs):
    pieces, (qkv, proj, fc2, small), sems = refs, refs[-5:-1], refs[-1]
    x, z, c, _ = place()
    copies = []
    for n, (k, dx, dz, array, row) in enumerate(keys):
        piece = pieces[array] if row is None else pieces[array].at[row]
        width = piece.shape[-1]
        xz, ck = near(x, dx, XS) * 2 + near(z, dz, ZS), near(c, k, CS)
        parts = []
        if width != UNIT - QP:
            parts = [(0, 3072, qkv.at[xz, ck]), (3072, 4096, proj.at[xz, ck]), (4096, QP, small.at[xz, ck])]
        if width != QP:
            for t in range(TAILS):
                first, col = 4 * GROWS + 64 * t, width - 1024 * (TAILS - t)
                parts.append((col, col + 1024, fc2.at[xz, ck, first : first + 64]))
        for t, (low, high, target) in enumerate(parts):
            copies.append(pltpu.make_async_copy(piece.at[:, low:high], target, sems.at[n, t]))
    start(copies)
    wait(copies)


def put_columns(weights, keys, arrays):
    held = list(weights or [])
    count = len(arrays)
    return list(
        call(
            lambda *refs: columns_kernel(keys, *refs),
            [((8, 2, 64, 3072), bf16), ((8, 2, 64, 1024), bf16), ((8, 2, 256, 1024), bf16), ((8, 2, 64, 128), bf16)],
            list(arrays) + held,
            [ANY] * count + [VM] * len(held),
            scratch=[pltpu.SemaphoreType.DMA((len(keys), 3 + TAILS))],
            moved=count * 2**20,
            name="put_columns",
            aliases={count + n: n for n in range(len(held))},
        )
    )


def rest_kernel(mine, other, held, fc2, sems):
    x, z, c, _ = place()
    xz = near(x, 2, XS) * 2 + near(z, 1, ZS)
    copies = []
    for k, piece in enumerate((mine, other)):
        for t in range(TAILS):
            first = 4 * GROWS + 64 * t
            target = fc2.at[xz, near(c, k, CS), first : first + 64]
            copies.append(pltpu.make_async_copy(piece.at[:, 1024 * t : 1024 * t + 1024], target, sems.at[k, t]))
    start(copies)
    wait(copies)


def put_rest(fc2, mine, other):
    return call(
        rest_kernel,
        [((8, 2, 256, 1024), bf16)],
        [mine, other, fc2],
        [ANY, ANY, VM],
        scratch=[pltpu.SemaphoreType.DMA((2, TAILS))],
        moved=2**20,
        name="put_rest",
        aliases={2: 0},
    )[0]


def parted_kernel(a, b, first, rest, sems):
    copies = [pltpu.make_async_copy(a.at[:, 0:QP], first, sems.at[0])]
    copies.append(pltpu.make_async_copy(b.at[:, QP:UNIT], rest, sems.at[1]))
    start(copies)
    wait(copies)


def parted(a, b):
    return call(
        parted_kernel,
        [((64, QP), bf16), ((64, UNIT - QP), bf16)],
        [a, b],
        [ANY] * 2,
        scratch=[pltpu.SemaphoreType.DMA((2,))],
        moved=2**20,
        name="parted",
    )


def stack_kernel(*refs):
    pieces, out, sems = refs[:-2], refs[-2], refs[-1]
    copies = [pltpu.make_async_copy(piece, out.at[n], sems.at[n]) for n, piece in enumerate(pieces)]
    start(copies)
    wait(copies)


def stacked(pieces):
    return call(
        stack_kernel,
        [((len(pieces),) + pieces[0].shape, bf16)],
        pieces,
        [ANY] * len(pieces),
        scratch=[pltpu.SemaphoreType.DMA((len(pieces),))],
        moved=4 * 2**20,
        name="stacked",
    )[0]


def rows_kernel(keys, *refs):
    count = len(keys)
    pieces, (fc1, fc2), sems = refs[:count], refs[-3:-1], refs[-1]
    _, _, c, y = place()
    copies = []
    for n, (k, kind) in enumerate(keys):
        ck, yk = near(c, k, CS), places(y, c, YS)[kind]
        copies.append(pltpu.make_async_copy(pieces[n].at[:, 0:64], fc1.at[yk, :, ck], sems.at[n, 0]))
        target = fc2.at[:, ck, pl.ds(pl.multiple_of(yk * GROWS, 16), GROWS)]
        copies.append(pltpu.make_async_copy(pieces[n].at[:, 64 : 64 + GROWS], target, sems.at[n, 1]))
    start(copies)
    wait(copies)


def put_rows(fc1, fc2, pieces):
    keys = list(pieces)
    held = [fc1, fc2] if fc1 is not None else [fc2]
    count = len(keys)
    return call(
        lambda *refs: rows_kernel(keys, *refs),
        [((4, 8, 2, 64, 1024), bf16), ((8, 2, 256, 1024), bf16)],
        [pieces[key] for key in keys] + held,
        [ANY] * count + [VM] * len(held),
        scratch=[pltpu.SemaphoreType.DMA((count, 2))],
        moved=2 * count * 2**20,
        name="put_rows",
        aliases={count + n: 2 - len(held) + n for n in range(len(held))},
    )


def vectors_kernel(small, vec, bias):
    lane = lax.broadcasted_iota(jnp.int32, (16, 128), 1)
    for t in range(8):
        a = small[t, 0, 0:16].astype(f32)
        b = small[t, 1, 0:16].astype(f32)
        vec[:, t * 128 : t * 128 + 128] = jnp.where(lane < 64, a, pltpu.roll(b, 64, 1))
    for s in range(16):
        tail = small[s // 2, s % 2, 16:32].astype(f32)
        bias[0:1, s * 256 : s * 256 + 128] = tail[0:1]
        bias[0:1, s * 256 + 128 : s * 256 + 256] = tail[1:2]


def gathered_vectors(small):
    return call(
        vectors_kernel, [((16, 1024), f32), ((1, FF), f32)], [small], [VM], moved=2**20, name="gathered_vectors"
    )


def stacked_heads(pair, lane):
    zero = jnp.zeros_like(pair)
    return jnp.concatenate([jnp.where(lane, pair, zero), jnp.where(lane, zero, pair)], axis=0)


def attention_forward_kernel(keep, x_ref, vec, w_qkv, w_proj, *refs):
    if keep:
        received, x_out, a_out, p_out, soft_out, m_out, o_out, x1_out, c_out = refs
        x_out[...] = jnp.where(lax.axis_index("section") == 0, x_ref[...].astype(f32), received[...].astype(f32)).astype(bf16)
        x = x_out[...].astype(f32)
    else:
        x1_out, c_out, p_out, m_out = refs
        x = x_ref[...].astype(f32)
    hat, _ = stats(x)
    a = (hat * vec[0:1, :] + vec[1:2, :]).astype(bf16)
    if keep:
        a_out[...] = a
    for j in range(6):
        part = dot(a, w_qkv[:, :, :, j * 512 : j * 512 + 512].reshape(D, 512))
        if j < 2:
            part = part + vec[2:3, j * 512 : j * 512 + 512]
        if j >= 4:
            part = part + vec[3:4, j * 512 - 2048 : j * 512 - 1536]
        p_out[:, j * 512 : j * 512 + 512] = part.astype(bf16)
    lane = lax.broadcasted_iota(jnp.int32, (128, 128), 1) < 64

    def unit(u, _):
        i, h = lax.div(u, jnp.int32(8)), lax.rem(u, jnp.int32(8))
        rows = pl.ds(pl.multiple_of(i * 128, 128), 128)
        q, k, v = [p_out[rows, pl.ds(pl.multiple_of(h * 128 + o, 128), 128)] for o in (0, 1024, 2048)]
        s = dot(stacked_heads(q, lane), k, NT) * 0.125
        e = jnp.exp(s - jnp.max(s, axis=-1, keepdims=True))
        soft = (e / jnp.sum(e, axis=-1, keepdims=True)).astype(bf16)
        if keep:
            soft_out[u] = soft
        mixed = dot(soft, v)
        m_out[rows, pl.ds(pl.multiple_of(h * 128, 128), 128)] = jnp.where(lane, mixed[:128], mixed[128:]).astype(bf16)
        return 0

    lax.fori_loop(0, 16, unit, 0, unroll=16)
    o = dot(m_out[...], w_proj[...].reshape(D, D)) + vec[4:5, :]
    x1 = x + vec[5:6, :] * o
    if keep:
        o_out[...] = o.astype(bf16)
    x1_out[...] = x1
    hat, _ = stats(x1)
    c_out[...] = (hat * vec[6:7, :] + vec[7:8, :]).astype(bf16)


def attention_forward(keep, x, vec, weights, received=None):
    outs = [((T, D), f32), ((T, D), bf16)]
    scratch = []
    if keep:
        outs = [((T, D), bf16)] * 2 + [((T, 3072), bf16), ((16, 256, 128), bf16), ((T, D), bf16), ((T, D), bf16)] + outs
    else:
        scratch = [pltpu.VMEM((T, 3072), bf16), pltpu.VMEM((T, D), bf16)]
    return call(
        lambda *refs: attention_forward_kernel(keep, *refs),
        outs,
        [x, vec, weights[0], weights[1]] + ([received] if keep else []),
        [VM] * (5 if keep else 4),
        scratch=scratch,
        flops=2 * T * D * 4 * D,
        moved=14 * 2**20,
        name="attention_forward" if keep else "first_attention",
        limit=6,
    )


def fc1_tile(w1, t):
    return w1[t // 2, :, :, :, (t % 2) * 512 : (t % 2) * 512 + 512].reshape(D, 512)


def feed_forward_kernel(keep, x1_ref, c_ref, vec, bias, w1, w2, *refs):
    if keep:
        u_out, gp_out, f_out, y_out = refs
    else:
        (y_out,) = refs
    c = c_ref[...]
    total = None
    ahead = dot(c, fc1_tile(w1, 0))
    for t in range(8):
        cols = slice(t * 512, t * 512 + 512)
        h = ahead + bias[0:1, cols]
        if t < 7:
            ahead = dot(c, fc1_tile(w1, t + 1))
        cdf = 0.5 * (1.0 + lax.erf(h * 0.7071067811865476))
        u = (h * cdf).astype(bf16)
        if keep:
            gp = cdf + h * (jnp.exp(-0.5 * h * h) * 0.3989422804014327)
            u_out[:, cols] = u
            gp_out[:, cols] = gp.astype(bf16)
        part = dot(u, w2[t].reshape(512, D))
        total = part if total is None else total + part
    f = total + vec[8:9, :]
    if keep:
        f_out[...] = f.astype(bf16)
    y_out[...] = (x1_ref[...] + vec[9:10, :] * f).astype(y_out.dtype)


def feed_forward(keep, x1, c, vec, bias, weights):
    outs = [((T, D), f32 if keep else bf16)]
    if keep:
        outs = [((T, FF), bf16), ((T, FF), bf16), ((T, D), bf16)] + outs
    return call(
        lambda *refs: feed_forward_kernel(keep, *refs),
        outs,
        [x1, c, vec, bias, weights[2], weights[3]],
        [VM] * 6,
        flops=4 * T * D * FF,
        moved=24 * 2**20,
        name="feed_forward",
        limit=6,
    )


def upstream_kernel(first, counts, source, *refs):
    vec, g_out, df_out = refs[-3:]
    image = lax.axis_index("shard") * YS + lax.axis_index("replica")
    for m in range(2):
        rows = slice(m * 128, m * 128 + 128)
        g = source[rows, :].astype(f32) * jnp.where(image < counts[m], 1.0, 0.0)
        if not first:
            g = jnp.where(lax.axis_index("section") == 1, g, refs[m][...].astype(f32))
        g_out[rows, :] = g
        df_out[rows, :] = (vec[9:10, :] * g).astype(bf16)


def upstream(counts, source, vec, received=None):
    extra = [] if received is None else list(received)
    return call(
        lambda *refs: upstream_kernel(received is None, *refs),
        [((T, D), f32), ((T, D), bf16)],
        [counts, source] + extra + [vec],
        [SM] + [VM] * (2 + len(extra)),
        moved=2**20,
        name="upstream",
    )


def feed_backward_kernel(keep, g_ref, df_ref, f_ref, gp_ref, x1_ref, o_ref, vec, w1, w2, dx1_out, do_out, *refs):
    g = g_ref[...]
    df = df_ref[...]
    if keep:
        dh_out, small = refs
        small[8:9, :] = jnp.sum(df.astype(f32), axis=0, keepdims=True)
        small[9:10, :] = jnp.sum(g * f_ref[...].astype(f32), axis=0, keepdims=True)
        small[0:4, :] = jnp.zeros((4, D), f32)
        small[14:16, :] = jnp.zeros((2, D), f32)
    total = None
    ahead = dot(df, w2[0].reshape(512, D), NT)
    for t in range(8):
        y, off = t // 2, (t % 2) * 512
        cols = slice(t * 512, t * 512 + 512)
        du = ahead
        if t < 7:
            ahead = dot(df, w2[t + 1].reshape(512, D), NT)
        dh = (gp_ref[:, cols].astype(f32) * du).astype(bf16)
        if keep:
            dh_out[:, cols] = dh
            small[10 + y : 11 + y, off : off + 512] = jnp.sum(dh.astype(f32), axis=0, keepdims=True)
        part = dot(dh, fc1_tile(w1, t), NT)
        total = part if total is None else total + part
    hat, scale = stats(x1_ref[...])
    d_norm, d_gain, d_shift = norm_back(total, vec[6:7, :], hat, scale)
    dx1 = g + d_norm
    dx1_out[...] = dx1
    do = (vec[5:6, :] * dx1).astype(bf16)
    do_out[...] = do
    if keep:
        small[4:5, :] = jnp.sum(do.astype(f32), axis=0, keepdims=True)
        small[5:6, :] = jnp.sum(dx1 * o_ref[...].astype(f32), axis=0, keepdims=True)
        small[6:7, :] = d_gain
        small[7:8, :] = d_shift


def feed_backward(keep, g, df, f, gp, x1, o, vec, weights):
    outs = [((T, D), f32), ((T, D), bf16)]
    if keep:
        outs += [((T, FF), bf16), ((16, D), f32)]
    return call(
        lambda *refs: feed_backward_kernel(keep, *refs),
        outs,
        [g, df, f, gp, x1, o, vec, weights[2], weights[3]],
        [VM] * 9,
        flops=4 * T * D * FF,
        moved=26 * 2**20,
        name="feed_backward",
        limit=6,
    )


def attention_backward_kernel(
    do_ref, dx1_ref, x_ref, p_ref, soft_ref, small_ref, vec, w_qkv, w_proj, *refs
):
    dp_out, dx_out, small, dm_ref = refs[-4:]
    dm_ref[...] = dot(do_ref[...], w_proj[...].reshape(D, D), NT).astype(bf16)
    lane = lax.broadcasted_iota(jnp.int32, (128, 128), 1) < 64

    def unit(u, _):
        i, h = lax.div(u, jnp.int32(8)), lax.rem(u, jnp.int32(8))
        rows = pl.ds(pl.multiple_of(i * 128, 128), 128)
        at = lambda o: pl.ds(pl.multiple_of(h * 128 + o, 128), 128)
        q, k, v = [p_ref[rows, at(o)] for o in (0, 1024, 2048)]
        dm = stacked_heads(dm_ref[rows, at(0)], lane)
        low = soft_ref[u]
        soft = low.astype(f32)
        dp_out[rows, at(2048)] = dot(low, dm, TN).astype(bf16)
        dw = dot(dm, v, NT)
        ds = (soft * (dw - jnp.sum(soft * dw, axis=-1, keepdims=True))).astype(bf16)
        dq = dot(ds, k) * 0.125
        dp_out[rows, at(0)] = jnp.where(lane, dq[:128], dq[128:]).astype(bf16)
        dp_out[rows, at(1024)] = (dot(ds, stacked_heads(q, lane), TN) * 0.125).astype(bf16)
        return 0

    lax.fori_loop(0, 16, unit, 0, unroll=16)
    small[2:3, :] = jnp.sum(dp_out[:, 0:1024].astype(f32), axis=0, keepdims=True)
    small[3:4, :] = jnp.sum(dp_out[:, 2048:3072].astype(f32), axis=0, keepdims=True)
    small[4:16, :] = small_ref[4:16, :]
    dp_out[:, 3072:4096] = do_ref[...]
    total = None
    for j in range(6):
        cols = slice(j * 512, j * 512 + 512)
        part = dot(dp_out[:, cols], w_qkv[:, :, :, cols].reshape(D, 512), NT)
        total = part if total is None else total + part
    hat, scale = stats(x_ref[...].astype(f32))
    d_norm, small[0:1, :], small[1:2, :] = norm_back(total, vec[0:1, :], hat, scale)
    dx = dx1_ref[...] + d_norm
    if len(refs) > 4:
        dx = jnp.where(lax.axis_index("section") == 0, dx, refs[0][...])
    dx_out[...] = dx.astype(dx_out.dtype)


def attention_input_grad_kernel(image, do_ref, dx1_ref, x_ref, p_ref, soft_ref, vec, w_qkv, w_proj, dx_out, dm_ref, dp_ref):
    rows = slice(image * 128, image * 128 + 128)
    dm_ref[...] = dot(do_ref[rows, :], w_proj[...].reshape(D, D), NT).astype(bf16)
    lane = lax.broadcasted_iota(jnp.int32, (128, 128), 1) < 64

    def unit(h, _):
        at = lambda o: pl.ds(pl.multiple_of(h * 128 + o, 128), 128)
        q, k, v = [p_ref[rows, at(o)] for o in (0, 1024, 2048)]
        dm = stacked_heads(dm_ref[:, at(0)], lane)
        low = soft_ref[image * 8 + h]
        soft = low.astype(f32)
        dp_ref[:, at(2048)] = dot(low, dm, TN).astype(bf16)
        dw = dot(dm, v, NT)
        ds = (soft * (dw - jnp.sum(soft * dw, axis=-1, keepdims=True))).astype(bf16)
        dq = dot(ds, k) * 0.125
        dp_ref[:, at(0)] = jnp.where(lane, dq[:128], dq[128:]).astype(bf16)
        dp_ref[:, at(1024)] = (dot(ds, stacked_heads(q, lane), TN) * 0.125).astype(bf16)
        return 0

    lax.fori_loop(0, 8, unit, 0, unroll=8)
    total = None
    for j in range(6):
        cols = slice(j * 512, j * 512 + 512)
        part = dot(dp_ref[:, cols], w_qkv[:, :, :, cols].reshape(D, 512), NT)
        total = part if total is None else total + part
    hat, scale = stats(x_ref[rows, :].astype(f32))
    d_norm, _, _ = norm_back(total, vec[0:1, :], hat, scale)
    dx_out[...] = (dx1_ref[rows, :] + d_norm).astype(bf16)


def attention_input_grad(image, do, dx1, x, p, soft, vec, weights):
    return call(
        lambda *refs: attention_input_grad_kernel(image, *refs),
        [((128, D), bf16)],
        [do, dx1, x, p, soft, vec, weights[0], weights[1]],
        [VM] * 8,
        scratch=[pltpu.VMEM((128, D), bf16), pltpu.VMEM((128, 3072), bf16)],
        flops=T * D * 4 * D,
        moved=10 * 2**20,
        name="attention_input_grad",
        limit=6,
    )[0]


def attention_backward(do, dx1, x, p, soft, small, vec, weights, output=None):
    extra = [] if output is None else [output]
    return call(
        attention_backward_kernel,
        [((T, 4096), bf16), ((T, D), f32 if extra else bf16), ((16, D), f32)],
        [do, dx1, x, p, soft, small, vec, weights[0], weights[1]] + extra,
        [VM] * (9 + len(extra)),
        scratch=[pltpu.VMEM((T, D), bf16)],
        flops=2 * T * D * 4 * D,
        moved=18 * 2**20,
        name="attention_backward",
        limit=6,
    )


def picked_kernel(a_ref, m_ref, c_ref, u_ref, mine, theirs):
    x, z, c, _ = place()
    row = lax.broadcasted_iota(jnp.int32, (512, D), 0)
    col = lax.broadcasted_iota(jnp.int32, (512, D), 1)
    eye_r = lax.broadcasted_iota(jnp.int32, (256, 256), 0)
    eye = jnp.where(eye_r == lax.broadcasted_iota(jnp.int32, (256, 256), 1), 1.0, 0.0).astype(bf16)
    kind, dz, inner = row >> 7, (row >> 6) & 1, row & 63
    for k, out in enumerate((mine, theirs)):
        ck = near(c, k, CS)
        step = 1 - 2 * ck
        there = jnp.where(kind == 0, 2, jnp.where(kind == 1, 4 - step, jnp.where(kind == 2, 4 + step, 0)))
        there = (((x + there) & 3) << 8) + (((z + dz) & 1) << 7) + inner + ck * 64
        chosen = jnp.where(col == there, 1.0, 0.0).astype(bf16)
        for n, ref in enumerate((a_ref, m_ref)):
            out[n * 512 : n * 512 + 512, :] = dot(chosen, ref[...], NT).astype(bf16)
        there = ((row >> 6) << 7) + inner + ck * 64
        chosen = jnp.where(col == there, 1.0, 0.0).astype(bf16)
        out[1024:1536, :] = dot(chosen, c_ref[...], NT).astype(bf16)
        for j in range(8):
            chip = near(x, j % 4, XS) * 2 + near(z, j // 4, ZS)
            block = u_ref[:, pl.ds(pl.multiple_of((2 * chip + ck) * 256, 256), 256)]
            turned = dot(eye, block, NT).astype(bf16)
            for k2 in range(YS):
                out[1536 + k2 * 512 + j * 64 : 1600 + k2 * 512 + j * 64, :] = turned[k2 * 64 : k2 * 64 + 64]


def picked(a, m, c, u):
    return call(
        picked_kernel,
        [((3584, T), bf16)] * 2,
        [a, m, c, u],
        [VM] * 4,
        flops=2 * 10**9,
        moved=8 * 2**20,
        name="transposed_acts",
    )


def fc2_grads_kernel(mine, theirs, df, df2, *outs):
    _, _, c, y = place()
    for n, yk in enumerate(places(y, c, YS)):
        rows = pl.ds(pl.multiple_of(1536 + yk * 512, 512), 512)
        grad = dot(mine[rows, :], df[...]) + dot(theirs[rows, :], df2[...])
        outs[n][...] = grad.astype(bf16).reshape(8, 64, 1024)


def fc1_grads_kernel(mine, theirs, dh, dh2, *outs):
    _, _, c, y = place()
    for n, yk in enumerate(places(y, c, YS)):
        cols = pl.ds(pl.multiple_of(yk * 1024, 1024), 1024)
        grad = dot(mine[1024:1536, :], dh[:, cols]) + dot(theirs[1024:1536, :], dh2[:, cols])
        outs[n][...] = grad.astype(bf16).reshape(8, 64, 1024)


def feed_grads(kernel, name, mine, theirs, given, given2):
    return call(
        kernel,
        [((8, 64, 1024), bf16)] * 4,
        [mine, theirs, given, given2],
        [VM] * 4,
        flops=4 * T * D * FF,
        moved=12 * 2**20,
        name=name,
    )


def attention_grads_kernel(mine, theirs, dp, dp2, small, small2, *refs):
    outs, total = refs[:4], refs[4]
    x, z, c, _ = place()
    total[...] = small[...] + small2[...]
    vec = total[...].astype(bf16)
    row = lax.broadcasted_iota(jnp.int32, (D, 128), 0)
    col = lax.broadcasted_iota(jnp.int32, (D, 128), 1)
    line = lax.broadcasted_iota(jnp.int32, (16, 128), 0)
    for n, x_there in enumerate(places(x, c, XS)):
        for dz in range(ZS):
            inner = near(z, dz, ZS) * 2 + c
            chosen = jnp.where((row == col + x_there * 256 + inner * 64) & (col < 64), 1.0, 0.0).astype(bf16)
            outs[n][dz, 32:64, 4096:4224] = jnp.zeros((32, 128), bf16)
            outs[n][dz, 0:16, 4096:4224] = dot(vec, chosen).astype(bf16)
            there = total[pl.ds(10 + x_there, 1), pl.ds(pl.multiple_of(inner * 256, 256), 256)]
            a, b = there[:, 0:128], there[:, 128:256]
            outs[n][dz, 16:32, 4096:4224] = jnp.where(line == 0, a, jnp.where(line == 1, b, 0.0)).astype(bf16)
    for t in range(8):
        low = 0 if t < 6 else 512
        cols = slice(t * 512, t * 512 + 512)
        grad = dot(mine[low : low + 512, :], dp[:, cols]) + dot(theirs[low : low + 512, :], dp2[:, cols])
        grad = grad.astype(bf16)
        for n in range(4):
            outs[n][:, :, cols] = grad[n * 128 : n * 128 + 128].reshape(2, 64, 512)


def attention_grads(mine, theirs, dp, dp2, small, small2):
    return call(
        attention_grads_kernel,
        [((2, 64, QP), bf16)] * 4,
        [mine, theirs, dp, dp2, small, small2],
        [VM] * 6,
        scratch=[pltpu.VMEM((16, D), f32)],
        flops=8 * T * D * 2 * D,
        moved=16 * 2**20,
        name="attention_grads",
    )


def sum_kernel(count, axis, *refs):
    total = refs[0][...].astype(f32)
    for ref in refs[1:count]:
        total = total + ref[...].astype(f32)
    outs = refs[count:]
    if axis == "add":
        outs[0][...] = jnp.sum(total, axis=0).astype(bf16)
    elif axis == "split":
        for n, out in enumerate(outs):
            out[...] = total[n].astype(bf16)
    elif axis == "halves":
        count = total.shape[0] // 2
        outs[0][...] = total[:count].astype(bf16)
        outs[1][...] = total[count:].astype(bf16)
    elif axis == "quarters":
        outs, held = outs[:4], outs[4]
        held[...] = total
        _, _, _, y = place()
        for dy, out in enumerate(outs):
            out[...] = held[pl.ds(pl.multiple_of(near(y, dy, YS) * 16, 16), 16), :].astype(bf16)
    else:
        outs[0][...] = total.astype(bf16)


def summed(parts, axis=None):
    shape = parts[0].shape
    scratch = []
    if axis == "split":
        outs = [(shape[1:], bf16)] * shape[0]
    elif axis == "halves":
        outs = [((shape[0] // 2,) + shape[1:], bf16)] * 2
    elif axis == "quarters":
        outs = [((16,) + shape[1:], bf16)] * 4
        scratch = [pltpu.VMEM(shape, f32)]
    else:
        outs = [(shape[1:] if axis else shape, bf16)]
    size = 1
    for n in shape:
        size *= n
    out = call(
        lambda *refs: sum_kernel(len(parts), axis, *refs),
        outs,
        parts,
        [VM] * len(parts),
        scratch=scratch,
        flops=size * len(parts),
        moved=2 * size * (len(parts) + 1),
        name="summed",
    )
    return out if len(outs) > 1 else out[0]


def gathered_copies(parts, target, sems):
    y = place()[3]
    copies = [pltpu.make_async_copy(part, target.at[near(y, dy, YS)], sems.at[dy]) for dy, part in enumerate(parts)]
    start(copies)
    return copies


def fc1_results_kernel(a, b, c, d, out, held, sems):
    wait(gathered_copies((a, b, c, d), held, sems))
    for k in range(YS):
        out[:, k * 1024 : k * 1024 + 1024] = held[k].astype(f32)


def fc2_results_kernel(a, b, c, d, out, held, sems):
    wait(gathered_copies((a, b, c, d), held, sems))
    for k in range(YS):
        out[k * 64 : k * 64 + 64, :] = held[k].astype(f32)


def column_results_kernel(a, b, c, d, qkv, proj, vec, bias, held, sems):
    wait(gathered_copies((a, b, c, d), held, sems))
    for k in range(YS):
        line = slice(k * 16, k * 16 + 16)
        qkv[line, :] = held[k, :, 0:3072].astype(f32)
        proj[line, :] = held[k, :, 3072:4096].astype(f32)
    vec[...] = held[0, 0:10, 4096:4160].astype(f32)
    tail = held[1, 0:16, 4096:4224].astype(f32)
    bias[:, 0:128] = tail[0:1]
    bias[:, 128:256] = tail[1:2]


def results(kernel, shapes, parts, name):
    return call(
        kernel,
        [(shape, f32) for shape in shapes],
        parts,
        [ANY] * 4,
        scratch=[pltpu.VMEM((4,) + parts[0].shape, bf16), pltpu.SemaphoreType.DMA((4,))],
        moved=10 * 2**20,
        name=name,
    )


def twin(value, name="twin"):
    with jax.named_scope(name):
        return from_shard(value, dc=1)


def around(value, name):
    with jax.named_scope(name):
        return [value] + [from_replica(value, dy) for dy in range(1, YS)]


def swap(value, name):
    groups = [[shard_of(x, z, c) for x in range(XS) for z in range(ZS)] for c in range(CS)]
    with jax.named_scope(name):
        return lax.all_to_all(value, "shard", split_axis=0, concat_axis=0, axis_index_groups=groups, tiled=True)


def gather(w_qkv, w_proj, w_fc1, w_fc2, vectors, fc1_bias):
    hold = lax.optimization_barrier
    here = swap(own_pieces(w_fc1, w_fc2), "here")
    unit = own_unit(w_qkv, w_proj, w_fc2, vectors, fc1_bias)
    twin_unit = twin(unit, "twin_unit")
    unit, here, twin_unit = hold((unit, here, twin_unit))
    behind, twin_here = onward(here, "y", "behind"), twin(here, "twin_here")
    other = from_shard(unit, dz=1, name="other")
    plus, minus = from_shard(unit, dx=1, name="plus"), from_shard(unit, dx=3, name="minus")
    behind, twin_here, other, plus, minus = hold((behind, twin_here, other, plus, minus))
    twin_behind = onward(twin_here, "y", "twin_behind")
    minus_other, plus_other = from_shard(other, dx=3, name="minus_other"), from_shard(plus, dz=1, name="plus_other")
    far = from_shard(plus, dx=1, name="far")
    first = stacked([other, plus, minus])
    twins = twin(first, "twin_first")
    weights = put_columns(None, [(0, 0, 0, 0, None), (1, 0, 0, 1, None)], [unit, twin_unit])
    fc1, weights[2] = put_rows(None, weights[2], {(0, 3): here, (1, 3): twin_here})
    held = hold((twin_behind, minus_other, plus_other, far, first, twins, fc1, weights))
    twin_behind, minus_other, plus_other, far, first, twins, fc1, weights = held
    far_first, far_rest = parted(far, minus_other)
    opposite = onward(after(behind, far_first), "y", "opposite")
    far_first, far_rest = from_shard(far_first, dz=1, name="far_first"), from_shard(far_rest, dx=3, name="far_rest")
    ahead, twin_ahead = twin(twin_behind, "ahead"), twin(behind, "twin_ahead")
    second = stacked([minus_other, plus_other, far])
    second_twins = twin(second, "twin_second")
    order = [(0, 1), (1, 0), (3, 0)]
    weights = put_columns(weights, [(k, dx, dz, k, n) for k in range(2) for n, (dx, dz) in enumerate(order)], [first, twins])
    fc1, weights[2] = put_rows(fc1, weights[2], {(0, 1): behind, (1, 1): twin_behind})
    held = hold((far_first, far_rest, ahead, twin_ahead, second, second_twins, fc1, weights))
    far_first, far_rest, ahead, twin_ahead, second, second_twins, fc1, weights = held
    order = [(3, 1), (1, 1), (2, 0)]
    keys = [(k, dx, dz, k, n) for k in range(2) for n, (dx, dz) in enumerate(order)]
    weights = put_columns(weights, keys, [second, second_twins])
    weights = put_columns(weights, [(0, 2, 1, 0, None), (1, 2, 1, 1, None)], [far_first, twin(far_first, "twin_far_first")])
    vec, bias = gathered_vectors(weights[3])
    fc1, fc2 = put_rows(fc1, weights[2], {(0, 2): ahead, (1, 2): twin_ahead})
    fc2 = put_rest(fc2, far_rest, twin(far_rest, "twin_far_rest"))
    opposite, fc2, vec = hold((opposite, fc2, vec))
    return [weights[0], weights[1], fc2], fc1, opposite, vec, bias


def put_last(weights, fc1, opposite):
    fc1, fc2 = put_rows(fc1, weights[2], {(0, 0): opposite, (1, 0): twin(opposite, "twin_opposite")})
    return weights[0], weights[1], fc1, fc2


def shards(edge_inputs, image_counts, w_qkv, w_proj, w_fc1, w_fc2, vectors, fc1_bias):
    source = edge_inputs[0, :, 0].reshape(T, D)
    weights, fc1, opposite, vec, bias = gather(w_qkv[0], w_proj[0], w_fc1[0], w_fc2[0], vectors[0], fc1_bias)
    hold = lax.optimization_barrier

    x1, c = attention_forward(False, source, vec, weights)
    weights = put_last(weights, fc1, opposite)
    (first_out,) = feed_forward(False, x1, c, vec, bias, weights)
    received = passed_along(first_out, 1)
    inputs, a, p, soft, m, o, x1, c = attention_forward(True, source, vec, weights, received)
    u, gp, f, output = feed_forward(True, x1, c, vec, bias, weights)

    g, df = upstream(image_counts, source, vec)
    dx1, do = feed_backward(False, g, df, f, gp, x1, o, vec, weights)
    halves = [attention_input_grad(m, do, dx1, inputs, p, soft, vec, weights) for m in range(2)]
    received_grad = [passed_along(half, -1) for half in halves]
    mine, theirs = picked(after(a, halves[1]), m, c, u)
    received_grad, mine, theirs = lax.optimization_barrier((received_grad, mine, twin(theirs)))

    hold = lax.optimization_barrier
    g, df = upstream(image_counts, source, vec, received_grad)
    parts_2 = feed_grads(fc2_grads_kernel, "fc2_grads", mine, theirs, df, twin(df, "twin_df"))
    far_2 = onward(parts_2[0], "y", "far_2")
    g = after(g, parts_2[0])
    dx1, do, dh, small = feed_backward(True, g, df, f, gp, x1, o, vec, weights)
    dh2 = twin(dh, "twin_dh")
    dp, edge, small = attention_backward(do, dx1, inputs, p, soft, small, vec, weights, output)
    dh, dh2, dp, far_2 = hold((dh, dh2, dp, far_2))
    dp2, small2 = twin(dp, "twin_dp"), twin(small, "twin_small")
    relay_2 = summed([parts_2[2], far_2])
    own_2, given_2 = onward(relay_2, "y", "own_2"), onward(after(parts_2[1], relay_2), "y", "given_2", -1)
    parts_1 = feed_grads(fc1_grads_kernel, "fc1_grads", mine, theirs, after(dh, relay_2), dh2)
    parts_c = attention_grads(mine, theirs, after(dp, parts_1[3]), dp2, small, small2)
    far_c, given_c = onward(parts_c[0], "x", "far_c"), onward(parts_c[1], "x", "given_c", -1)
    parts_1, own_2, given_2, last = hold((parts_1, own_2, given_2, parts_c[3]))
    far_1, given_1 = onward(parts_1[0], "y", "far_1"), onward(parts_1[1], "y", "given_1", -1)

    same_2, other_2 = summed([parts_2[3], own_2, given_2], "halves")
    with jax.named_scope("other_2"):
        other_2 = from_shard(other_2, dz=1)
    far_c, given_c = hold((far_c, given_c))
    relay_c = summed([after(parts_c[2], same_2), far_c])
    own_c = onward(relay_c, "x", "own_c")
    along = summed([after(same_2, relay_c), other_2], "split")
    with jax.named_scope("along_2"):
        along = [along[0]] + [from_shard(along[dx], dx=XS - dx) for dx in range(1, XS)]
    far_1, given_1 = hold((far_1, given_1))
    relay_1 = summed([after(parts_1[2], along[0]), far_1])
    own_1 = onward(relay_1, "y", "own_1")
    same, other = summed([after(last, relay_1), own_c, given_c], "split")
    fc2 = summed([after(along[0], same)] + along[1:])
    with jax.named_scope("other_z"):
        other = from_shard(other, dz=1)
    quarters = summed([after(same, fc2), other], "quarters")
    sum_1 = summed([after(parts_1[3], quarters[0]), own_1, given_1])
    with jax.named_scope("quarters"):
        quarters = [quarters[0]] + [from_replica(quarters[dy], YS - dy) for dy in range(1, YS)]
    got_1 = swap(sum_1, "swap_1")
    (g_fc2,) = results(fc2_results_kernel, [(256, D)], around(fc2, "around_fc2"), "fc2_results")
    column = around(summed([after(quarters[0], g_fc2)] + quarters[1:]), "around_c")
    fc1 = around(summed([got_1], "add"), "around_fc1")
    g_qkv, g_proj, g_vec, g_bias = results(
        column_results_kernel, [(64, 3072), (64, 1024), (10, 64), (1, 256)], column, "column_results"
    )
    (g_fc1,) = results(fc1_results_kernel, [(64, FF)], fc1, "fc1_results")
    return (
        edge.reshape(1, 2, 1, 128, D),
        g_qkv[None],
        g_proj[None],
        g_fc1[None],
        g_fc2[None],
        g_vec[None],
        g_bias,
    )


def solution(mesh):
    placed = (
        P("section", None, ("shard", "replica"), None, None),
        P(),
        P("section", "shard", None),
        P("section", "shard", None),
        P("section", "shard", None),
        P("section", "shard", None),
        P("section", None, "shard"),
        P("section", "shard"),
    )
    return jax.shard_map(
        shards,
        mesh=mesh,
        in_specs=placed,
        out_specs=(placed[0],) + placed[2:],
        check_vma=False,
    )
```
